256 devices in a mesh: lat: 32 (over x_hi, z, core), ch: 8 (over y, x_lo).
Axes of the slice: x: 4 (x_hi: 2, x_lo: 2; x = x_hi * 2 + x_lo), y: 4, z: 8, core: 2. Of those that a mesh axis runs over, the one named last changes fastest.
Arguments:
- fields: bfloat16 [768, 224, 384], P('ch', 'lat'), may hold values from -60 to 60
- gain_first: float32 [768], P('ch'), may hold values from 0.5 to 1.5
- w_inner: float32 [2, 8, 96, 96], P(None, 'ch'), may hold values from -0.4375 to 0.4375
- w_outer: float32 [2, 8, 96, 96], P(None, 'ch'), may hold values from -0.4375 to 0.4375
- gain_second: float32 [768], P('ch'), may hold values from 0.5 to 1.5
- fc_in: bfloat16 [768, 3072], P(None, 'ch'), may hold values from -0.21875 to 0.21875
- fc_out: bfloat16 [3072, 768], P('ch'), may hold values from -0.109375 to 0.109375
- cotangent: bfloat16 [768, 224, 384], P('ch', 'lat'), may hold values from -40 to 40
Outputs:
- output: bfloat16 [768, 224, 384], P('ch', 'lat')
- grad_fields: bfloat16 [768, 224, 384], P('ch', 'lat')
- grad_gain_first: float32 [768], P('ch')
- grad_w_inner: float32 [2, 8, 96, 96], P(None, 'ch')
- grad_w_outer: float32 [2, 8, 96, 96], P(None, 'ch')
- grad_gain_second: float32 [768], P('ch')
- grad_fc_in: float32 [768, 3072], P(None, 'ch')
- grad_fc_out: float32 [3072, 768], P('ch')
The draws below stay inside these ranges and needn't reach their ends.
All inputs are finite; a program needn't handle non-finite values.
Results may differ from the reference program's by a relative error of at most 0.0056.
Values may be sent and summed in bfloat16 or wider, within the bound.
No kernel may reach another device: no remote copies, remote signals or barrier semaphores. Data moves between devices by JAX's collectives and lax.ppermute only.
A program may use at most 128 MiB of HBM per device.

```python
import math
import jax
import jax.numpy as jnp
from jax import lax

NB = 8
BS = 96
H = 224
W = 384
KW = 192
C = 768
FF = 3072
LAT_DEV = 7
N_LAT = 32


def draw_fields(key, part):
    key = jax.random.fold_in(key, 17)
    keys = jax.random.split(key, 3)
    channel_ramp = jnp.exp(jnp.arange(C, dtype=jnp.float32) * (math.log(3.0) / (C - 1)))
    spread = jnp.exp(jax.random.uniform(keys[0], (C,), dtype=jnp.float32) * math.log(4.0))
    base = jax.random.normal(keys[1], (C, H, W), dtype=jnp.float32)
    common = 0.3 * jax.random.normal(keys[2], (1, H, 1), dtype=jnp.float32)
    factor = (channel_ramp * spread)[:, None, None]
    return jnp.clip(base * factor + common, -60.0, 60.0).astype(jnp.bfloat16)


def draw_cotangent(key, part):
    key = jax.random.fold_in(key, 29)
    keys = jax.random.split(key, 2)
    row_ramp = 1.0 + 2.0 * jnp.arange(H, dtype=jnp.float32) / (H - 1)
    spread = jnp.exp(jax.random.uniform(keys[0], (C,), dtype=jnp.float32) * math.log(3.0))
    base = jax.random.normal(keys[1], (C, H, W), dtype=jnp.float32)
    values = base * spread[:, None, None] * row_ramp[None, :, None]
    return jnp.clip(values, -40.0, 40.0).astype(jnp.bfloat16)


def block_levels(stream_key, dims, cuts, smallest, high):
    def one(dim, shards_of):
        draws = jax.random.uniform(jax.random.fold_in(jax.random.fold_in(stream_key, 6), dim), (shards_of,), jnp.float32, smallest / len(cuts), high / len(cuts))
        return jnp.repeat(jnp.exp(draws), dims[dim] // shards_of).reshape((-1,) + (1,) * (len(dims) - dim - 1))

    level = one(*cuts[0])
    for cut in cuts[1:]:
        level = level * one(*cut)
    return level


def gaussian(own_key, dims, scale, limit, shards=(), kind=jnp.bfloat16):
    drawn = jax.random.normal(own_key, dims, jnp.float32) * scale
    if len(shards) > 0:
        drawn = block_levels(own_key, dims, shards, -0.22, 0.18) * drawn
    return jnp.clip(drawn, min=-limit, max=limit).astype(kind)


def setup_inputs(seed: int = 0) -> dict:
    arg_keys = jax.random.split(jax.random.key(seed), 9)
    return {
        "fields": draw_fields(jax.random.fold_in(arg_keys[8], 71), 0),
        "gain_first": jnp.clip(1.0 + 0.1 * jax.random.normal(arg_keys[1], (C,), jnp.float32), 0.5, 1.5),
        "w_inner": gaussian(arg_keys[2], (2, NB, BS, BS), (2 * BS) ** -0.5, 0.4375, ((1, 8),), jnp.float32),
        "w_outer": gaussian(arg_keys[3], (2, NB, BS, BS), (2 * BS) ** -0.5, 0.4375, ((1, 8),), jnp.float32),
        "gain_second": jnp.clip(1.0 + 0.1 * jax.random.normal(arg_keys[4], (C,), jnp.float32), 0.5, 1.5),
        "fc_in": gaussian(arg_keys[5], (C, FF), C ** -0.5, 0.21875, ((1, 8),)),
        "fc_out": gaussian(arg_keys[6], (FF, C), FF ** -0.5, 0.109375, ((0, 8),)),
        "cotangent": draw_cotangent(jax.random.fold_in(arg_keys[8], 71), 0),
    }


EPSILON = 1e-05
HIGHEST = lax.Precision.HIGHEST

def gelu_value(values):
    return 0.5 * values * (1.0 + lax.erf(values * 0.7071067811865476))

def gelu_slope(values):
    return 0.5 * (1.0 + lax.erf(values * 0.7071067811865476)) + values * 0.3989422804014327 * jnp.exp(-0.5 * values * values)

def normalize(values):
    average = lax.optimization_barrier(jnp.sum(values, 0)) / C
    squares = lax.optimization_barrier(jnp.sum(values * values, 0)) / C
    inv_std = lax.rsqrt(squares - average * average + EPSILON)
    return ((values - average) * inv_std, inv_std)

def norm_back(gradient, normed, inv_std):
    leading = lax.optimization_barrier(jnp.sum(gradient, 0)) / C
    paired = lax.optimization_barrier(jnp.sum(gradient * normed, 0)) / C
    return inv_std * (gradient - leading - normed * paired)

def spectral(lifted, w_inner, w_outer):
    spectrum = jnp.fft.rfft(lifted, axis=2, norm='ortho')[:, :, :KW]
    spectrum = jnp.fft.fft(spectrum, axis=1, norm='ortho').reshape(NB, BS, H, KW)
    inner_matrix = w_inner[0] + 1j * w_inner[1]
    outer_matrix = w_outer[0] + 1j * w_outer[1]
    hidden_modes = jnp.einsum('bij,bjhk->bihk', inner_matrix, spectrum, precision=HIGHEST)
    hidden_modes = gelu_value(hidden_modes.real) + 1j * gelu_value(hidden_modes.imag)
    mixed_modes = jnp.einsum('bij,bjhk->bihk', outer_matrix, hidden_modes, precision=HIGHEST).reshape(C, H, KW)
    mixed_modes = jnp.pad(mixed_modes, ((0, 0), (0, 0), (0, W // 2 + 1 - KW)))
    mixed_modes = jnp.fft.ifft(mixed_modes, axis=1, norm='ortho')
    return jnp.fft.irfft(mixed_modes, n=W, axis=2, norm='ortho')

def unband(stacked):
    return stacked.reshape(N_LAT, C, LAT_DEV, W).transpose(1, 0, 2, 3).reshape(C, H, W)

def reference(fields, gain_first, w_inner, w_outer, gain_second, fc_in, fc_out, cotangent):
    x_float = fields.astype(jnp.float32)
    normed_in, inv_std_in = normalize(x_float)
    lifted = normed_in * gain_first[:, None, None]
    filtered, spectral_back = jax.vjp(spectral, lifted, w_inner, w_outer)
    mixed_in = filtered + lifted + x_float
    normed_mid, inv_std_mid = normalize(mixed_in)
    mlp_input = (normed_mid * gain_second[:, None, None]).astype(jnp.bfloat16)
    weight_in = fc_in.astype(jnp.float32)
    weight_out = fc_out.astype(jnp.float32)

    def lat_band(running, band_index):
        grad_in, grad_out, grad_gain = running
        offset = (band_index * LAT_DEV).astype(jnp.int32)

        def rows_of(values):
            return lax.dynamic_slice_in_dim(values, offset, LAT_DEV, 1).reshape(values.shape[0], LAT_DEV * W)
        inputs_band = rows_of(mlp_input).astype(jnp.float32)
        pre_act = jnp.dot(weight_in.T, inputs_band, preferred_element_type=jnp.float32)
        hidden = lax.optimization_barrier(gelu_value(pre_act).astype(jnp.bfloat16)).astype(jnp.float32)
        projected = jnp.dot(weight_out.T, hidden, preferred_element_type=jnp.float32)
        out_band = (rows_of(mixed_in) + projected).astype(jnp.bfloat16)
        grad_band = rows_of(cotangent).astype(jnp.float32)
        grad_hidden = jnp.dot(weight_out, grad_band, preferred_element_type=jnp.float32)
        grad_pre = lax.optimization_barrier((grad_hidden * gelu_slope(pre_act)).astype(jnp.bfloat16)).astype(jnp.float32)
        grad_out = grad_out + jnp.dot(hidden, grad_band.T, preferred_element_type=jnp.float32)
        grad_in = grad_in + jnp.dot(inputs_band, grad_pre.T, preferred_element_type=jnp.float32)
        grad_input = jnp.dot(weight_in, grad_pre, preferred_element_type=jnp.float32)
        normed_band = rows_of(normed_mid)
        std_band = lax.dynamic_slice_in_dim(inv_std_mid, offset, LAT_DEV, 0).reshape(LAT_DEV * W)
        grad_gain = grad_gain + lax.optimization_barrier(jnp.sum(grad_input * normed_band, 1))
        back_band = grad_band + norm_back(grad_input * gain_second[:, None], normed_band, std_band)
        return ((grad_in, grad_out, grad_gain), (out_band, back_band))
    start_state = (jnp.zeros((C, FF), jnp.float32), jnp.zeros((FF, C), jnp.float32), jnp.zeros((C,), jnp.float32))
    sums_final, stacked = lax.scan(lat_band, start_state, jnp.arange(N_LAT, dtype=jnp.int32))
    grad_fc_in, grad_fc_out, grad_gain_second = sums_final
    output = unband(stacked[0])
    grad_mixed = unband(stacked[1])
    grad_lifted, grad_w_inner, grad_w_outer = spectral_back(grad_mixed)
    grad_lifted = grad_lifted + grad_mixed
    grad_gain_first = lax.optimization_barrier(jnp.sum(grad_lifted * normed_in, (1, 2)))
    grad_fields = grad_mixed + norm_back(grad_lifted * gain_first[:, None, None], normed_in, inv_std_in)
    return (output, grad_fields.astype(jnp.bfloat16), grad_gain_first, grad_w_inner, grad_w_outer, grad_gain_second, grad_fc_in, grad_fc_out)
```

```python
import math

import jax
import jax.numpy as jnp
import ml_dtypes
import numpy as np
from jax import lax
from jax.experimental import pallas as pl
from jax.experimental.pallas import tpu as pltpu
from jax.sharding import PartitionSpec as P

C = 768
BS = 96
H = 224
W = 384
KW = 192
N_LAT = 32
N_CH = 8
ROWS = 7
FF_DEV = 384
MODES = KW // N_LAT
PLANES = 2 * MODES
LANES = PLANES * BS
GROUP = 384
EPSILON = 1e-05
BF16 = jnp.bfloat16
F32 = jnp.float32
VMEM_BYTES = 56 * 1024 * 1024


def halves(table):
    high = table.astype(ml_dtypes.bfloat16)
    low = (table - high.astype(np.float64)).astype(ml_dtypes.bfloat16)
    return high, low


def lon_table():
    mode = np.arange(MODES)[:, None] + MODES * np.arange(N_LAT)[None, :]
    angles = 2 * np.pi * ((mode[:, :, None] * np.arange(W)) % W) / W
    table = np.stack([np.cos(angles), -np.sin(angles)], 1) / math.sqrt(W)
    return table.reshape(PLANES * N_LAT, W)


def lat_tables():
    index = np.arange(H)
    angles = 2 * np.pi * ((index[:, None] * index[None, :]) % H) / H
    cosine = np.cos(angles) / math.sqrt(H)
    sine = np.sin(angles) / math.sqrt(H)
    forward = np.zeros((H, 2, N_LAT, 8))
    forward[:, 0, :, :ROWS] = cosine.reshape(H, N_LAT, ROWS)
    forward[:, 1, :, :ROWS] = sine.reshape(H, N_LAT, ROWS)
    inverse = np.zeros((N_LAT, 8, 2, H))
    inverse[:, :ROWS, 0] = cosine.reshape(N_LAT, ROWS, H)
    inverse[:, :ROWS, 1] = -sine.reshape(N_LAT, ROWS, H)
    return forward.reshape(H, 2 * N_LAT * 8), inverse.reshape(N_LAT * 8, 2 * H)


def swap_table():
    table = np.zeros((GROUP, GROUP))
    for mode in range(2):
        for c in range(BS):
            real = mode * 2 * BS + c
            table[real + BS, real] = 1
            table[real, real + BS] = -1
    return table.astype(ml_dtypes.bfloat16)


def dot(left, right):
    return lax.dot_general(left, right, (((1,), (0,)), ((), ())), preferred_element_type=F32)


def dot_nt(left, right):
    return lax.dot_general(left, right, (((1,), (1,)), ((), ())), preferred_element_type=F32)


def dot_tn(left, right):
    return lax.dot_general(left, right, (((0,), (0,)), ((), ())), preferred_element_type=F32)


def split(values):
    high = values.astype(BF16)
    return high, (values - high.astype(F32)).astype(BF16)


def dot3(kind, left, right):
    return kind(left[0], right[0]) + kind(left[1], right[0]) + kind(left[0], right[1])


def gelu_parts(values):
    cdf = 0.5 * (1.0 + lax.erf(values * 0.7071067811865476))
    return values * cdf, cdf + values * 0.3989422804014327 * jnp.exp(-0.5 * values * values)


def gelu_value(values):
    return 0.5 * values * (1.0 + lax.erf(values * 0.7071067811865476))


def norm_rows(stats):
    total = stats[0]
    for e in range(1, N_CH):
        total = total + stats[e]
    average = total[0:8] * (1.0 / C)
    squares = total[8:16] * (1.0 / C)
    return average, lax.rsqrt(squares - average * average + EPSILON)


def put_row(scratch, row, modes):
    wide = jnp.concatenate([modes[32 * k : 32 * k + 32] for k in range(PLANES)], axis=1)
    for t in range(LANES // 128):
        scratch[t, pl.ds(row, N_LAT, stride=8), :] = wide[:, 128 * t : 128 * t + 128]


def flush_rows(scratch, wire):
    for t in range(LANES // 128):
        scratch[t, pl.ds(ROWS, N_LAT, stride=8), :] = jnp.zeros((N_LAT, 128), F32)
        wire[:, 128 * t : 128 * t + 128] = scratch[t].astype(BF16)


def load_rows(wire, scratch):
    for t in range(LANES // 128):
        scratch[t] = wire[:, 128 * t : 128 * t + 128].astype(F32)


def get_row(scratch, row):
    wide = jnp.concatenate(
        [scratch[t, pl.ds(row, N_LAT, stride=8), :] for t in range(LANES // 128)], axis=1
    )
    return jnp.concatenate([wide[:, BS * k : BS * k + BS] for k in range(PLANES)], axis=0)


def to_chunk(rows, e):
    return jnp.concatenate(
        [
            jnp.concatenate(
                [values[48 * e + 8 * a : 48 * e + 8 * a + 8] for a in range(6)], axis=1
            )
            for values in rows
        ],
        axis=0,
    )


def from_chunks(chunks, row):
    return jnp.concatenate(
        [
            chunk[8 * row : 8 * row + 8, BS * a : BS * a + BS]
            for chunk in chunks
            for a in range(6)
        ],
        axis=0,
    )


def cot_kernel(cot, wire):
    rows = [cot[r].astype(F32).T for r in range(ROWS)]
    for e in range(N_CH):
        wire[e] = to_chunk(rows, e).astype(BF16)


def lon_kernel(x, stats, gain, t_high, t_low, wire, scratch):
    average, inv_std = norm_rows(stats)
    table = (t_high[...], t_low[...])
    for r in range(ROWS):
        normed = (x[r].astype(F32) - average[r : r + 1]) * inv_std[r : r + 1]
        lifted = split(normed * gain[...])
        put_row(scratch, r, dot3(dot_nt, table, lifted))
    flush_rows(scratch, wire)


def lat_forward(wire, lf_high, lf_low, swap):
    values = wire[...]
    swapped = dot(values, swap[...]).astype(BF16)
    both = jnp.concatenate([values, swapped], axis=0)
    return dot(lf_high[...], both) + dot(lf_low[...], both)


def lat_inverse(modes, li_high, li_low):
    both = split(jnp.concatenate([modes[:, :GROUP], modes[:, GROUP:]], axis=0))
    return dot3(dot, (li_high[...], li_low[...]), both)


def spectral_kernel(
    wire, lf_high, lf_low, swap, m1_high, m1_low, m2_high, m2_low, doubled, li_high, li_low,
    out, spectrum, pre_modes,
):
    modes = lat_forward(wire, lf_high, lf_low, swap)
    spectrum[...] = modes
    pre = dot3(dot, split(modes), (m1_high[...], m1_low[...]))
    pre_modes[...] = pre
    act = split(gelu_value(pre))
    scale = doubled[...]
    result = dot3(dot, act, (m2_high[...], m2_low[...])) * jnp.concatenate([scale, scale], axis=1)
    out[...] = lat_inverse(result, li_high, li_low).astype(BF16)


def spectral_back_kernel(
    wire, spectrum, pre_modes, lf_high, lf_low, swap, m1_high, m1_low, m2_high, m2_low, doubled,
    li_high, li_low, out, grad_outer, grad_inner, gain_part,
):
    @pl.when(pl.program_id(0) == 0)
    def _():
        grad_outer[...] = jnp.zeros_like(grad_outer)
        grad_inner[...] = jnp.zeros_like(grad_inner)

    grad = split(lat_forward(wire, lf_high, lf_low, swap) * doubled[...])
    act, slope = gelu_parts(pre_modes[...])
    grad_act = dot3(dot_nt, grad, (m2_high[:, :GROUP], m2_low[:, :GROUP]))
    grad_outer[...] += dot3(dot_tn, grad, split(act))
    grad_pre = split(grad_act * slope)
    modes = spectrum[...]
    grad_inner[...] += dot3(dot_tn, grad_pre, split(modes))
    grad_spectrum = dot3(dot_nt, grad_pre, (m1_high[...], m1_low[...]))
    gain_part[...] = jnp.sum(grad_spectrum[:, :GROUP] * modes, axis=0, keepdims=True)
    out[...] = lat_inverse(grad_spectrum, li_high, li_low).astype(BF16)


def mix_kernel(wire, tt_high, tt_low, x, stats, gain, mixed, chunks, scratch):
    average, inv_std = norm_rows(stats)
    load_rows(wire, scratch)
    rows = []
    for r in range(ROWS):
        x_float = x[r].astype(F32)
        lifted = (x_float - average[r : r + 1]) * inv_std[r : r + 1] * gain[...]
        modes = get_row(scratch, r).astype(BF16)
        filtered = dot(tt_high[...], modes) + dot(tt_low[...], modes)
        values = filtered + (lifted + x_float).T
        mixed[r] = values
        rows.append(values)
    for e in range(N_CH):
        chunks[e] = to_chunk(rows, e)


def mlp_kernel(
    core, mixed, cot, gain, own, other, out_chunks, grad_chunks, grad_own, grad_other,
    normed, inputs, cots, inv_std, sum_out, sum_grad,
):
    step = pl.program_id(0)
    turn = 4 * core[0]
    cells = 6 * 8 * ROWS
    part = 8 * ROWS

    def gain_row():
        return jnp.concatenate([gain[e ^ turn] for e in range(N_CH)], axis=1)

    @pl.when(step == 0)
    def _():
        pieces = [mixed[e ^ turn] for e in range(N_CH)]
        values = jnp.concatenate(
            [
                jnp.concatenate([piece[:, BS * a : BS * a + BS] for piece in pieces], axis=1)
                for a in range(6)
            ],
            axis=0,
        )
        average = jnp.sum(values, axis=1, keepdims=True) * (1.0 / C)
        squares = jnp.sum(values * values, axis=1, keepdims=True) * (1.0 / C)
        inv = lax.rsqrt(squares - average * average + EPSILON)
        values = (values - average) * inv
        normed[...] = values
        inv_std[...] = jnp.broadcast_to(inv, (cells, 128))
        inputs[...] = (values * gain_row()).astype(BF16)
        pieces = [cot[e ^ turn].astype(F32) for e in range(N_CH)]
        cots[...] = jnp.concatenate(
            [
                jnp.concatenate([piece[:, BS * a : BS * a + BS] for piece in pieces], axis=1)
                for a in range(6)
            ],
            axis=0,
        ).astype(BF16)
        sum_out[...] = jnp.zeros_like(sum_out)
        sum_grad[...] = jnp.zeros_like(sum_grad)

    first, second = inputs[:, :384], inputs[:, 384:]
    cot_first, cot_second = cots[:, :384], cots[:, 384:]
    in_own, out_own = own[0, 0], own[0, 1]
    in_other, out_other = other[0, 0], other[0, 1]
    pre_act = dot(first, in_own) + dot(second, in_other)
    hidden, slope = gelu_parts(pre_act)
    hidden = hidden.astype(BF16)
    grad_hidden = dot_nt(cot_first, out_own) + dot_nt(cot_second, out_other)
    grad_pre = (grad_hidden * slope).astype(BF16)
    sum_out[:, :384] += dot(hidden, out_own)
    sum_out[:, 384:] += dot(hidden, out_other)
    sum_grad[:, :384] += dot_nt(grad_pre, in_own)
    sum_grad[:, 384:] += dot_nt(grad_pre, in_other)
    grad_own[0, 0] = dot_tn(first, grad_pre)
    grad_other[0, 0] = dot_tn(second, grad_pre).astype(BF16)
    grad_own[0, 1] = dot_tn(hidden, cot_first)
    grad_other[0, 1] = dot_tn(hidden, cot_second).astype(BF16)

    @pl.when(step == N_CH - 1)
    def _():
        grad_input = sum_grad[...]
        values = normed[...]
        gain_sum = jnp.sum(grad_input * values, axis=0, keepdims=True)
        scaled = grad_input * gain_row()
        leading = jnp.sum(scaled, axis=1, keepdims=True) * (1.0 / C)
        paired = jnp.sum(scaled * values, axis=1, keepdims=True) * (1.0 / C)
        grad_mixed = cots[...].astype(F32) + inv_std[:, :1] * (scaled - leading - values * paired)
        outputs = sum_out[...]

        def chunk(array, e):
            return jnp.concatenate(
                [array[part * a : part * a + part, BS * e : BS * e + BS] for a in range(6)],
                axis=1,
            )

        for e in range(N_CH):
            out_chunks[e ^ turn] = chunk(outputs, e).astype(BF16)
            gain_piece = gain_sum[:, BS * e : BS * e + BS]
            gain_high = gain_piece.astype(BF16).astype(F32)
            extra = jnp.concatenate(
                [gain_high, gain_piece - gain_high, jnp.zeros((1, 4 * BS), F32)], axis=1
            )
            extra = jnp.concatenate([extra, jnp.zeros((7, 6 * BS), F32)], axis=0)
            grad_chunks[e ^ turn] = jnp.concatenate(
                [chunk(grad_mixed, e), extra], axis=0
            ).astype(BF16)


def lon_back_kernel(chunks, x, stats, t_high, t_low, wire, grad_mixed, gains, scratch):
    average, inv_std = norm_rows(stats)
    pieces = [chunks[e].astype(F32) for e in range(N_CH)]
    gain_first = jnp.zeros((BS, 1), F32)
    for r in range(ROWS):
        values = from_chunks(pieces, r)
        rounded = values.astype(BF16)
        put_row(scratch, r, dot(t_high[...], rounded) + dot(t_low[...], rounded))
        turned = values.T
        grad_mixed[r] = turned.astype(BF16)
        normed = (x[r].astype(F32) - average[r : r + 1]) * inv_std[r : r + 1]
        gain_first = gain_first + jnp.sum(turned * normed, axis=1, keepdims=True)
    flush_rows(scratch, wire)
    gain_second = jnp.zeros((1, BS), F32)
    for piece in pieces:
        row = piece[8 * ROWS : 8 * ROWS + 1]
        gain_second = gain_second + row[:, :BS] + row[:, BS : 2 * BS]
    turned_first = jnp.broadcast_to(gain_first, (BS, 128)).T[0:1, :]
    gains[0:1, :BS] = turned_first
    gains[1:2, :BS] = gain_second


def unmix_kernel(wire, tt_high, tt_low, grad_mixed, x, stats, gain, scaled, sums, scratch):
    average, inv_std = norm_rows(stats)
    load_rows(wire, scratch)
    for r in range(ROWS):
        modes = get_row(scratch, r).astype(BF16)
        back = dot(tt_high[...], modes) + dot(tt_low[...], modes)
        values = (back.T + grad_mixed[r].astype(F32)) * gain[...]
        normed = (x[r].astype(F32) - average[r : r + 1]) * inv_std[r : r + 1]
        scaled[r] = values
        sums[r : r + 1] = jnp.sum(values, axis=0, keepdims=True)
        sums[8 + r : 9 + r] = jnp.sum(values * normed, axis=0, keepdims=True)
    sums[7:8] = jnp.zeros((1, W), F32)
    sums[15:16] = jnp.zeros((1, W), F32)


def final_kernel(scaled, grad_mixed, x, stats, back_stats, out):
    average, inv_std = norm_rows(stats)
    total = back_stats[0]
    for e in range(1, N_CH):
        total = total + back_stats[e]
    total = total * (1.0 / C)
    for r in range(ROWS):
        inv = inv_std[r : r + 1]
        normed = (x[r].astype(F32) - average[r : r + 1]) * inv
        change = scaled[r] - total[r : r + 1] - normed * total[8 + r : 9 + r]
        out[r] = (grad_mixed[r].astype(F32) + inv * change).astype(BF16)


def output_kernel(chunks, mixed, out):
    pieces = [chunks[e].astype(F32) for e in range(N_CH)]
    for r in range(ROWS):
        out[r] = (from_chunks(pieces, r) + mixed[r]).T.astype(BF16)


def call(kernel, out_shape, *args, scratch=(), name=None):
    return pl.pallas_call(
        kernel,
        out_shape=out_shape,
        scratch_shapes=scratch,
        compiler_params=pltpu.CompilerParams(vmem_limit_bytes=VMEM_BYTES),
        name=name,
    )(*args)


def shaped(*shape, dtype=F32):
    return jax.ShapeDtypeStruct(shape, dtype)


def whole(shape):
    return pl.BlockSpec(shape, lambda g: (0,) * len(shape))


def lane_block(rows):
    return pl.BlockSpec((rows, GROUP), lambda g: (0, g))


def block_matrix(weight, swap_columns, swap_rows):
    real, imag = weight[0, 0].T, weight[1, 0].T
    base = [[real, imag], [-imag, real]]
    if swap_columns:
        base = [[imag, -real], [real, imag]]
    if swap_rows:
        base = [[-imag, real], [-real, -imag]]
    one = jnp.concatenate([jnp.concatenate(line, axis=1) for line in base], axis=0)
    zero = jnp.zeros_like(one)
    return jnp.concatenate(
        [jnp.concatenate([one, zero], axis=1), jnp.concatenate([zero, one], axis=1)], axis=0
    )


def weight_sum(blocks):
    parts = blocks.reshape(2, 2, BS, 2, 2, BS)
    parts = parts[0, :, :, 0] + parts[1, :, :, 1]
    return jnp.stack(
        [parts[0, :, 0] + parts[1, :, 1], parts[1, :, 0] - parts[0, :, 1]], axis=0
    )


def to_all(values, axis, count, **kwargs):
    spread = jnp.broadcast_to(values[None], (count,) + values.shape)
    return lax.all_to_all(spread, axis, 0, 0, tiled=True, **kwargs)


def body(fields, gain_first, w_inner, w_outer, gain_second, fc_in, fc_out, cotangent):
    lat = lax.axis_index("lat")
    core = lat % 2
    siblings = [(i, i ^ 1) for i in range(N_LAT)]
    cores = [list(range(0, N_LAT, 2)), list(range(1, N_LAT, 2))]
    t_high, t_low = (jnp.asarray(t) for t in halves(lon_table()))
    tt_high, tt_low = (jnp.asarray(t) for t in halves(lon_table().T))
    forward, inverse = lat_tables()
    lf_high, lf_low = (jnp.asarray(t) for t in halves(forward))
    li_high, li_low = (jnp.asarray(t) for t in halves(inverse))
    swap = jnp.asarray(swap_table())

    x = fields.transpose(1, 0, 2)
    cot = cotangent.transpose(1, 0, 2)
    gain_column = gain_first[:, None]

    with jax.named_scope("weights"):
        half_in = lax.dynamic_slice_in_dim(fc_in, core * 384, 384, 0)
        half_out = lax.dynamic_slice_in_dim(fc_out, core * 384, 384, 1)
        own = lax.all_gather(jnp.stack([half_in, half_out]), "ch")
        other = lax.ppermute(own, "lat", siblings)

    with jax.named_scope("stats"):
        x_float = x.astype(F32)
        zero = jnp.zeros((1, W), F32)
        payload = jnp.concatenate(
            [
                jnp.sum(x_float, 1),
                zero,
                jnp.sum(x_float * x_float, 1),
                zero,
                jnp.pad(gain_second, (0, W - BS))[None],
                jnp.zeros((7, W), F32),
            ],
            axis=0,
        )
        gathered = to_all(payload, "ch", N_CH)
        stats = gathered[:, :16]
        gains = gathered[:, 16:17, :BS]

    scratch = pltpu.VMEM((LANES // 128, 8 * N_LAT, 128), F32)
    wire_shape = shaped(8 * N_LAT, LANES, dtype=BF16)
    with jax.named_scope("lon"):
        wire = call(
            lon_kernel, wire_shape, x, stats, gain_column, t_high, t_low, scratch=[scratch]
        )
        wire = lax.all_to_all(wire, "lat", 0, 0, tiled=True)

    with jax.named_scope("cot"):
        cot_chunks = call(cot_kernel, shaped(N_CH, 8 * ROWS, 6 * BS, dtype=BF16), cot)
        cot_chunks = lax.all_to_all(cot_chunks, "ch", 0, 0, tiled=True)

    with jax.named_scope("matrices"):
        m1 = split(
            jnp.concatenate(
                [block_matrix(w_inner, False, False), block_matrix(w_inner, False, True)], axis=0
            )
        )
        m2 = split(
            jnp.concatenate(
                [block_matrix(w_outer, False, False), block_matrix(w_outer, True, False)], axis=1
            )
        )
        lane = jnp.arange(LANES, dtype=jnp.int32)[None]
        doubled = jnp.where((lat == 0) & (lane < 2 * BS), 1.0, 2.0).astype(F32)

    table_specs = [whole((H, 512)), whole((H, 512)), whole((GROUP, GROUP))]
    inverse_specs = [lane_block(1), whole((256, 448)), whole((256, 448))]
    params = pltpu.CompilerParams(vmem_limit_bytes=VMEM_BYTES)
    with jax.named_scope("spectral"):
        wire, spectrum, pre_modes = pl.pallas_call(
            spectral_kernel,
            grid=(3,),
            in_specs=[lane_block(256)]
            + table_specs
            + [whole((GROUP, GROUP))] * 2
            + [whole((GROUP, 2 * GROUP))] * 2
            + inverse_specs,
            out_specs=[lane_block(256), lane_block(H), lane_block(H)],
            out_shape=[wire_shape, shaped(H, LANES), shaped(H, LANES)],
            compiler_params=params,
        )(
            wire, lf_high, lf_low, swap, m1[0][:GROUP], m1[1][:GROUP], m2[0], m2[1], doubled,
            li_high, li_low,
        )
        wire = lax.all_to_all(wire, "lat", 0, 0, tiled=True)

    with jax.named_scope("mix"):
        mixed, chunks = call(
            mix_kernel,
            [shaped(ROWS, W, BS), shaped(N_CH, 8 * ROWS, 6 * BS)],
            wire, tt_high, tt_low, x, stats, gain_column,
            scratch=[scratch],
        )
        chunks = lax.all_to_all(chunks, "ch", 0, 0, tiled=True)

    cells = 48 * ROWS
    weight_spec = pl.BlockSpec((1, 2, 384, 384), lambda e: (e, 0, 0, 0))
    with jax.named_scope("mlp"):
        out_chunks, grad_chunks, grad_own, grad_other = pl.pallas_call(
            mlp_kernel,
            grid=(N_CH,),
            in_specs=[
                pl.BlockSpec(memory_space=pltpu.SMEM),
                whole((N_CH, 8 * ROWS, 6 * BS)),
                whole((N_CH, 8 * ROWS, 6 * BS)),
                whole((N_CH, 1, BS)),
                weight_spec,
                weight_spec,
            ],
            out_specs=[
                whole((N_CH, 8 * ROWS, 6 * BS)),
                whole((N_CH, 8 * ROWS + 8, 6 * BS)),
                weight_spec,
                weight_spec,
            ],
            out_shape=[
                shaped(N_CH, 8 * ROWS, 6 * BS, dtype=BF16),
                shaped(N_CH, 8 * ROWS + 8, 6 * BS, dtype=BF16),
                shaped(N_CH, 2, 384, 384),
                shaped(N_CH, 2, 384, 384, dtype=BF16),
            ],
            scratch_shapes=[
                pltpu.VMEM((cells, C), F32),
                pltpu.VMEM((cells, C), BF16),
                pltpu.VMEM((cells, C), BF16),
                pltpu.VMEM((cells, 128), F32),
                pltpu.VMEM((cells, C), F32),
                pltpu.VMEM((cells, C), F32),
            ],
            compiler_params=params,
        )(core[None].astype(jnp.int32), chunks, cot_chunks, gains, own, other)
        grad_chunks = lax.all_to_all(grad_chunks, "ch", 0, 0, tiled=True)

    with jax.named_scope("lon_back"):
        wire, grad_mixed, gain_parts = call(
            lon_back_kernel,
            [wire_shape, shaped(ROWS, BS, W, dtype=BF16), shaped(8, 128)],
            grad_chunks, x, stats, t_high, t_low,
            scratch=[scratch],
        )
        wire = lax.all_to_all(wire, "lat", 0, 0, tiled=True)

    with jax.named_scope("output"):
        out_chunks = lax.all_to_all(out_chunks, "ch", 0, 0, tiled=True)
        output = call(output_kernel, shaped(ROWS, BS, W, dtype=BF16), out_chunks, mixed)

    with jax.named_scope("spectral_back"):
        wire, blocks_outer, blocks_inner, gain_modes = pl.pallas_call(
            spectral_back_kernel,
            grid=(3,),
            in_specs=[lane_block(256), lane_block(H), lane_block(H)]
            + table_specs
            + [whole((2 * GROUP, GROUP))] * 2
            + [whole((GROUP, 2 * GROUP))] * 2
            + inverse_specs,
            out_specs=[lane_block(256), whole((GROUP, GROUP)), whole((GROUP, GROUP)), lane_block(1)],
            out_shape=[wire_shape, shaped(GROUP, GROUP), shaped(GROUP, GROUP), shaped(1, LANES)],
            compiler_params=params,
        )(
            wire, spectrum, pre_modes, lf_high, lf_low, swap, m1[0], m1[1], m2[0], m2[1], doubled,
            li_high, li_low,
        )
        wire = lax.all_to_all(wire, "lat", 0, 0, tiled=True)

    with jax.named_scope("unmix"):
        scaled, sums = call(
            unmix_kernel,
            [shaped(ROWS, BS, W), shaped(16, W)],
            wire, tt_high, tt_low, grad_mixed, x, stats, gain_column,
            scratch=[scratch],
        )
        back_stats = to_all(sums, "ch", N_CH)
        grad_fields = call(
            final_kernel, shaped(ROWS, BS, W, dtype=BF16), scaled, grad_mixed, x, stats, back_stats
        )

    with jax.named_scope("small_grads"):
        grad_gain_first = gain_parts[0, :BS] + (
            jnp.sum(gain_modes.reshape(PLANES, BS), 0) / gain_first
        )
        flat = jnp.concatenate(
            [
                weight_sum(blocks_inner).reshape(-1),
                weight_sum(blocks_outer).reshape(-1),
                grad_gain_first,
                gain_parts[1, :BS],
            ]
        )
        count = flat.shape[0]
        padded = -(-count // (N_LAT * 128)) * N_LAT * 128
        flat = jnp.pad(flat, (0, padded - count)).reshape(N_LAT, padded // N_LAT // 128, 128)
        flat = jnp.sum(lax.all_to_all(flat, "lat", 0, 0, tiled=True), 0)
        flat = to_all(flat, "lat", N_LAT).reshape(-1)
        size = 2 * BS * BS
        grad_w_inner = flat[:size].reshape(2, 1, BS, BS)
        grad_w_outer = flat[size : 2 * size].reshape(2, 1, BS, BS)
        grad_gain_first = flat[2 * size : 2 * size + BS]
        grad_gain_second = flat[2 * size + BS : 2 * size + 2 * BS]

    with jax.named_scope("weight_grads"):
        received = lax.ppermute(grad_other, "lat", siblings)
        partial = (grad_own + received.astype(F32)).astype(BF16)
        partial = lax.all_to_all(partial, "ch", 0, 0, tiled=True)
        partial = jnp.sum(partial.astype(F32), 0).astype(BF16).reshape(N_LAT // 2, 48, 384)
        partial = lax.all_to_all(partial, "lat", 0, 0, tiled=True, axis_index_groups=cores)
        partial = jnp.sum(partial.astype(F32), 0).astype(BF16)
        mine = to_all(partial, "lat", N_LAT // 2, axis_index_groups=cores)
        mine = mine.reshape(2, 384, 384)
        theirs = lax.ppermute(mine, "lat", siblings)
        low = jnp.where(core == 0, mine, theirs).astype(F32)
        high = jnp.where(core == 0, theirs, mine).astype(F32)
        grad_fc_in = jnp.concatenate([low[0], high[0]], axis=0)
        grad_fc_out = jnp.concatenate([low[1], high[1]], axis=1)

    return (
        output.transpose(1, 0, 2),
        grad_fields.transpose(1, 0, 2),
        grad_gain_first,
        grad_w_inner,
        grad_w_outer,
        grad_gain_second,
        grad_fc_in,
        grad_fc_out,
    )


def solution(mesh):
    placed = (
        P("ch", "lat", None),
        P("ch"),
        P(None, "ch", None, None),
        P(None, "ch", None, None),
        P("ch"),
        P(None, "ch"),
        P("ch", None),
        P("ch", "lat", None),
    )
    return jax.shard_map(
        body,
        mesh=mesh,
        in_specs=placed,
        out_specs=(
            P("ch", "lat", None),
            P("ch", "lat", None),
            P("ch"),
            P(None, "ch", None, None),
            P(None, "ch", None, None),
            P("ch"),
            P(None, "ch"),
            P("ch", None),
        ),
        check_vma=False,
    )
```

```python
import math

import jax
import jax.numpy as jnp
import ml_dtypes
import numpy as np
from jax import lax
from jax.experimental import pallas as pl
from jax.experimental.pallas import tpu as pltpu
from jax.sharding import PartitionSpec as P

C = 768
BS = 96
H = 224
W = 384
KW = 192
N_LAT = 32
N_CH = 8
ROWS = 7
FF_DEV = 384
MODES = KW // N_LAT
PLANES = 2 * MODES
LANES = PLANES * BS
GROUP = 384
EPSILON = 1e-05
BF16 = jnp.bfloat16
F32 = jnp.float32
VMEM_BYTES = 56 * 1024 * 1024


def halves(table):
    high = table.astype(ml_dtypes.bfloat16)
    low = (table - high.astype(np.float64)).astype(ml_dtypes.bfloat16)
    return high, low


def lon_table():
    mode = np.arange(MODES)[:, None] + MODES * np.arange(N_LAT)[None, :]
    angles = 2 * np.pi * ((mode[:, :, None] * np.arange(W)) % W) / W
    table = np.stack([np.cos(angles), -np.sin(angles)], 1) / math.sqrt(W)
    return table.reshape(PLANES * N_LAT, W)


def lat_tables():
    index = np.arange(H)
    angles = 2 * np.pi * ((index[:, None] * index[None, :]) % H) / H
    cosine = np.cos(angles) / math.sqrt(H)
    sine = np.sin(angles) / math.sqrt(H)
    forward = np.zeros((H, 2, N_LAT, 8))
    forward[:, 0, :, :ROWS] = cosine.reshape(H, N_LAT, ROWS)
    forward[:, 1, :, :ROWS] = sine.reshape(H, N_LAT, ROWS)
    inverse = np.zeros((N_LAT, 8, 2, H))
    inverse[:, :ROWS, 0] = cosine.reshape(N_LAT, ROWS, H)
    inverse[:, :ROWS, 1] = -sine.reshape(N_LAT, ROWS, H)
    return forward.reshape(H, 2 * N_LAT * 8), inverse.reshape(N_LAT * 8, 2 * H)


def swap_table():
    table = np.zeros((GROUP, GROUP))
    for mode in range(2):
        for c in range(BS):
            real = mode * 2 * BS + c
            table[real + BS, real] = 1
            table[real, real + BS] = -1
    return table.astype(ml_dtypes.bfloat16)


def dot(left, right):
    return lax.dot_general(left, right, (((1,), (0,)), ((), ())), preferred_element_type=F32)


def dot_nt(left, right):
    return lax.dot_general(left, right, (((1,), (1,)), ((), ())), preferred_element_type=F32)


def dot_tn(left, right):
    return lax.dot_general(left, right, (((0,), (0,)), ((), ())), preferred_element_type=F32)


def split(values):
    high = values.astype(BF16)
    return high, (values - high.astype(F32)).astype(BF16)


def dot3(kind, left, right):
    return kind(left[0], right[0]) + kind(left[1], right[0]) + kind(left[0], right[1])


def gelu_parts(values):
    cdf = 0.5 * (1.0 + lax.erf(values * 0.7071067811865476))
    return values * cdf, cdf + values * 0.3989422804014327 * jnp.exp(-0.5 * values * values)


def gelu_value(values):
    return 0.5 * values * (1.0 + lax.erf(values * 0.7071067811865476))


def norm_rows(stats):
    total = stats[0]
    for e in range(1, N_CH):
        total = total + stats[e]
    average = total[0:8] * (1.0 / C)
    squares = total[8:16] * (1.0 / C)
    return average, lax.rsqrt(squares - average * average + EPSILON)


def put_row(scratch, row, modes):
    wide = jnp.concatenate([modes[32 * k : 32 * k + 32] for k in range(PLANES)], axis=1)
    for t in range(LANES // 128):
        scratch[t, pl.ds(row, N_LAT, stride=8), :] = wide[:, 128 * t : 128 * t + 128]


def flush_rows(scratch, wire):
    for t in range(LANES // 128):
        scratch[t, pl.ds(ROWS, N_LAT, stride=8), :] = jnp.zeros((N_LAT, 128), F32)
        wire[:, 128 * t : 128 * t + 128] = scratch[t].astype(BF16)


def load_rows(wire, scratch):
    for t in range(LANES // 128):
        scratch[t] = wire[:, 128 * t : 128 * t + 128].astype(F32)


def get_row(scratch, row):
    wide = jnp.concatenate(
        [scratch[t, pl.ds(row, N_LAT, stride=8), :] for t in range(LANES // 128)], axis=1
    )
    return jnp.concatenate([wide[:, BS * k : BS * k + BS] for k in range(PLANES)], axis=0)


def to_chunk(rows, e):
    return jnp.concatenate(
        [
            jnp.concatenate(
                [values[48 * e + 8 * a : 48 * e + 8 * a + 8] for a in range(6)], axis=1
            )
            for values in rows
        ],
        axis=0,
    )


def from_chunks(chunks, row):
    return jnp.concatenate(
        [
            chunk[8 * row : 8 * row + 8, BS * a : BS * a + BS]
            for chunk in chunks
            for a in range(6)
        ],
        axis=0,
    )


def cot_kernel(place, cot, wire):
    rows = [cot[r].astype(F32).T for r in range(ROWS)]
    for e in range(N_CH):
        wire[e ^ place[0]] = to_chunk(rows, e).astype(BF16)


def lon_kernel(x, stats, gain, t_high, t_low, wire, scratch):
    average, inv_std = norm_rows(stats)
    table = (t_high[...], t_low[...])
    for r in range(ROWS):
        normed = (x[r].astype(F32) - average[r : r + 1]) * inv_std[r : r + 1]
        lifted = split(normed * gain[...])
        put_row(scratch, r, dot3(dot_nt, table, lifted))
    flush_rows(scratch, wire)


def lat_forward(wire, lf_high, lf_low, swap):
    values = wire[...]
    swapped = dot(values, swap[...]).astype(BF16)
    both = jnp.concatenate([values, swapped], axis=0)
    return dot(lf_high[...], both) + dot(lf_low[...], both)


def lat_inverse(modes, li_high, li_low):
    both = split(jnp.concatenate([modes[:, :GROUP], modes[:, GROUP:]], axis=0))
    return dot3(dot, (li_high[...], li_low[...]), both)


def weight_sum(blocks):
    def block(part, other):
        pieces = [
            blocks[m + BS * part : m + BS * part + BS, m + BS * other : m + BS * other + BS]
            for m in (0, 2 * BS)
        ]
        return pieces[0] + pieces[1]

    return jnp.concatenate(
        [block(0, 0) + block(1, 1), block(1, 0) - block(0, 1)], axis=0
    )


def spectral_kernel(
    wire, lf_high, lf_low, swap, m1_high, m1_low, m2_high, m2_low, doubled, li_high, li_low,
    out, spectrum, pre_modes,
):
    modes = lat_forward(wire, lf_high, lf_low, swap)
    spectrum[...] = modes
    pre = dot3(dot, split(modes), (m1_high[...], m1_low[...]))
    pre_modes[...] = pre
    act = split(gelu_value(pre))
    scale = doubled[...]
    result = dot3(dot, act, (m2_high[...], m2_low[...])) * jnp.concatenate([scale, scale], axis=1)
    out[...] = lat_inverse(result, li_high, li_low).astype(BF16)


def spectral_back_kernel(
    wire, spectrum, pre_modes, lf_high, lf_low, swap, m1_high, m1_low, m2_high, m2_low, doubled,
    li_high, li_low, gain, gain_parts, out, small, grad_outer, grad_inner, gain_sum,
):
    @pl.when(pl.program_id(0) == 0)
    def _():
        grad_outer[...] = jnp.zeros_like(grad_outer)
        grad_inner[...] = jnp.zeros_like(grad_inner)
        gain_sum[...] = jnp.zeros_like(gain_sum)

    grad = split(lat_forward(wire, lf_high, lf_low, swap) * doubled[...])
    act, slope = gelu_parts(pre_modes[...])
    grad_act = dot3(dot_nt, grad, (m2_high[:, :GROUP], m2_low[:, :GROUP]))
    grad_outer[...] += dot3(dot_tn, grad, split(act))
    grad_pre = split(grad_act * slope)
    modes = spectrum[...]
    grad_inner[...] += dot3(dot_tn, grad_pre, split(modes))
    grad_spectrum = dot3(dot_nt, grad_pre, (m1_high[...], m1_low[...]))
    gain_row = jnp.sum(grad_spectrum[:, :GROUP] * modes, axis=0, keepdims=True)
    gain_row = sum(gain_row[:, BS * k : BS * k + BS] for k in range(4))
    gain_sum[0:1, :BS] += gain_row
    out[...] = lat_inverse(grad_spectrum, li_high, li_low).astype(BF16)

    @pl.when(pl.program_id(0) == 2)
    def _():
        first = gain_sum[0:1, :BS] / gain[...] + gain_parts[0:1, :BS]
        for half, blocks, row in (
            (0, grad_inner[...], first),
            (1, grad_outer[...], gain_parts[1:2, :BS]),
        ):
            weight = weight_sum(blocks)
            for i in range(3):
                small[half, i] = jnp.concatenate(
                    [weight[48 * q + 16 * i : 48 * q + 16 * i + 16] for q in range(4)], axis=1
                )
            high = row.astype(BF16).astype(F32)
            row = jnp.concatenate([high, row - high, jnp.zeros((1, 2 * BS), F32)], axis=1)
            small[half, 3] = jnp.concatenate([row, jnp.zeros((15, 4 * BS), F32)], axis=0)


def mix_kernel(wire, tt_high, tt_low, x, stats, gain, mixed, chunks, scratch):
    average, inv_std = norm_rows(stats)
    load_rows(wire, scratch)
    rows = []
    for r in range(ROWS):
        x_float = x[r].astype(F32)
        lifted = (x_float - average[r : r + 1]) * inv_std[r : r + 1] * gain[...]
        modes = get_row(scratch, r).astype(BF16)
        filtered = dot(tt_high[...], modes) + dot(tt_low[...], modes)
        values = filtered + (lifted + x_float).T
        mixed[r] = values
        rows.append(values)
    for e in range(N_CH):
        chunks[e] = to_chunk(rows, e)


def mlp_kernel(
    core, mixed, cot, gain, own, other, out_chunks, grad_chunks, grad_own, grad_other,
    normed, inputs, cots, inv_std, sum_out, sum_grad,
):
    step = pl.program_id(0)
    turn = 4 * core[0]
    mixed_turn = turn ^ core[1]
    cells = 6 * 8 * ROWS
    part = 8 * ROWS

    def gain_row():
        return jnp.concatenate([gain[e ^ turn] for e in range(N_CH)], axis=1)

    @pl.when(step == 0)
    def _():
        pieces = [mixed[e ^ turn] for e in range(N_CH)]
        values = jnp.concatenate(
            [
                jnp.concatenate([piece[:, BS * a : BS * a + BS] for piece in pieces], axis=1)
                for a in range(6)
            ],
            axis=0,
        )
        average = jnp.sum(values, axis=1, keepdims=True) * (1.0 / C)
        squares = jnp.sum(values * values, axis=1, keepdims=True) * (1.0 / C)
        inv = lax.rsqrt(squares - average * average + EPSILON)
        values = (values - average) * inv
        normed[...] = values
        inv_std[...] = jnp.broadcast_to(inv, (cells, 128))
        inputs[...] = (values * gain_row()).astype(BF16)
        pieces = [cot[e ^ mixed_turn].astype(F32) for e in range(N_CH)]
        cots[...] = jnp.concatenate(
            [
                jnp.concatenate([piece[:, BS * a : BS * a + BS] for piece in pieces], axis=1)
                for a in range(6)
            ],
            axis=0,
        ).astype(BF16)
        sum_out[...] = jnp.zeros_like(sum_out)
        sum_grad[...] = jnp.zeros_like(sum_grad)

    first, second = inputs[:, :384], inputs[:, 384:]
    cot_first, cot_second = cots[:, :384], cots[:, 384:]
    in_own, out_own = own[0, 0], own[0, 1]
    in_other, out_other = other[0, 0], other[0, 1]
    pre_act = dot(first, in_own) + dot(second, in_other)
    hidden, slope = gelu_parts(pre_act)
    hidden = hidden.astype(BF16)
    grad_hidden = dot_nt(cot_first, out_own) + dot_nt(cot_second, out_other)
    grad_pre = (grad_hidden * slope).astype(BF16)
    sum_out[:, :384] += dot(hidden, out_own)
    sum_out[:, 384:] += dot(hidden, out_other)
    sum_grad[:, :384] += dot_nt(grad_pre, in_own)
    sum_grad[:, 384:] += dot_nt(grad_pre, in_other)
    grad_own[0, 0] = dot_tn(first, grad_pre)
    grad_other[0, 0] = dot_tn(second, grad_pre).astype(BF16)
    grad_own[0, 1] = dot_tn(hidden, cot_first)
    grad_other[0, 1] = dot_tn(hidden, cot_second).astype(BF16)

    @pl.when(step == N_CH - 1)
    def _():
        grad_input = sum_grad[...]
        values = normed[...]
        gain_sum = jnp.sum(grad_input * values, axis=0, keepdims=True)
        scaled = grad_input * gain_row()
        leading = jnp.sum(scaled, axis=1, keepdims=True) * (1.0 / C)
        paired = jnp.sum(scaled * values, axis=1, keepdims=True) * (1.0 / C)
        grad_mixed = cots[...].astype(F32) + inv_std[:, :1] * (scaled - leading - values * paired)
        outputs = sum_out[...]

        def chunk(array, e):
            return jnp.concatenate(
                [array[part * a : part * a + part, BS * e : BS * e + BS] for a in range(6)],
                axis=1,
            )

        for e in range(N_CH):
            out_chunks[e ^ mixed_turn] = chunk(outputs, e).astype(BF16)
            gain_piece = gain_sum[:, BS * e : BS * e + BS]
            gain_high = gain_piece.astype(BF16).astype(F32)
            extra = jnp.concatenate(
                [gain_high, gain_piece - gain_high, jnp.zeros((1, 4 * BS), F32)], axis=1
            )
            extra = jnp.concatenate([extra, jnp.zeros((7, 6 * BS), F32)], axis=0)
            grad_chunks[e ^ turn] = jnp.concatenate(
                [chunk(grad_mixed, e), extra], axis=0
            ).astype(BF16)


def lon_back_kernel(chunks, x, stats, t_high, t_low, wire, grad_mixed, gains, scratch):
    average, inv_std = norm_rows(stats)
    pieces = [chunks[e].astype(F32) for e in range(N_CH)]
    gain_first = jnp.zeros((BS, 1), F32)
    for r in range(ROWS):
        values = from_chunks(pieces, r)
        rounded = values.astype(BF16)
        put_row(scratch, r, dot(t_high[...], rounded) + dot(t_low[...], rounded))
        turned = values.T
        grad_mixed[r] = turned.astype(BF16)
        normed = (x[r].astype(F32) - average[r : r + 1]) * inv_std[r : r + 1]
        gain_first = gain_first + jnp.sum(turned * normed, axis=1, keepdims=True)
    flush_rows(scratch, wire)
    gain_second = jnp.zeros((1, BS), F32)
    for piece in pieces:
        row = piece[8 * ROWS : 8 * ROWS + 1]
        gain_second = gain_second + row[:, :BS] + row[:, BS : 2 * BS]
    turned_first = jnp.broadcast_to(gain_first, (BS, 128)).T[0:1, :]
    gains[0:1, :BS] = turned_first
    gains[1:2, :BS] = gain_second


def unmix_kernel(wire, tt_high, tt_low, grad_mixed, x, stats, gain, scaled, sums, scratch):
    average, inv_std = norm_rows(stats)
    load_rows(wire, scratch)
    for r in range(ROWS):
        modes = get_row(scratch, r).astype(BF16)
        back = dot(tt_high[...], modes) + dot(tt_low[...], modes)
        values = (back.T + grad_mixed[r].astype(F32)) * gain[...]
        normed = (x[r].astype(F32) - average[r : r + 1]) * inv_std[r : r + 1]
        scaled[r] = values
        sums[r : r + 1] = jnp.sum(values, axis=0, keepdims=True)
        sums[8 + r : 9 + r] = jnp.sum(values * normed, axis=0, keepdims=True)
    sums[7:8] = jnp.zeros((1, W), F32)
    sums[15:16] = jnp.zeros((1, W), F32)


def final_kernel(scaled, grad_mixed, x, stats, *rest):
    average, inv_std = norm_rows(stats)
    out = rest[-1]
    total = rest[0][...]
    for part in rest[1:-1]:
        total = total + part[...]
    total = total * (1.0 / C)
    for r in range(ROWS):
        inv = inv_std[r : r + 1]
        normed = (x[r].astype(F32) - average[r : r + 1]) * inv
        change = scaled[r] - total[r : r + 1] - normed * total[8 + r : 9 + r]
        out[r] = (grad_mixed[r].astype(F32) + inv * change).astype(BF16)


def collect_kernel(small, own, *rest):
    total = own[...]
    for part in rest[:-1]:
        total = total + part[...].astype(F32)
    out = rest[-1]
    out[:, :48] = total.reshape(16, 48, 384).astype(BF16)
    rows = [small[i] for i in range(4)]
    for n in range(16):
        out[n, 48:] = jnp.concatenate(
            [row[n : n + 1] for row in rows] + [jnp.zeros((12, 384), F32)], axis=0
        ).astype(BF16)


def spread_kernel(parts, out):
    total = parts[0].astype(F32)
    for n in range(1, 16):
        total = total + parts[n].astype(F32)
    total = total.astype(BF16)
    for n in range(16):
        out[n] = total


def finish_kernel(place, mine, theirs, grad_in, grad_out, grad_weights, grad_gains):
    first = place[0] == 0

    def ordered(take):
        one, two = take(mine), take(theirs)
        return jnp.where(first, one, two), jnp.where(first, two, one)

    def large(array):
        return array[:, :48].astype(F32).reshape(768, 384)

    low, high = ordered(large)
    grad_in[:384] = low[:384]
    grad_in[384:] = high[:384]
    grad_out[:, :384] = low[384:]
    grad_out[:, 384:] = high[384:]

    def small(array):
        return array[:, 48:].astype(F32).reshape(256, 384)

    for half, values in enumerate(ordered(small)):
        planes = [
            jnp.concatenate([values[16 * n + i : 16 * n + i + 1] for n in range(16)], axis=0)
            for i in range(3)
        ]
        grad_weights[half] = jnp.concatenate(
            [plane[:, BS * q : BS * q + BS] for q in range(4) for plane in planes], axis=0
        )
        grad_gains[half : half + 1] = values[3:4, :BS] + values[3:4, BS : 2 * BS]


def output_kernel(place, chunks, mixed, out):
    pieces = [chunks[e ^ place[0]].astype(F32) for e in range(N_CH)]
    for r in range(ROWS):
        out[r] = (from_chunks(pieces, r) + mixed[r]).T.astype(BF16)


def call(kernel, out_shape, *args, scratch=(), name=None, place=None):
    specs = [pl.BlockSpec(memory_space=pltpu.VMEM)] * len(args)
    if place is not None:
        args = (place,) + args
        specs = [pl.BlockSpec(memory_space=pltpu.SMEM)] + specs
    return pl.pallas_call(
        kernel,
        out_shape=out_shape,
        in_specs=specs,
        scratch_shapes=scratch,
        compiler_params=pltpu.CompilerParams(vmem_limit_bytes=VMEM_BYTES),
        name=name,
    )(*args)


def shaped(*shape, dtype=F32):
    return jax.ShapeDtypeStruct(shape, dtype)


def whole(shape):
    return pl.BlockSpec(shape, lambda g: (0,) * len(shape))


def lane_block(rows):
    return pl.BlockSpec((rows, GROUP), lambda g: (0, g))


def block_matrix(weight, swap_columns, swap_rows):
    real, imag = weight[0, 0].T, weight[1, 0].T
    base = [[real, imag], [-imag, real]]
    if swap_columns:
        base = [[imag, -real], [real, imag]]
    if swap_rows:
        base = [[-imag, real], [-real, -imag]]
    one = jnp.concatenate([jnp.concatenate(line, axis=1) for line in base], axis=0)
    zero = jnp.zeros_like(one)
    return jnp.concatenate(
        [jnp.concatenate([one, zero], axis=1), jnp.concatenate([zero, one], axis=1)], axis=0
    )


def to_all(values, axis, count, **kwargs):
    spread = jnp.broadcast_to(values[None], (count,) + values.shape)
    return lax.all_to_all(spread, axis, 0, 0, tiled=True, **kwargs)


def swap_all(chunks):
    return [chunks[0]] + [
        lax.ppermute(chunks[k], "ch", [(i, i ^ k) for i in range(N_CH)]) for k in range(1, N_CH)
    ]


def body(fields, gain_first, w_inner, w_outer, gain_second, fc_in, fc_out, cotangent):
    lat = lax.axis_index("lat")
    core = lat % 2
    me = lax.axis_index("ch")
    me_place = me[None].astype(jnp.int32)
    core_place = core[None].astype(jnp.int32)
    siblings = [(i, i ^ 1) for i in range(N_LAT)]
    cores = [list(range(0, N_LAT, 2)), list(range(1, N_LAT, 2))]
    t_high, t_low = (jnp.asarray(t) for t in halves(lon_table()))
    tt_high, tt_low = (jnp.asarray(t) for t in halves(lon_table().T))
    forward, inverse = lat_tables()
    lf_high, lf_low = (jnp.asarray(t) for t in halves(forward))
    li_high, li_low = (jnp.asarray(t) for t in halves(inverse))
    swap = jnp.asarray(swap_table())

    x = fields.transpose(1, 0, 2)
    cot = cotangent.transpose(1, 0, 2)
    gain_column = gain_first[:, None]

    with jax.named_scope("weights"):
        half_in = lax.dynamic_slice_in_dim(fc_in, core * 384, 384, 0)
        half_out = lax.dynamic_slice_in_dim(fc_out, core * 384, 384, 1)
        own = lax.all_gather(jnp.stack([half_in, half_out]), "ch")

    with jax.named_scope("stats"):
        x_float = x.astype(F32)
        zero = jnp.zeros((1, W), F32)
        payload = jnp.concatenate(
            [
                jnp.sum(x_float, 1),
                zero,
                jnp.sum(x_float * x_float, 1),
                zero,
                jnp.pad(gain_second, (0, W - BS))[None],
                jnp.zeros((7, W), F32),
            ],
            axis=0,
        )
        gathered = to_all(payload, "ch", N_CH)
        stats = gathered[:, :16]
        gains = gathered[:, 16:17, :BS]

    scratch = pltpu.VMEM((LANES // 128, 8 * N_LAT, 128), F32)
    wire_shape = shaped(8 * N_LAT, LANES, dtype=BF16)
    with jax.named_scope("lon"):
        wire = call(
            lon_kernel, wire_shape, x, stats, gain_column, t_high, t_low, scratch=[scratch]
        )
        wire = lax.all_to_all(wire, "lat", 0, 0, tiled=True)

    with jax.named_scope("cot"):
        cot_chunks = call(
            cot_kernel, shaped(N_CH, 8 * ROWS, 6 * BS, dtype=BF16), cot, place=me_place
        )
        cot_chunks = jnp.stack(swap_all(cot_chunks))

    with jax.named_scope("matrices"):
        m1 = split(
            jnp.concatenate(
                [block_matrix(w_inner, False, False), block_matrix(w_inner, False, True)], axis=0
            )
        )
        m2 = split(
            jnp.concatenate(
                [block_matrix(w_outer, False, False), block_matrix(w_outer, True, False)], axis=1
            )
        )
        lane = jnp.arange(LANES, dtype=jnp.int32)[None]
        doubled = jnp.where((lat == 0) & (lane < 2 * BS), 1.0, 2.0).astype(F32)

    table_specs = [whole((H, 512)), whole((H, 512)), whole((GROUP, GROUP))]
    inverse_specs = [lane_block(1), whole((256, 448)), whole((256, 448))]
    params = pltpu.CompilerParams(vmem_limit_bytes=VMEM_BYTES)
    with jax.named_scope("spectral"):
        wire, spectrum, pre_modes = pl.pallas_call(
            spectral_kernel,
            grid=(3,),
            in_specs=[lane_block(256)]
            + table_specs
            + [whole((GROUP, GROUP))] * 2
            + [whole((GROUP, 2 * GROUP))] * 2
            + inverse_specs,
            out_specs=[lane_block(256), lane_block(H), lane_block(H)],
            out_shape=[wire_shape, shaped(H, LANES), shaped(H, LANES)],
            compiler_params=params,
        )(
            wire, lf_high, lf_low, swap, m1[0][:GROUP], m1[1][:GROUP], m2[0], m2[1], doubled,
            li_high, li_low,
        )
        wire = lax.all_to_all(wire, "lat", 0, 0, tiled=True)

    with jax.named_scope("mix"):
        mixed, chunks = call(
            mix_kernel,
            [shaped(ROWS, W, BS), shaped(N_CH, 8 * ROWS, 6 * BS)],
            wire, tt_high, tt_low, x, stats, gain_column,
            scratch=[scratch],
        )
        own, chunks = lax.optimization_barrier((own, chunks))
        other = lax.ppermute(own, "lat", siblings)
        chunks = lax.all_to_all(chunks, "ch", 0, 0, tiled=True)

    cells = 48 * ROWS
    weight_spec = pl.BlockSpec((1, 2, 384, 384), lambda e: (e, 0, 0, 0))
    with jax.named_scope("mlp"):
        out_chunks, grad_chunks, grad_own, grad_other = pl.pallas_call(
            mlp_kernel,
            grid=(N_CH,),
            in_specs=[
                pl.BlockSpec(memory_space=pltpu.SMEM),
                whole((N_CH, 8 * ROWS, 6 * BS)),
                whole((N_CH, 8 * ROWS, 6 * BS)),
                whole((N_CH, 1, BS)),
                weight_spec,
                weight_spec,
            ],
            out_specs=[
                whole((N_CH, 8 * ROWS, 6 * BS)),
                whole((N_CH, 8 * ROWS + 8, 6 * BS)),
                weight_spec,
                weight_spec,
            ],
            out_shape=[
                shaped(N_CH, 8 * ROWS, 6 * BS, dtype=BF16),
                shaped(N_CH, 8 * ROWS + 8, 6 * BS, dtype=BF16),
                shaped(N_CH, 2, 384, 384),
                shaped(N_CH, 2, 384, 384, dtype=BF16),
            ],
            scratch_shapes=[
                pltpu.VMEM((cells, C), F32),
                pltpu.VMEM((cells, C), BF16),
                pltpu.VMEM((cells, C), BF16),
                pltpu.VMEM((cells, 128), F32),
                pltpu.VMEM((cells, C), F32),
                pltpu.VMEM((cells, C), F32),
            ],
            compiler_params=params,
        )(jnp.concatenate([core_place, me_place]), chunks, cot_chunks, gains, own, other)
        grad_chunks = lax.all_to_all(grad_chunks, "ch", 0, 0, tiled=True)

    with jax.named_scope("lon_back"):
        wire, grad_mixed, gain_parts = call(
            lon_back_kernel,
            [wire_shape, shaped(ROWS, BS, W, dtype=BF16), shaped(8, 128)],
            grad_chunks, x, stats, t_high, t_low,
            scratch=[scratch],
        )
        wire = lax.all_to_all(wire, "lat", 0, 0, tiled=True)

    with jax.named_scope("output"):
        out_chunks = jnp.stack(swap_all(out_chunks))
        output = call(
            output_kernel, shaped(ROWS, BS, W, dtype=BF16), out_chunks, mixed, place=me_place
        )

    with jax.named_scope("grads_ch"):
        received = lax.ppermute(grad_other, "lat", siblings)
        to_send = []
        for k in range(N_CH):
            mine = lax.dynamic_index_in_dim(grad_own, me ^ k, 0, keepdims=False)
            theirs = lax.dynamic_index_in_dim(received, me ^ k, 0, keepdims=False)
            mine = mine + theirs.astype(F32)
            to_send.append(mine if k == 0 else mine.astype(BF16))
        grad_parts = swap_all(to_send)

    with jax.named_scope("spectral_back"):
        wire, small = pl.pallas_call(
            spectral_back_kernel,
            grid=(3,),
            in_specs=[lane_block(256), lane_block(H), lane_block(H)]
            + table_specs
            + [whole((2 * GROUP, GROUP))] * 2
            + [whole((GROUP, 2 * GROUP))] * 2
            + inverse_specs
            + [whole((1, BS)), whole((8, 128))],
            out_specs=[lane_block(256), whole((2, 4, 16, 384))],
            out_shape=[wire_shape, shaped(2, 4, 16, 384)],
            scratch_shapes=[
                pltpu.VMEM((GROUP, GROUP), F32),
                pltpu.VMEM((GROUP, GROUP), F32),
                pltpu.VMEM((8, 128), F32),
            ],
            compiler_params=params,
        )(
            wire, spectrum, pre_modes, lf_high, lf_low, swap, m1[0], m1[1], m2[0], m2[1], doubled,
            li_high, li_low, gain_first[None], gain_parts,
        )
        small_send = lax.dynamic_index_in_dim(small, 1 - core, 0, keepdims=False)
        small_own = lax.dynamic_index_in_dim(small, core, 0, keepdims=False)
        small_sum = small_own + lax.ppermute(small_send, "lat", siblings)
        *grad_parts, wire = lax.optimization_barrier((*grad_parts, wire))
        wire = lax.all_to_all(wire, "lat", 0, 0, tiled=True)

    with jax.named_scope("grads_collect"):
        payload = call(
            collect_kernel, shaped(16, 64, 384, dtype=BF16), small_sum, *grad_parts
        )
        payload, wire = lax.optimization_barrier((payload, wire))

    with jax.named_scope("unmix"):
        scaled, sums = call(
            unmix_kernel,
            [shaped(ROWS, BS, W), shaped(16, W)],
            wire, tt_high, tt_low, grad_mixed, x, stats, gain_column,
            scratch=[scratch],
        )
        sums = [sums] + [
            lax.ppermute(sums, "ch", [(i, i ^ k) for i in range(N_CH)]) for k in range(1, N_CH)
        ]
        grad_fields = call(
            final_kernel, shaped(ROWS, BS, W, dtype=BF16), scaled, grad_mixed, x, stats, *sums
        )

    with jax.named_scope("grads_lat"):
        payload = lax.all_to_all(payload, "lat", 0, 0, tiled=True, axis_index_groups=cores)
        payload = call(spread_kernel, shaped(16, 64, 384, dtype=BF16), payload)
        mine = lax.all_to_all(payload, "lat", 0, 0, tiled=True, axis_index_groups=cores)
        theirs = lax.ppermute(mine, "lat", siblings)
        grad_fc_in, grad_fc_out, grad_weights, grad_gains = call(
            finish_kernel,
            [shaped(C, FF_DEV), shaped(FF_DEV, C), shaped(2, 2 * BS, BS), shaped(2, BS)],
            mine, theirs, place=core_place,
        )

    return (
        output.transpose(1, 0, 2),
        grad_fields.transpose(1, 0, 2),
        grad_gains[0],
        grad_weights[0].reshape(2, 1, BS, BS),
        grad_weights[1].reshape(2, 1, BS, BS),
        grad_gains[1],
        grad_fc_in,
        grad_fc_out,
    )


def solution(mesh):
    placed = (
        P("ch", "lat", None),
        P("ch"),
        P(None, "ch", None, None),
        P(None, "ch", None, None),
        P("ch"),
        P(None, "ch"),
        P("ch", None),
        P("ch", "lat", None),
    )
    return jax.shard_map(
        body,
        mesh=mesh,
        in_specs=placed,
        out_specs=(
            P("ch", "lat", None),
            P("ch", "lat", None),
            P("ch"),
            P(None, "ch", None, None),
            P(None, "ch", None, None),
            P("ch"),
            P(None, "ch"),
            P("ch", None),
        ),
        check_vma=False,
    )
```

```python
import math

import jax
import jax.numpy as jnp
import ml_dtypes
import numpy as np
from jax import lax
from jax.experimental import pallas as pl
from jax.experimental.pallas import tpu as pltpu
from jax.sharding import PartitionSpec as P

C = 768
BS = 96
H = 224
W = 384
KW = 192
N_LAT = 32
N_CH = 8
ROWS = 7
FF_DEV = 384
MODES = KW // N_LAT
PLANES = 2 * MODES
LANES = PLANES * BS
GROUP = 384
EPSILON = 1e-05
BF16 = jnp.bfloat16
F32 = jnp.float32
VMEM_BYTES = 56 * 1024 * 1024


def halves(table):
    high = table.astype(ml_dtypes.bfloat16)
    low = (table - high.astype(np.float64)).astype(ml_dtypes.bfloat16)
    return high, low


def lon_table():
    mode = np.arange(MODES)[:, None] + MODES * np.arange(N_LAT)[None, :]
    angles = 2 * np.pi * ((mode[:, :, None] * np.arange(W)) % W) / W
    table = np.stack([np.cos(angles), -np.sin(angles)], 1) / math.sqrt(W)
    return table.reshape(PLANES * N_LAT, W)


def lat_tables():
    index = np.arange(H)
    angles = 2 * np.pi * ((index[:, None] * index[None, :]) % H) / H
    cosine = np.cos(angles) / math.sqrt(H)
    sine = np.sin(angles) / math.sqrt(H)
    forward = np.zeros((H, 2, N_LAT, 8))
    forward[:, 0, :, :ROWS] = cosine.reshape(H, N_LAT, ROWS)
    forward[:, 1, :, :ROWS] = sine.reshape(H, N_LAT, ROWS)
    inverse = np.zeros((N_LAT, 8, 2, H))
    inverse[:, :ROWS, 0] = cosine.reshape(N_LAT, ROWS, H)
    inverse[:, :ROWS, 1] = -sine.reshape(N_LAT, ROWS, H)
    return forward.reshape(H, 2 * N_LAT * 8), inverse.reshape(N_LAT * 8, 2 * H)


def swap_table():
    table = np.zeros((GROUP, GROUP))
    for mode in range(2):
        for c in range(BS):
            real = mode * 2 * BS + c
            table[real + BS, real] = 1
            table[real, real + BS] = -1
    return table.astype(ml_dtypes.bfloat16)


def dot(left, right):
    return lax.dot_general(left, right, (((1,), (0,)), ((), ())), preferred_element_type=F32)


def dot_nt(left, right):
    return lax.dot_general(left, right, (((1,), (1,)), ((), ())), preferred_element_type=F32)


def dot_tn(left, right):
    return lax.dot_general(left, right, (((0,), (0,)), ((), ())), preferred_element_type=F32)


def split(values):
    high = values.astype(BF16)
    return high, (values - high.astype(F32)).astype(BF16)


def dot3(kind, left, right):
    return kind(left[0], right[0]) + kind(left[1], right[0]) + kind(left[0], right[1])


def gelu_parts(values):
    cdf = 0.5 * (1.0 + lax.erf(values * 0.7071067811865476))
    return values * cdf, cdf + values * 0.3989422804014327 * jnp.exp(-0.5 * values * values)


def gelu_value(values):
    return 0.5 * values * (1.0 + lax.erf(values * 0.7071067811865476))


def norm_rows(stats):
    total = stats[0]
    for e in range(1, N_CH):
        total = total + stats[e]
    average = total[0:8] * (1.0 / C)
    squares = total[8:16] * (1.0 / C)
    return average, lax.rsqrt(squares - average * average + EPSILON)


def put_row(scratch, row, modes):
    wide = jnp.concatenate([modes[32 * k : 32 * k + 32] for k in range(PLANES)], axis=1)
    for t in range(LANES // 128):
        scratch[t, pl.ds(row, N_LAT, stride=8), :] = wide[:, 128 * t : 128 * t + 128]


def flush_rows(scratch, wire):
    for t in range(LANES // 128):
        scratch[t, pl.ds(ROWS, N_LAT, stride=8), :] = jnp.zeros((N_LAT, 128), F32)
        wire[:, 128 * t : 128 * t + 128] = scratch[t].astype(BF16)


def load_rows(wire, scratch):
    for t in range(LANES // 128):
        scratch[t] = wire[:, 128 * t : 128 * t + 128].astype(F32)


def get_row(scratch, row):
    wide = jnp.concatenate(
        [scratch[t, pl.ds(row, N_LAT, stride=8), :] for t in range(LANES // 128)], axis=1
    )
    return jnp.concatenate([wide[:, BS * k : BS * k + BS] for k in range(PLANES)], axis=0)


def to_chunk(rows, e):
    return jnp.concatenate(
        [
            jnp.concatenate(
                [values[48 * e + 8 * a : 48 * e + 8 * a + 8] for a in range(6)], axis=1
            )
            for values in rows
        ],
        axis=0,
    )


def from_chunks(chunks, row):
    return jnp.concatenate(
        [
            chunk[8 * row : 8 * row + 8, BS * a : BS * a + BS]
            for chunk in chunks
            for a in range(6)
        ],
        axis=0,
    )


def cot_kernel(place, cot, wire):
    rows = [cot[r].astype(F32).T for r in range(ROWS)]
    for e in range(N_CH):
        wire[e ^ place[0]] = to_chunk(rows, e).astype(BF16)


def lon_kernel(x, stats, gain, t_high, t_low, wire, scratch):
    average, inv_std = norm_rows(stats)
    table = (t_high[...], t_low[...])
    for r in range(ROWS):
        normed = (x[r].astype(F32) - average[r : r + 1]) * inv_std[r : r + 1]
        lifted = split(normed * gain[...])
        put_row(scratch, r, dot3(dot_nt, table, lifted))
    flush_rows(scratch, wire)


def lat_forward(wire, lf_high, lf_low, swap):
    values = wire[...]
    swapped = dot(values, swap[...]).astype(BF16)
    both = jnp.concatenate([values, swapped], axis=0)
    return dot(lf_high[...], both) + dot(lf_low[...], both)


def lat_inverse(modes, li_high, li_low):
    both = split(jnp.concatenate([modes[:, :GROUP], modes[:, GROUP:]], axis=0))
    return dot3(dot, (li_high[...], li_low[...]), both)


def weight_sum(blocks):
    def block(part, other):
        pieces = [
            blocks[m + BS * part : m + BS * part + BS, m + BS * other : m + BS * other + BS]
            for m in (0, 2 * BS)
        ]
        return pieces[0] + pieces[1]

    return jnp.concatenate(
        [block(0, 0) + block(1, 1), block(1, 0) - block(0, 1)], axis=0
    )


def spectral_kernel(
    wire, lf_high, lf_low, swap, m1_high, m1_low, m2_high, m2_low, doubled, li_high, li_low,
    out, spectrum, pre_modes,
):
    modes = lat_forward(wire, lf_high, lf_low, swap)
    spectrum[...] = modes
    pre = dot3(dot, split(modes), (m1_high[...], m1_low[...]))
    pre_modes[...] = pre
    act = split(gelu_value(pre))
    scale = doubled[...]
    result = dot3(dot, act, (m2_high[...], m2_low[...])) * jnp.concatenate([scale, scale], axis=1)
    out[...] = lat_inverse(result, li_high, li_low).astype(BF16)


def spectral_back_kernel(
    wire, spectrum, pre_modes, lf_high, lf_low, swap, m1_high, m1_low, m2_high, m2_low, doubled,
    li_high, li_low, gain, gain_parts, out, small, grad_outer, grad_inner, gain_sum,
):
    @pl.when(pl.program_id(0) == 0)
    def _():
        grad_outer[...] = jnp.zeros_like(grad_outer)
        grad_inner[...] = jnp.zeros_like(grad_inner)
        gain_sum[...] = jnp.zeros_like(gain_sum)

    grad = split(lat_forward(wire, lf_high, lf_low, swap) * doubled[...])
    act, slope = gelu_parts(pre_modes[...])
    grad_act = dot3(dot_nt, grad, (m2_high[:, :GROUP], m2_low[:, :GROUP]))
    grad_outer[...] += dot3(dot_tn, grad, split(act))
    grad_pre = split(grad_act * slope)
    modes = spectrum[...]
    grad_inner[...] += dot3(dot_tn, grad_pre, split(modes))
    grad_spectrum = dot3(dot_nt, grad_pre, (m1_high[...], m1_low[...]))
    gain_row = jnp.sum(grad_spectrum[:, :GROUP] * modes, axis=0, keepdims=True)
    gain_row = sum(gain_row[:, BS * k : BS * k + BS] for k in range(4))
    gain_sum[0:1, :BS] += gain_row
    out[...] = lat_inverse(grad_spectrum, li_high, li_low).astype(BF16)

    @pl.when(pl.program_id(0) == 2)
    def _():
        first = gain_sum[0:1, :BS] / gain[...] + gain_parts[0:1, :BS]
        for half, blocks, row in (
            (0, grad_inner[...], first),
            (1, grad_outer[...], gain_parts[1:2, :BS]),
        ):
            weight = weight_sum(blocks)
            for i in range(3):
                small[half, i] = jnp.concatenate(
                    [weight[48 * q + 16 * i : 48 * q + 16 * i + 16] for q in range(4)], axis=1
                )
            high = row.astype(BF16).astype(F32)
            row = jnp.concatenate([high, row - high, jnp.zeros((1, 2 * BS), F32)], axis=1)
            small[half, 3] = jnp.concatenate([row, jnp.zeros((15, 4 * BS), F32)], axis=0)


def mix_kernel(wire, tt_high, tt_low, x, stats, gain, mixed, chunks, scratch):
    average, inv_std = norm_rows(stats)
    load_rows(wire, scratch)
    rows = []
    for r in range(ROWS):
        x_float = x[r].astype(F32)
        lifted = (x_float - average[r : r + 1]) * inv_std[r : r + 1] * gain[...]
        modes = get_row(scratch, r).astype(BF16)
        filtered = dot(tt_high[...], modes) + dot(tt_low[...], modes)
        values = filtered + (lifted + x_float).T
        mixed[r] = values
        rows.append(values)
    for e in range(N_CH):
        chunks[e] = to_chunk(rows, e)


def mlp_kernel(
    core, mixed, cot, gain, own_in, other_in, own_out, other_out,
    out_chunks, grad_chunks, grad_own, grad_other,
    normed, inputs, cots, inv_std, sum_out, sum_grad,
):
    step = pl.program_id(0)
    turn = 4 * core[0]
    mixed_turn = turn ^ core[1]
    cells = 6 * 8 * ROWS
    part = 8 * ROWS

    def gain_row():
        return jnp.concatenate([gain[e ^ turn] for e in range(N_CH)], axis=1)

    @pl.when(step == 0)
    def _():
        pieces = [mixed[e ^ turn] for e in range(N_CH)]
        values = jnp.concatenate(
            [
                jnp.concatenate([piece[:, BS * a : BS * a + BS] for piece in pieces], axis=1)
                for a in range(6)
            ],
            axis=0,
        )
        average = jnp.sum(values, axis=1, keepdims=True) * (1.0 / C)
        squares = jnp.sum(values * values, axis=1, keepdims=True) * (1.0 / C)
        inv = lax.rsqrt(squares - average * average + EPSILON)
        values = (values - average) * inv
        normed[...] = values
        inv_std[...] = jnp.broadcast_to(inv, (cells, 128))
        inputs[...] = (values * gain_row()).astype(BF16)
        pieces = [cot[e ^ mixed_turn].astype(F32) for e in range(N_CH)]
        cots[...] = jnp.concatenate(
            [
                jnp.concatenate([piece[:, BS * a : BS * a + BS] for piece in pieces], axis=1)
                for a in range(6)
            ],
            axis=0,
        ).astype(BF16)
        sum_out[...] = jnp.zeros_like(sum_out)
        sum_grad[...] = jnp.zeros_like(sum_grad)

    first, second = inputs[:, :384], inputs[:, 384:]
    cot_first, cot_second = cots[:, :384], cots[:, 384:]
    in_own, out_own = own_in[0], own_out[0]
    in_other, out_other = other_in[0], other_out[0]
    pre_act = dot(first, in_own) + dot(second, in_other)
    hidden, slope = gelu_parts(pre_act)
    hidden = hidden.astype(BF16)
    grad_hidden = dot_nt(cot_first, out_own) + dot_nt(cot_second, out_other)
    grad_pre = (grad_hidden * slope).astype(BF16)
    sum_out[:, :384] += dot(hidden, out_own)
    sum_out[:, 384:] += dot(hidden, out_other)
    sum_grad[:, :384] += dot_nt(grad_pre, in_own)
    sum_grad[:, 384:] += dot_nt(grad_pre, in_other)
    grad_own[0, 0] = dot_tn(first, grad_pre)
    grad_other[0, 0] = dot_tn(second, grad_pre).astype(BF16)
    grad_own[0, 1] = dot_tn(hidden, cot_first)
    grad_other[0, 1] = dot_tn(hidden, cot_second).astype(BF16)

    @pl.when(step == N_CH - 1)
    def _():
        grad_input = sum_grad[...]
        values = normed[...]
        gain_sum = jnp.sum(grad_input * values, axis=0, keepdims=True)
        scaled = grad_input * gain_row()
        leading = jnp.sum(scaled, axis=1, keepdims=True) * (1.0 / C)
        paired = jnp.sum(scaled * values, axis=1, keepdims=True) * (1.0 / C)
        grad_mixed = cots[...].astype(F32) + inv_std[:, :1] * (scaled - leading - values * paired)
        outputs = sum_out[...]

        def chunk(array, e):
            return jnp.concatenate(
                [array[part * a : part * a + part, BS * e : BS * e + BS] for a in range(6)],
                axis=1,
            )

        for e in range(N_CH):
            out_chunks[e ^ mixed_turn] = chunk(outputs, e).astype(BF16)
            gain_piece = gain_sum[:, BS * e : BS * e + BS]
            gain_high = gain_piece.astype(BF16).astype(F32)
            extra = jnp.concatenate(
                [gain_high, gain_piece - gain_high, jnp.zeros((1, 4 * BS), F32)], axis=1
            )
            extra = jnp.concatenate([extra, jnp.zeros((7, 6 * BS), F32)], axis=0)
            grad_chunks[e ^ turn] = jnp.concatenate(
                [chunk(grad_mixed, e), extra], axis=0
            ).astype(BF16)


def lon_back_kernel(chunks, x, stats, t_high, t_low, wire, grad_mixed, gains, scratch):
    average, inv_std = norm_rows(stats)
    pieces = [chunks[e].astype(F32) for e in range(N_CH)]
    gain_first = jnp.zeros((BS, 1), F32)
    for r in range(ROWS):
        values = from_chunks(pieces, r)
        rounded = values.astype(BF16)
        put_row(scratch, r, dot(t_high[...], rounded) + dot(t_low[...], rounded))
        turned = values.T
        grad_mixed[r] = turned.astype(BF16)
        normed = (x[r].astype(F32) - average[r : r + 1]) * inv_std[r : r + 1]
        gain_first = gain_first + jnp.sum(turned * normed, axis=1, keepdims=True)
    flush_rows(scratch, wire)
    gain_second = jnp.zeros((1, BS), F32)
    for piece in pieces:
        row = piece[8 * ROWS : 8 * ROWS + 1]
        gain_second = gain_second + row[:, :BS] + row[:, BS : 2 * BS]
    turned_first = jnp.broadcast_to(gain_first, (BS, 128)).T[0:1, :]
    gains[0:1, :BS] = turned_first
    gains[1:2, :BS] = gain_second


def unmix_kernel(wire, tt_high, tt_low, grad_mixed, x, stats, gain, scaled, sums, scratch):
    average, inv_std = norm_rows(stats)
    load_rows(wire, scratch)
    for r in range(ROWS):
        modes = get_row(scratch, r).astype(BF16)
        back = dot(tt_high[...], modes) + dot(tt_low[...], modes)
        values = (back.T + grad_mixed[r].astype(F32)) * gain[...]
        normed = (x[r].astype(F32) - average[r : r + 1]) * inv_std[r : r + 1]
        scaled[r] = values
        sums[r : r + 1] = jnp.sum(values, axis=0, keepdims=True)
        sums[8 + r : 9 + r] = jnp.sum(values * normed, axis=0, keepdims=True)
    sums[7:8] = jnp.zeros((1, W), F32)
    sums[15:16] = jnp.zeros((1, W), F32)


def final_kernel(scaled, grad_mixed, x, stats, *rest):
    average, inv_std = norm_rows(stats)
    out = rest[-1]
    total = rest[0][...]
    for part in rest[1:-1]:
        total = total + part[...]
    total = total * (1.0 / C)
    for r in range(ROWS):
        inv = inv_std[r : r + 1]
        normed = (x[r].astype(F32) - average[r : r + 1]) * inv
        change = scaled[r] - total[r : r + 1] - normed * total[8 + r : 9 + r]
        out[r] = (grad_mixed[r].astype(F32) + inv * change).astype(BF16)


def collect_kernel(small, own, *rest):
    total = own[...]
    for part in rest[:-1]:
        total = total + part[...].astype(F32)
    out = rest[-1]
    out[:, :48] = total.reshape(16, 48, 384).astype(BF16)
    rows = [small[i] for i in range(4)]
    for n in range(16):
        out[n, 48:] = jnp.concatenate(
            [row[n : n + 1] for row in rows] + [jnp.zeros((4, 384), F32)], axis=0
        ).astype(BF16)


def spread_kernel(parts, out):
    total = parts[0].astype(F32)
    for n in range(1, 16):
        total = total + parts[n].astype(F32)
    total = total.astype(BF16)
    for n in range(16):
        out[n] = total


def finish_kernel(place, mine, theirs, grad_in, grad_out, grad_weights, grad_gains):
    first = place[0] == 0

    def ordered(take):
        one, two = take(mine), take(theirs)
        return jnp.where(first, one, two), jnp.where(first, two, one)

    def large(array):
        return array[:, :48].astype(F32).reshape(768, 384)

    low, high = ordered(large)
    grad_in[:384] = low[:384]
    grad_in[384:] = high[:384]
    grad_out[:, :384] = low[384:]
    grad_out[:, 384:] = high[384:]

    def small(array):
        return array[:, 48:].astype(F32).reshape(128, 384)

    for half, values in enumerate(ordered(small)):
        planes = [
            jnp.concatenate([values[8 * n + i : 8 * n + i + 1] for n in range(16)], axis=0)
            for i in range(3)
        ]
        grad_weights[half] = jnp.concatenate(
            [plane[:, BS * q : BS * q + BS] for q in range(4) for plane in planes], axis=0
        )
        grad_gains[half : half + 1] = values[3:4, :BS] + values[3:4, BS : 2 * BS]


def output_kernel(place, chunks, mixed, out):
    pieces = [chunks[e ^ place[0]].astype(F32) for e in range(N_CH)]
    for r in range(ROWS):
        out[r] = (from_chunks(pieces, r) + mixed[r]).T.astype(BF16)


def call(kernel, out_shape, *args, scratch=(), name=None, place=None):
    specs = [pl.BlockSpec(memory_space=pltpu.VMEM)] * len(args)
    if place is not None:
        args = (place,) + args
        specs = [pl.BlockSpec(memory_space=pltpu.SMEM)] + specs
    return pl.pallas_call(
        kernel,
        out_shape=out_shape,
        in_specs=specs,
        scratch_shapes=scratch,
        compiler_params=pltpu.CompilerParams(vmem_limit_bytes=VMEM_BYTES),
        name=name,
    )(*args)


def shaped(*shape, dtype=F32):
    return jax.ShapeDtypeStruct(shape, dtype)


def whole(shape):
    return pl.BlockSpec(shape, lambda g: (0,) * len(shape))


def lane_block(rows):
    return pl.BlockSpec((rows, GROUP), lambda g: (0, g))


def block_matrix(weight, swap_columns, swap_rows):
    real, imag = weight[0, 0].T, weight[1, 0].T
    base = [[real, imag], [-imag, real]]
    if swap_columns:
        base = [[imag, -real], [real, imag]]
    if swap_rows:
        base = [[-imag, real], [-real, -imag]]
    one = jnp.concatenate([jnp.concatenate(line, axis=1) for line in base], axis=0)
    zero = jnp.zeros_like(one)
    return jnp.concatenate(
        [jnp.concatenate([one, zero], axis=1), jnp.concatenate([zero, one], axis=1)], axis=0
    )


def to_all(values, axis, count, **kwargs):
    spread = jnp.broadcast_to(values[None], (count,) + values.shape)
    return lax.all_to_all(spread, axis, 0, 0, tiled=True, **kwargs)


def swap_all(chunks):
    return [chunks[0]] + [
        lax.ppermute(chunks[k], "ch", [(i, i ^ k) for i in range(N_CH)]) for k in range(1, N_CH)
    ]


def body(fields, gain_first, w_inner, w_outer, gain_second, fc_in, fc_out, cotangent):
    lat = lax.axis_index("lat")
    core = lat % 2
    me = lax.axis_index("ch")
    me_place = me[None].astype(jnp.int32)
    core_place = core[None].astype(jnp.int32)
    siblings = [(i, i ^ 1) for i in range(N_LAT)]
    cores = [list(range(0, N_LAT, 2)), list(range(1, N_LAT, 2))]
    t_high, t_low = (jnp.asarray(t) for t in halves(lon_table()))
    tt_high, tt_low = (jnp.asarray(t) for t in halves(lon_table().T))
    forward, inverse = lat_tables()
    lf_high, lf_low = (jnp.asarray(t) for t in halves(forward))
    li_high, li_low = (jnp.asarray(t) for t in halves(inverse))
    swap = jnp.asarray(swap_table())

    x = fields.transpose(1, 0, 2)
    cot = cotangent.transpose(1, 0, 2)
    gain_column = gain_first[:, None]

    with jax.named_scope("weights"):
        half_in = lax.dynamic_slice_in_dim(fc_in, core * 384, 384, 0)
        half_out = lax.dynamic_slice_in_dim(fc_out, core * 384, 384, 1)
        own_in = lax.all_gather(half_in, "ch")
        own_out = jnp.stack(swap_all([half_out] * N_CH))

    with jax.named_scope("stats"):
        x_float = x.astype(F32)
        zero = jnp.zeros((1, W), F32)
        payload = jnp.concatenate(
            [
                jnp.sum(x_float, 1),
                zero,
                jnp.sum(x_float * x_float, 1),
                zero,
                jnp.pad(gain_second, (0, W - BS))[None],
                jnp.zeros((7, W), F32),
            ],
            axis=0,
        )
        gathered = to_all(payload, "ch", N_CH)
        stats = gathered[:, :16]
        gains = gathered[:, 16:17, :BS]

    scratch = pltpu.VMEM((LANES // 128, 8 * N_LAT, 128), F32)
    wire_shape = shaped(8 * N_LAT, LANES, dtype=BF16)
    with jax.named_scope("lon"):
        wire = call(
            lon_kernel, wire_shape, x, stats, gain_column, t_high, t_low, scratch=[scratch]
        )
        wire = lax.all_to_all(wire, "lat", 0, 0, tiled=True)

    with jax.named_scope("cot"):
        cot_chunks = call(
            cot_kernel, shaped(N_CH, 8 * ROWS, 6 * BS, dtype=BF16), cot, place=me_place
        )
        cot_chunks = swap_all(cot_chunks)
        *cot_chunks, wire = lax.optimization_barrier((*cot_chunks, wire))
        cot_chunks = jnp.stack(cot_chunks)

    with jax.named_scope("matrices"):
        m1 = split(
            jnp.concatenate(
                [block_matrix(w_inner, False, False), block_matrix(w_inner, False, True)], axis=0
            )
        )
        m2 = split(
            jnp.concatenate(
                [block_matrix(w_outer, False, False), block_matrix(w_outer, True, False)], axis=1
            )
        )
        lane = jnp.arange(LANES, dtype=jnp.int32)[None]
        doubled = jnp.where((lat == 0) & (lane < 2 * BS), 1.0, 2.0).astype(F32)

    table_specs = [whole((H, 512)), whole((H, 512)), whole((GROUP, GROUP))]
    inverse_specs = [lane_block(1), whole((256, 448)), whole((256, 448))]
    params = pltpu.CompilerParams(vmem_limit_bytes=VMEM_BYTES)
    with jax.named_scope("spectral"):
        wire, spectrum, pre_modes = pl.pallas_call(
            spectral_kernel,
            grid=(3,),
            in_specs=[lane_block(256)]
            + table_specs
            + [whole((GROUP, GROUP))] * 2
            + [whole((GROUP, 2 * GROUP))] * 2
            + inverse_specs,
            out_specs=[lane_block(256), lane_block(H), lane_block(H)],
            out_shape=[wire_shape, shaped(H, LANES), shaped(H, LANES)],
            compiler_params=params,
        )(
            wire, lf_high, lf_low, swap, m1[0][:GROUP], m1[1][:GROUP], m2[0], m2[1], doubled,
            li_high, li_low,
        )
        wire = lax.all_to_all(wire, "lat", 0, 0, tiled=True)

    with jax.named_scope("mix"):
        mixed, chunks = call(
            mix_kernel,
            [shaped(ROWS, W, BS), shaped(N_CH, 8 * ROWS, 6 * BS)],
            wire, tt_high, tt_low, x, stats, gain_column,
            scratch=[scratch],
        )
        own_in, own_out, _ = lax.optimization_barrier((own_in, own_out, chunks))
        other_in = lax.ppermute(own_in, "lat", siblings)
        other_out = lax.ppermute(own_out, "lat", siblings)
        chunks = lax.all_to_all(chunks, "ch", 0, 0, tiled=True)

    cells = 48 * ROWS
    direct = pl.BlockSpec((1, 384, 384), lambda e, place: (e ^ place[1], 0, 0))
    turned = pl.BlockSpec((1, 384, 384), lambda e, place: (e, 0, 0))
    grad_spec = pl.BlockSpec((1, 2, 384, 384), lambda e, place: (e, 0, 0, 0))

    def all_of(shape):
        return pl.BlockSpec(shape, lambda e, place: (0,) * len(shape))

    with jax.named_scope("mlp"):
        out_chunks, grad_chunks, grad_own, grad_other = pl.pallas_call(
            mlp_kernel,
            grid_spec=pltpu.PrefetchScalarGridSpec(
                num_scalar_prefetch=1,
                grid=(N_CH,),
                in_specs=[
                    all_of((N_CH, 8 * ROWS, 6 * BS)),
                    all_of((N_CH, 8 * ROWS, 6 * BS)),
                    all_of((N_CH, 1, BS)),
                    direct,
                    direct,
                    turned,
                    turned,
                ],
                out_specs=[
                    all_of((N_CH, 8 * ROWS, 6 * BS)),
                    all_of((N_CH, 8 * ROWS + 8, 6 * BS)),
                    grad_spec,
                    grad_spec,
                ],
                scratch_shapes=[
                    pltpu.VMEM((cells, C), F32),
                    pltpu.VMEM((cells, C), BF16),
                    pltpu.VMEM((cells, C), BF16),
                    pltpu.VMEM((cells, 128), F32),
                    pltpu.VMEM((cells, C), F32),
                    pltpu.VMEM((cells, C), F32),
                ],
            ),
            out_shape=[
                shaped(N_CH, 8 * ROWS, 6 * BS, dtype=BF16),
                shaped(N_CH, 8 * ROWS + 8, 6 * BS, dtype=BF16),
                shaped(N_CH, 2, 384, 384),
                shaped(N_CH, 2, 384, 384, dtype=BF16),
            ],
            compiler_params=params,
        )(jnp.concatenate([core_place, me_place]), chunks, cot_chunks, gains,
          own_in, other_in, own_out, other_out)
        grad_chunks = lax.all_to_all(grad_chunks, "ch", 0, 0, tiled=True)

    with jax.named_scope("lon_back"):
        wire, grad_mixed, gain_parts = call(
            lon_back_kernel,
            [wire_shape, shaped(ROWS, BS, W, dtype=BF16), shaped(8, 128)],
            grad_chunks, x, stats, t_high, t_low,
            scratch=[scratch],
        )
        wire = lax.all_to_all(wire, "lat", 0, 0, tiled=True)

    with jax.named_scope("output"):
        out_chunks = jnp.stack(swap_all(out_chunks))
        output = call(
            output_kernel, shaped(ROWS, BS, W, dtype=BF16), out_chunks, mixed, place=me_place
        )

    with jax.named_scope("grads_ch"):
        received = lax.ppermute(grad_other, "lat", siblings)
        to_send = []
        for k in range(N_CH):
            mine = grad_own[k] + received[k].astype(F32)
            to_send.append(mine if k == 0 else mine.astype(BF16))
        grad_parts = swap_all(to_send)

    with jax.named_scope("spectral_back"):
        wire, small = pl.pallas_call(
            spectral_back_kernel,
            grid=(3,),
            in_specs=[lane_block(256), lane_block(H), lane_block(H)]
            + table_specs
            + [whole((2 * GROUP, GROUP))] * 2
            + [whole((GROUP, 2 * GROUP))] * 2
            + inverse_specs
            + [whole((1, BS)), whole((8, 128))],
            out_specs=[lane_block(256), whole((2, 4, 16, 384))],
            out_shape=[wire_shape, shaped(2, 4, 16, 384)],
            scratch_shapes=[
                pltpu.VMEM((GROUP, GROUP), F32),
                pltpu.VMEM((GROUP, GROUP), F32),
                pltpu.VMEM((8, 128), F32),
            ],
            compiler_params=params,
        )(
            wire, spectrum, pre_modes, lf_high, lf_low, swap, m1[0], m1[1], m2[0], m2[1], doubled,
            li_high, li_low, gain_first[None], gain_parts,
        )
        small_send = lax.dynamic_index_in_dim(small, 1 - core, 0, keepdims=False)
        small_own = lax.dynamic_index_in_dim(small, core, 0, keepdims=False)
        small_sum = small_own + lax.ppermute(small_send, "lat", siblings)
        *grad_parts, _ = lax.optimization_barrier((*grad_parts, wire))
        wire = lax.all_to_all(wire, "lat", 0, 0, tiled=True)

    with jax.named_scope("grads_collect"):
        payload = call(
            collect_kernel, shaped(16, 56, 384, dtype=BF16), small_sum, *grad_parts
        )
        payload, wire = lax.optimization_barrier((payload, wire))

    with jax.named_scope("unmix"):
        scaled, sums = call(
            unmix_kernel,
            [shaped(ROWS, BS, W), shaped(16, W)],
            wire, tt_high, tt_low, grad_mixed, x, stats, gain_column,
            scratch=[scratch],
        )
    with jax.named_scope("grads_lat"):
        payload = lax.all_to_all(payload, "lat", 0, 0, tiled=True, axis_index_groups=cores)
        payload, _ = lax.optimization_barrier((payload, sums))
        sums = [sums] + [
            lax.ppermute(sums, "ch", [(i, i ^ k) for i in range(N_CH)]) for k in range(1, N_CH)
        ]
        grad_fields = call(
            final_kernel, shaped(ROWS, BS, W, dtype=BF16), scaled, grad_mixed, x, stats, *sums
        )
        payload = call(spread_kernel, shaped(16, 56, 384, dtype=BF16), payload)
        mine = lax.all_to_all(payload, "lat", 0, 0, tiled=True, axis_index_groups=cores)
        theirs = lax.ppermute(mine, "lat", siblings)
        grad_fc_in, grad_fc_out, grad_weights, grad_gains = call(
            finish_kernel,
            [shaped(C, FF_DEV), shaped(FF_DEV, C), shaped(2, 2 * BS, BS), shaped(2, BS)],
            mine, theirs, place=core_place,
        )

    return (
        output.transpose(1, 0, 2),
        grad_fields.transpose(1, 0, 2),
        grad_gains[0],
        grad_weights[0].reshape(2, 1, BS, BS),
        grad_weights[1].reshape(2, 1, BS, BS),
        grad_gains[1],
        grad_fc_in,
        grad_fc_out,
    )


def solution(mesh):
    placed = (
        P("ch", "lat", None),
        P("ch"),
        P(None, "ch", None, None),
        P(None, "ch", None, None),
        P("ch"),
        P(None, "ch"),
        P("ch", None),
        P("ch", "lat", None),
    )
    return jax.shard_map(
        body,
        mesh=mesh,
        in_specs=placed,
        out_specs=(
            P("ch", "lat", None),
            P("ch", "lat", None),
            P("ch"),
            P(None, "ch", None, None),
            P(None, "ch", None, None),
            P("ch"),
            P(None, "ch"),
            P("ch", None),
        ),
        check_vma=False,
    )
```

```python
import math

import jax
import jax.numpy as jnp
import ml_dtypes
import numpy as np
from jax import lax
from jax.experimental import pallas as pl
from jax.experimental.pallas import tpu as pltpu
from jax.sharding import PartitionSpec as P

C = 768
BS = 96
H = 224
W = 384
KW = 192
N_LAT = 32
N_CH = 8
ROWS = 7
FF_DEV = 384
MODES = KW // N_LAT
PLANES = 2 * MODES
LANES = PLANES * BS
GROUP = 384
EPSILON = 1e-05
BF16 = jnp.bfloat16
F32 = jnp.float32
VMEM_BYTES = 56 * 1024 * 1024


def halves(table):
    high = table.astype(ml_dtypes.bfloat16)
    low = (table - high.astype(np.float64)).astype(ml_dtypes.bfloat16)
    return high, low


def lon_table():
    mode = np.arange(MODES)[:, None] + MODES * np.arange(N_LAT)[None, :]
    angles = 2 * np.pi * ((mode[:, :, None] * np.arange(W)) % W) / W
    table = np.stack([np.cos(angles), -np.sin(angles)], 1) / math.sqrt(W)
    return table.reshape(PLANES * N_LAT, W)


def lat_tables():
    index = np.arange(H)
    angles = 2 * np.pi * ((index[:, None] * index[None, :]) % H) / H
    cosine = np.cos(angles) / math.sqrt(H)
    sine = np.sin(angles) / math.sqrt(H)
    forward = np.zeros((H, 2, N_LAT, 8))
    forward[:, 0, :, :ROWS] = cosine.reshape(H, N_LAT, ROWS)
    forward[:, 1, :, :ROWS] = sine.reshape(H, N_LAT, ROWS)
    inverse = np.zeros((N_LAT, 8, 2, H))
    inverse[:, :ROWS, 0] = cosine.reshape(N_LAT, ROWS, H)
    inverse[:, :ROWS, 1] = -sine.reshape(N_LAT, ROWS, H)
    return forward.reshape(H, 2 * N_LAT * 8), inverse.reshape(N_LAT * 8, 2 * H)


def swap_table():
    table = np.zeros((GROUP, GROUP))
    for mode in range(2):
        for c in range(BS):
            real = mode * 2 * BS + c
            table[real + BS, real] = 1
            table[real, real + BS] = -1
    return table.astype(ml_dtypes.bfloat16)


def dot(left, right):
    return lax.dot_general(left, right, (((1,), (0,)), ((), ())), preferred_element_type=F32)


def dot_nt(left, right):
    return lax.dot_general(left, right, (((1,), (1,)), ((), ())), preferred_element_type=F32)


def dot_tn(left, right):
    return lax.dot_general(left, right, (((0,), (0,)), ((), ())), preferred_element_type=F32)


def split(values):
    high = values.astype(BF16)
    return high, (values - high.astype(F32)).astype(BF16)


def dot3(kind, left, right):
    return kind(left[0], right[0]) + kind(left[1], right[0]) + kind(left[0], right[1])


def gelu_parts(values):
    cdf = 0.5 * (1.0 + lax.erf(values * 0.7071067811865476))
    return values * cdf, cdf + values * 0.3989422804014327 * jnp.exp(-0.5 * values * values)


def gelu_value(values):
    return 0.5 * values * (1.0 + lax.erf(values * 0.7071067811865476))


def norm_rows(stats):
    total = stats[0]
    for e in range(1, N_CH):
        total = total + stats[e]
    average = total[0:8] * (1.0 / C)
    squares = total[8:16] * (1.0 / C)
    return average, lax.rsqrt(squares - average * average + EPSILON)


def put_row(scratch, row, modes):
    wide = jnp.concatenate([modes[32 * k : 32 * k + 32] for k in range(PLANES)], axis=1)
    for t in range(LANES // 128):
        scratch[t, pl.ds(row, N_LAT, stride=8), :] = wide[:, 128 * t : 128 * t + 128]


def flush_rows(scratch, wire):
    for t in range(LANES // 128):
        scratch[t, pl.ds(ROWS, N_LAT, stride=8), :] = jnp.zeros((N_LAT, 128), F32)
        wire[:, 128 * t : 128 * t + 128] = scratch[t].astype(BF16)


def load_rows(wire, scratch):
    for t in range(LANES // 128):
        scratch[t] = wire[:, 128 * t : 128 * t + 128].astype(F32)


def get_row(scratch, row):
    wide = jnp.concatenate(
        [scratch[t, pl.ds(row, N_LAT, stride=8), :] for t in range(LANES // 128)], axis=1
    )
    return jnp.concatenate([wide[:, BS * k : BS * k + BS] for k in range(PLANES)], axis=0)


def to_chunk(rows, e):
    return jnp.concatenate(
        [
            jnp.concatenate(
                [values[48 * e + 8 * a : 48 * e + 8 * a + 8] for a in range(6)], axis=1
            )
            for values in rows
        ],
        axis=0,
    )


def from_chunks(chunks, row):
    return jnp.concatenate(
        [
            chunk[8 * row : 8 * row + 8, BS * a : BS * a + BS]
            for chunk in chunks
            for a in range(6)
        ],
        axis=0,
    )


def cot_kernel(cot, wire):
    rows = [cot[r].astype(F32).T for r in range(ROWS)]
    for e in range(N_CH):
        wire[e] = to_chunk(rows, e).astype(BF16)


def lon_kernel(x, stats, gain, t_high, t_low, wire, scratch):
    average, inv_std = norm_rows(stats)
    table = (t_high[...], t_low[...])
    for r in range(ROWS):
        normed = (x[r].astype(F32) - average[r : r + 1]) * inv_std[r : r + 1]
        lifted = split(normed * gain[...])
        put_row(scratch, r, dot3(dot_nt, table, lifted))
    flush_rows(scratch, wire)


def lat_forward(wire, lf_high, lf_low, swap):
    values = wire[...]
    swapped = dot(values, swap[...]).astype(BF16)
    both = jnp.concatenate([values, swapped], axis=0)
    return dot(lf_high[...], both) + dot(lf_low[...], both)


def lat_inverse(modes, li_high, li_low):
    both = split(jnp.concatenate([modes[:, :GROUP], modes[:, GROUP:]], axis=0))
    return dot3(dot, (li_high[...], li_low[...]), both)


def weight_sum(blocks):
    def block(part, other):
        pieces = [
            blocks[m + BS * part : m + BS * part + BS, m + BS * other : m + BS * other + BS]
            for m in (0, 2 * BS)
        ]
        return pieces[0] + pieces[1]

    return jnp.concatenate(
        [block(0, 0) + block(1, 1), block(1, 0) - block(0, 1)], axis=0
    )


def spectral_kernel(
    wire, lf_high, lf_low, swap, m1_high, m1_low, m2_high, m2_low, doubled, li_high, li_low,
    out, spectrum, pre_modes,
):
    modes = lat_forward(wire, lf_high, lf_low, swap)
    spectrum[...] = modes
    pre = dot3(dot, split(modes), (m1_high[...], m1_low[...]))
    pre_modes[...] = pre
    act = split(gelu_value(pre))
    scale = doubled[...]
    result = dot3(dot, act, (m2_high[...], m2_low[...])) * jnp.concatenate([scale, scale], axis=1)
    out[...] = lat_inverse(result, li_high, li_low).astype(BF16)


def spectral_back_kernel(
    wire, spectrum, pre_modes, lf_high, lf_low, swap, m1_high, m1_low, m2_high, m2_low, doubled,
    li_high, li_low, gain, gain_parts, out, small, grad_outer, grad_inner, gain_sum,
):
    @pl.when(pl.program_id(0) == 0)
    def _():
        grad_outer[...] = jnp.zeros_like(grad_outer)
        grad_inner[...] = jnp.zeros_like(grad_inner)
        gain_sum[...] = jnp.zeros_like(gain_sum)

    grad = split(lat_forward(wire, lf_high, lf_low, swap) * doubled[...])
    act, slope = gelu_parts(pre_modes[...])
    grad_act = dot3(dot_nt, grad, (m2_high[:, :GROUP], m2_low[:, :GROUP]))
    grad_outer[...] += dot3(dot_tn, grad, split(act))
    grad_pre = split(grad_act * slope)
    modes = spectrum[...]
    grad_inner[...] += dot3(dot_tn, grad_pre, split(modes))
    grad_spectrum = dot3(dot_nt, grad_pre, (m1_high[...], m1_low[...]))
    gain_row = jnp.sum(grad_spectrum[:, :GROUP] * modes, axis=0, keepdims=True)
    gain_row = sum(gain_row[:, BS * k : BS * k + BS] for k in range(4))
    gain_sum[0:1, :BS] += gain_row
    out[...] = lat_inverse(grad_spectrum, li_high, li_low).astype(BF16)

    @pl.when(pl.program_id(0) == 2)
    def _():
        first = gain_sum[0:1, :BS] / gain[...] + gain_parts[0:1, :BS]
        for half, blocks, row in (
            (0, grad_inner[...], first),
            (1, grad_outer[...], gain_parts[1:2, :BS]),
        ):
            weight = weight_sum(blocks)
            for i in range(3):
                small[half, i] = jnp.concatenate(
                    [weight[48 * q + 16 * i : 48 * q + 16 * i + 16] for q in range(4)], axis=1
                )
            high = row.astype(BF16).astype(F32)
            row = jnp.concatenate([high, row - high, jnp.zeros((1, 2 * BS), F32)], axis=1)
            small[half, 3] = jnp.concatenate([row, jnp.zeros((15, 4 * BS), F32)], axis=0)


def mix_kernel(wire, tt_high, tt_low, x, stats, gain, mixed, chunks, scratch):
    average, inv_std = norm_rows(stats)
    load_rows(wire, scratch)
    rows = []
    for r in range(ROWS):
        x_float = x[r].astype(F32)
        lifted = (x_float - average[r : r + 1]) * inv_std[r : r + 1] * gain[...]
        modes = get_row(scratch, r).astype(BF16)
        filtered = dot(tt_high[...], modes) + dot(tt_low[...], modes)
        values = filtered + (lifted + x_float).T
        mixed[r] = values
        rows.append(values)
    for e in range(N_CH):
        chunks[e] = to_chunk(rows, e)


def mlp_kernel(
    core, mixed, cot, gain, own_in, other_in, own_out, other_out,
    out_chunks, grad_chunks, grad_in_own, grad_in_other, grad_out_own, grad_out_other,
    normed, inputs, cots, inv_std, sum_out, sum_grad,
):
    step = pl.program_id(0)
    turn = 4 * core[0]
    cells = 6 * 8 * ROWS
    part = 8 * ROWS

    def gain_row():
        return jnp.concatenate([gain[e ^ turn] for e in range(N_CH)], axis=1)

    @pl.when(step == 0)
    def _():
        pieces = [mixed[e ^ turn] for e in range(N_CH)]
        values = jnp.concatenate(
            [
                jnp.concatenate([piece[:, BS * a : BS * a + BS] for piece in pieces], axis=1)
                for a in range(6)
            ],
            axis=0,
        )
        average = jnp.sum(values, axis=1, keepdims=True) * (1.0 / C)
        squares = jnp.sum(values * values, axis=1, keepdims=True) * (1.0 / C)
        inv = lax.rsqrt(squares - average * average + EPSILON)
        values = (values - average) * inv
        normed[...] = values
        inv_std[...] = jnp.broadcast_to(inv, (cells, 128))
        inputs[...] = (values * gain_row()).astype(BF16)
        pieces = [cot[e ^ turn].astype(F32) for e in range(N_CH)]
        cots[...] = jnp.concatenate(
            [
                jnp.concatenate([piece[:, BS * a : BS * a + BS] for piece in pieces], axis=1)
                for a in range(6)
            ],
            axis=0,
        ).astype(BF16)
        sum_out[...] = jnp.zeros_like(sum_out)
        sum_grad[...] = jnp.zeros_like(sum_grad)

    first, second = inputs[:, :384], inputs[:, 384:]
    cot_first, cot_second = cots[:, :384], cots[:, 384:]
    in_own, out_own = own_in[0], own_out[0]
    in_other, out_other = other_in[0], other_out[0]
    pre_act = dot(first, in_own) + dot(second, in_other)
    hidden, slope = gelu_parts(pre_act)
    hidden = hidden.astype(BF16)
    grad_hidden = dot_nt(cot_first, out_own) + dot_nt(cot_second, out_other)
    grad_pre = (grad_hidden * slope).astype(BF16)
    sum_out[:, :384] += dot(hidden, out_own)
    sum_out[:, 384:] += dot(hidden, out_other)
    sum_grad[:, :384] += dot_nt(grad_pre, in_own)
    sum_grad[:, 384:] += dot_nt(grad_pre, in_other)
    grad_in_own[0] = dot_tn(first, grad_pre)
    grad_in_other[0] = dot_tn(second, grad_pre).astype(BF16)
    grad_out_own[0] = dot_tn(hidden, cot_first)
    grad_out_other[0] = dot_tn(hidden, cot_second).astype(BF16)

    @pl.when(step == N_CH - 1)
    def _():
        grad_input = sum_grad[...]
        values = normed[...]
        gain_sum = jnp.sum(grad_input * values, axis=0, keepdims=True)
        scaled = grad_input * gain_row()
        leading = jnp.sum(scaled, axis=1, keepdims=True) * (1.0 / C)
        paired = jnp.sum(scaled * values, axis=1, keepdims=True) * (1.0 / C)
        grad_mixed = cots[...].astype(F32) + inv_std[:, :1] * (scaled - leading - values * paired)
        outputs = sum_out[...]

        def chunk(array, e):
            return jnp.concatenate(
                [array[part * a : part * a + part, BS * e : BS * e + BS] for a in range(6)],
                axis=1,
            )

        for e in range(N_CH):
            out_chunks[e ^ turn] = chunk(outputs, e).astype(BF16)
            gain_piece = gain_sum[:, BS * e : BS * e + BS]
            gain_high = gain_piece.astype(BF16).astype(F32)
            extra = jnp.concatenate(
                [gain_high, gain_piece - gain_high, jnp.zeros((1, 4 * BS), F32)], axis=1
            )
            extra = jnp.concatenate([extra, jnp.zeros((7, 6 * BS), F32)], axis=0)
            grad_chunks[e ^ turn] = jnp.concatenate(
                [chunk(grad_mixed, e), extra], axis=0
            ).astype(BF16)


def lon_back_kernel(chunks, x, stats, t_high, t_low, wire, grad_mixed, gains, scratch):
    average, inv_std = norm_rows(stats)
    pieces = [chunks[e].astype(F32) for e in range(N_CH)]
    gain_first = jnp.zeros((BS, 1), F32)
    for r in range(ROWS):
        values = from_chunks(pieces, r)
        rounded = values.astype(BF16)
        put_row(scratch, r, dot(t_high[...], rounded) + dot(t_low[...], rounded))
        turned = values.T
        grad_mixed[r] = turned.astype(BF16)
        normed = (x[r].astype(F32) - average[r : r + 1]) * inv_std[r : r + 1]
        gain_first = gain_first + jnp.sum(turned * normed, axis=1, keepdims=True)
    flush_rows(scratch, wire)
    gain_second = jnp.zeros((1, BS), F32)
    for piece in pieces:
        row = piece[8 * ROWS : 8 * ROWS + 1]
        gain_second = gain_second + row[:, :BS] + row[:, BS : 2 * BS]
    turned_first = jnp.broadcast_to(gain_first, (BS, 128)).T[0:1, :]
    gains[0:1, :BS] = turned_first
    gains[1:2, :BS] = gain_second


def unmix_kernel(wire, tt_high, tt_low, grad_mixed, x, stats, gain, scaled, sums, scratch):
    average, inv_std = norm_rows(stats)
    load_rows(wire, scratch)
    for r in range(ROWS):
        modes = get_row(scratch, r).astype(BF16)
        back = dot(tt_high[...], modes) + dot(tt_low[...], modes)
        values = (back.T + grad_mixed[r].astype(F32)) * gain[...]
        normed = (x[r].astype(F32) - average[r : r + 1]) * inv_std[r : r + 1]
        scaled[r] = values
        sums[r : r + 1] = jnp.sum(values, axis=0, keepdims=True)
        sums[8 + r : 9 + r] = jnp.sum(values * normed, axis=0, keepdims=True)
    sums[7:8] = jnp.zeros((1, W), F32)
    sums[15:16] = jnp.zeros((1, W), F32)


def final_kernel(scaled, grad_mixed, x, stats, *rest):
    average, inv_std = norm_rows(stats)
    out = rest[-1]
    total = rest[0][...]
    for part in rest[1:-1]:
        total = total + part[...]
    total = total * (1.0 / C)
    for r in range(ROWS):
        inv = inv_std[r : r + 1]
        normed = (x[r].astype(F32) - average[r : r + 1]) * inv
        change = scaled[r] - total[r : r + 1] - normed * total[8 + r : 9 + r]
        out[r] = (grad_mixed[r].astype(F32) + inv * change).astype(BF16)


def collect_kernel(small, in_0, in_2, in_4, in_6, out_0, out_1, out):
    total = in_0[...] + in_2[...].astype(F32) + in_4[...].astype(F32) + in_6[...].astype(F32)
    out[:8, :48] = total.reshape(8, 48, 384).astype(BF16)
    total = out_0[...] + out_1[...].astype(F32)
    out[8:, :48] = total.reshape(8, 48, 384).astype(BF16)
    rows = [small[i] for i in range(4)]
    for n in range(16):
        out[n, 48:] = jnp.concatenate(
            [row[n : n + 1] for row in rows] + [jnp.zeros((4, 384), F32)], axis=0
        ).astype(BF16)


def spread_kernel(parts, out):
    total = parts[0].astype(F32)
    for n in range(1, 16):
        total = total + parts[n].astype(F32)
    total = total.astype(BF16)
    for n in range(16):
        out[n] = total


def finish_kernel(place, mine, theirs, grad_in, grad_out, grad_weights, grad_gains):
    first = place[0] == 0

    def ordered(take):
        one, two = take(mine), take(theirs)
        return jnp.where(first, one, two), jnp.where(first, two, one)

    def large(array):
        return array[:, :48].astype(F32).reshape(768, 384)

    low, high = ordered(large)
    grad_in[:384] = low[:384]
    grad_in[384:] = high[:384]
    grad_out[:, :384] = low[384:]
    grad_out[:, 384:] = high[384:]

    def small(array):
        return array[:, 48:].astype(F32).reshape(128, 384)

    for half, values in enumerate(ordered(small)):
        planes = [
            jnp.concatenate([values[8 * n + i : 8 * n + i + 1] for n in range(16)], axis=0)
            for i in range(3)
        ]
        grad_weights[half] = jnp.concatenate(
            [plane[:, BS * q : BS * q + BS] for q in range(4) for plane in planes], axis=0
        )
        grad_gains[half : half + 1] = values[3:4, :BS] + values[3:4, BS : 2 * BS]


def output_kernel(chunks, mixed, out):
    pieces = [chunks[e].astype(F32) for e in range(N_CH)]
    for r in range(ROWS):
        out[r] = (from_chunks(pieces, r) + mixed[r]).T.astype(BF16)


def cost(micros):
    return pl.CostEstimate(
        flops=int(micros * 1.0e9), bytes_accessed=int(micros * 2.0e6), transcendentals=0
    )


def call(kernel, out_shape, *args, scratch=(), micros=3, place=None):
    specs = [pl.BlockSpec(memory_space=pltpu.VMEM)] * len(args)
    if place is not None:
        args = (place,) + args
        specs = [pl.BlockSpec(memory_space=pltpu.SMEM)] + specs
    return pl.pallas_call(
        kernel,
        out_shape=out_shape,
        in_specs=specs,
        scratch_shapes=scratch,
        compiler_params=pltpu.CompilerParams(vmem_limit_bytes=VMEM_BYTES),
        cost_estimate=cost(micros),
    )(*args)


def shaped(*shape, dtype=F32):
    return jax.ShapeDtypeStruct(shape, dtype)


def whole(shape):
    return pl.BlockSpec(shape, lambda g: (0,) * len(shape))


def lane_block(rows):
    return pl.BlockSpec((rows, GROUP), lambda g: (0, g))


def block_matrix(weight, swap_columns, swap_rows):
    real, imag = weight[0, 0].T, weight[1, 0].T
    base = [[real, imag], [-imag, real]]
    if swap_columns:
        base = [[imag, -real], [real, imag]]
    if swap_rows:
        base = [[-imag, real], [-real, -imag]]
    one = jnp.concatenate([jnp.concatenate(line, axis=1) for line in base], axis=0)
    zero = jnp.zeros_like(one)
    return jnp.concatenate(
        [jnp.concatenate([one, zero], axis=1), jnp.concatenate([zero, one], axis=1)], axis=0
    )


def to_all(values, axis, count, **kwargs):
    spread = jnp.broadcast_to(values[None], (count,) + values.shape)
    return lax.all_to_all(spread, axis, 0, 0, tiled=True, **kwargs)


def near(values, k):
    return lax.ppermute(values, "ch", [(i, i ^ k) for i in range(N_CH)])


def body(fields, gain_first, w_inner, w_outer, gain_second, fc_in, fc_out, cotangent):
    lat = lax.axis_index("lat")
    core = lat % 2
    core_place = core[None].astype(jnp.int32)
    siblings = [(i, i ^ 1) for i in range(N_LAT)]
    cores = [list(range(0, N_LAT, 2)), list(range(1, N_LAT, 2))]
    t_high, t_low = (jnp.asarray(t) for t in halves(lon_table()))
    tt_high, tt_low = (jnp.asarray(t) for t in halves(lon_table().T))
    forward, inverse = lat_tables()
    lf_high, lf_low = (jnp.asarray(t) for t in halves(forward))
    li_high, li_low = (jnp.asarray(t) for t in halves(inverse))
    swap = jnp.asarray(swap_table())

    x = fields.transpose(1, 0, 2)
    cot = cotangent.transpose(1, 0, 2)
    gain_column = gain_first[:, None]

    with jax.named_scope("weights"):
        half_in = lax.dynamic_slice_in_dim(fc_in, core * 384, 384, 0)
        half_out = lax.dynamic_slice_in_dim(fc_out, core * 384, 384, 1)
        pair = jnp.stack([half_in, near(half_in, 1)])
        own_in = [pair] + [near(pair, k) for k in (2, 4, 6)]
        quad = jnp.stack([half_out] + [near(half_out, k) for k in (2, 4, 6)])
        own_out = [quad, near(quad, 1)]

    with jax.named_scope("stats"):
        x_float = x.astype(F32)
        zero = jnp.zeros((1, W), F32)
        payload = jnp.concatenate(
            [
                jnp.sum(x_float, 1),
                zero,
                jnp.sum(x_float * x_float, 1),
                zero,
                jnp.pad(gain_second, (0, W - BS))[None],
                jnp.zeros((7, W), F32),
            ],
            axis=0,
        )
        gathered = to_all(payload, "ch", N_CH)
        stats = gathered[:, :16]
        gains = gathered[:, 16:17, :BS]

    scratch = pltpu.VMEM((LANES // 128, 8 * N_LAT, 128), F32)
    wire_shape = shaped(8 * N_LAT, LANES, dtype=BF16)
    with jax.named_scope("lon"):
        wire = call(
            lon_kernel, wire_shape, x, stats, gain_column, t_high, t_low, scratch=[scratch]
        )
        wire = lax.all_to_all(wire, "lat", 0, 0, tiled=True)

    with jax.named_scope("cot"):
        cot_chunks = call(cot_kernel, shaped(N_CH, 8 * ROWS, 6 * BS, dtype=BF16), cot)
        *weights, cot_chunks, wire = lax.optimization_barrier(
            (*own_in, *own_out, cot_chunks, wire)
        )
        cot_chunks = lax.all_to_all(cot_chunks, "ch", 0, 0, tiled=True)
        own_in = jnp.concatenate(weights[:4], axis=0)
        own_out = jnp.concatenate(weights[4:], axis=0)
        other_in = lax.ppermute(own_in, "lat", siblings)
        other_out = lax.ppermute(own_out, "lat", siblings)

    with jax.named_scope("matrices"):
        m1 = split(
            jnp.concatenate(
                [block_matrix(w_inner, False, False), block_matrix(w_inner, False, True)], axis=0
            )
        )
        m2 = split(
            jnp.concatenate(
                [block_matrix(w_outer, False, False), block_matrix(w_outer, True, False)], axis=1
            )
        )
        lane = jnp.arange(LANES, dtype=jnp.int32)[None]
        doubled = jnp.where((lat == 0) & (lane < 2 * BS), 1.0, 2.0).astype(F32)

    table_specs = [whole((H, 512)), whole((H, 512)), whole((GROUP, GROUP))]
    inverse_specs = [lane_block(1), whole((256, 448)), whole((256, 448))]
    params = pltpu.CompilerParams(vmem_limit_bytes=VMEM_BYTES)
    with jax.named_scope("spectral"):
        wire, spectrum, pre_modes = pl.pallas_call(
            spectral_kernel,
            grid=(3,),
            in_specs=[lane_block(256)]
            + table_specs
            + [whole((GROUP, GROUP))] * 2
            + [whole((GROUP, 2 * GROUP))] * 2
            + inverse_specs,
            out_specs=[lane_block(256), lane_block(H), lane_block(H)],
            out_shape=[wire_shape, shaped(H, LANES), shaped(H, LANES)],
            compiler_params=params,
            cost_estimate=cost(11),
        )(
            wire, lf_high, lf_low, swap, m1[0][:GROUP], m1[1][:GROUP], m2[0], m2[1], doubled,
            li_high, li_low,
        )
        wire, cot_chunks = lax.optimization_barrier((wire, cot_chunks))
        wire = lax.all_to_all(wire, "lat", 0, 0, tiled=True)
        wire, other_in, other_out = lax.optimization_barrier((wire, other_in, other_out))

    with jax.named_scope("mix"):
        mixed, chunks = call(
            mix_kernel,
            [shaped(ROWS, W, BS), shaped(N_CH, 8 * ROWS, 6 * BS)],
            wire, tt_high, tt_low, x, stats, gain_column,
            scratch=[scratch],
        )
        chunks = lax.all_to_all(chunks, "ch", 0, 0, tiled=True)

    cells = 48 * ROWS
    direct = pl.BlockSpec((1, 384, 384), lambda e, place: (e, 0, 0))
    halved = pl.BlockSpec((1, 384, 384), lambda e, place: (e % 2 * 4 + e // 2, 0, 0))

    def all_of(shape):
        return pl.BlockSpec(shape, lambda e, place: (0,) * len(shape))

    with jax.named_scope("mlp"):
        out_chunks, grad_chunks, in_own, in_other, out_own, out_other = pl.pallas_call(
            mlp_kernel,
            grid_spec=pltpu.PrefetchScalarGridSpec(
                num_scalar_prefetch=1,
                grid=(N_CH,),
                in_specs=[
                    all_of((N_CH, 8 * ROWS, 6 * BS)),
                    all_of((N_CH, 8 * ROWS, 6 * BS)),
                    all_of((N_CH, 1, BS)),
                    direct,
                    direct,
                    halved,
                    halved,
                ],
                out_specs=[
                    all_of((N_CH, 8 * ROWS, 6 * BS)),
                    all_of((N_CH, 8 * ROWS + 8, 6 * BS)),
                    halved,
                    halved,
                    direct,
                    direct,
                ],
                scratch_shapes=[
                    pltpu.VMEM((cells, C), F32),
                    pltpu.VMEM((cells, C), BF16),
                    pltpu.VMEM((cells, C), BF16),
                    pltpu.VMEM((cells, 128), F32),
                    pltpu.VMEM((cells, C), F32),
                    pltpu.VMEM((cells, C), F32),
                ],
            ),
            out_shape=[
                shaped(N_CH, 8 * ROWS, 6 * BS, dtype=BF16),
                shaped(N_CH, 8 * ROWS + 8, 6 * BS, dtype=BF16),
                shaped(N_CH, 384, 384),
                shaped(N_CH, 384, 384, dtype=BF16),
                shaped(N_CH, 384, 384),
                shaped(N_CH, 384, 384, dtype=BF16),
            ],
            compiler_params=params,
            cost_estimate=cost(24),
        )(core_place, chunks, cot_chunks, gains,
          own_in, other_in, own_out, other_out)
        grad_chunks = lax.all_to_all(grad_chunks, "ch", 0, 0, tiled=True)

    with jax.named_scope("lon_back"):
        wire, grad_mixed, gain_parts = call(
            lon_back_kernel,
            [wire_shape, shaped(ROWS, BS, W, dtype=BF16), shaped(8, 128)],
            grad_chunks, x, stats, t_high, t_low,
            scratch=[scratch],
        )
        wire = lax.all_to_all(wire, "lat", 0, 0, tiled=True)

    with jax.named_scope("output"):
        out_chunks, wire = lax.optimization_barrier((out_chunks, wire))
        out_chunks = lax.all_to_all(out_chunks, "ch", 0, 0, tiled=True)

    with jax.named_scope("grads_ch"):
        theirs = lax.ppermute(in_other, "lat", siblings)
        odd = near((in_own[4:] + theirs[4:].astype(F32)).astype(BF16), 1)
        even = in_own[:4] + theirs[:4].astype(F32) + odd.astype(F32)
        in_parts = [even[0]] + [near(even[k // 2].astype(BF16), k) for k in (2, 4, 6)]
        theirs = lax.ppermute(out_other, "lat", siblings)
        pair = out_own[:2] + theirs[:2].astype(F32)
        for k in (2, 4, 6):
            part = (out_own[k : k + 2] + theirs[k : k + 2].astype(F32)).astype(BF16)
            pair = pair + near(part, k).astype(F32)
        out_parts = [pair[0], near(pair[1].astype(BF16), 1)]

    with jax.named_scope("spectral_back"):
        wire, small = pl.pallas_call(
            spectral_back_kernel,
            grid=(3,),
            in_specs=[lane_block(256), lane_block(H), lane_block(H)]
            + table_specs
            + [whole((2 * GROUP, GROUP))] * 2
            + [whole((GROUP, 2 * GROUP))] * 2
            + inverse_specs
            + [whole((1, BS)), whole((8, 128))],
            out_specs=[lane_block(256), whole((2, 4, 16, 384))],
            out_shape=[wire_shape, shaped(2, 4, 16, 384)],
            scratch_shapes=[
                pltpu.VMEM((GROUP, GROUP), F32),
                pltpu.VMEM((GROUP, GROUP), F32),
                pltpu.VMEM((8, 128), F32),
            ],
            compiler_params=params,
            cost_estimate=cost(14),
        )(
            wire, spectrum, pre_modes, lf_high, lf_low, swap, m1[0], m1[1], m2[0], m2[1], doubled,
            li_high, li_low, gain_first[None], gain_parts,
        )
        small_send = lax.dynamic_index_in_dim(small, 1 - core, 0, keepdims=False)
        small_own = lax.dynamic_index_in_dim(small, core, 0, keepdims=False)
        small_sum = small_own + lax.ppermute(small_send, "lat", siblings)
        *grad_parts, out_chunks, wire = lax.optimization_barrier(
            (*in_parts, *out_parts, out_chunks, wire)
        )
        wire = lax.all_to_all(wire, "lat", 0, 0, tiled=True)

    with jax.named_scope("output_mix"):
        output = call(output_kernel, shaped(ROWS, BS, W, dtype=BF16), out_chunks, mixed)

    with jax.named_scope("grads_collect"):
        payload = call(
            collect_kernel, shaped(16, 56, 384, dtype=BF16), small_sum, *grad_parts
        )
        payload, wire = lax.optimization_barrier((payload, wire))

    with jax.named_scope("unmix"):
        scaled, sums = call(
            unmix_kernel,
            [shaped(ROWS, BS, W), shaped(16, W)],
            wire, tt_high, tt_low, grad_mixed, x, stats, gain_column,
            scratch=[scratch],
        )
    with jax.named_scope("grads_lat"):
        payload = lax.all_to_all(payload, "lat", 0, 0, tiled=True, axis_index_groups=cores)
        payload, _ = lax.optimization_barrier((payload, sums))
        sums = [sums] + [
            lax.ppermute(sums, "ch", [(i, i ^ k) for i in range(N_CH)]) for k in range(1, N_CH)
        ]
        grad_fields = call(
            final_kernel, shaped(ROWS, BS, W, dtype=BF16), scaled, grad_mixed, x, stats, *sums
        )
        payload = call(spread_kernel, shaped(16, 56, 384, dtype=BF16), payload)
        mine = lax.all_to_all(payload, "lat", 0, 0, tiled=True, axis_index_groups=cores)
        theirs = lax.ppermute(mine, "lat", siblings)
        grad_fc_in, grad_fc_out, grad_weights, grad_gains = call(
            finish_kernel,
            [shaped(C, FF_DEV), shaped(FF_DEV, C), shaped(2, 2 * BS, BS), shaped(2, BS)],
            mine, theirs, place=core_place,
        )

    return (
        output.transpose(1, 0, 2),
        grad_fields.transpose(1, 0, 2),
        grad_gains[0],
        grad_weights[0].reshape(2, 1, BS, BS),
        grad_weights[1].reshape(2, 1, BS, BS),
        grad_gains[1],
        grad_fc_in,
        grad_fc_out,
    )


def solution(mesh):
    placed = (
        P("ch", "lat", None),
        P("ch"),
        P(None, "ch", None, None),
        P(None, "ch", None, None),
        P("ch"),
        P(None, "ch"),
        P("ch", None),
        P("ch", "lat", None),
    )
    return jax.shard_map(
        body,
        mesh=mesh,
        in_specs=placed,
        out_specs=(
            P("ch", "lat", None),
            P("ch", "lat", None),
            P("ch"),
            P(None, "ch", None, None),
            P(None, "ch", None, None),
            P("ch"),
            P(None, "ch"),
            P("ch", None),
        ),
        check_vma=False,
    )
```

```python
import math

import jax
import jax.numpy as jnp
import ml_dtypes
import numpy as np
from jax import lax
from jax.experimental import pallas as pl
from jax.experimental.pallas import tpu as pltpu
from jax.sharding import PartitionSpec as P

C = 768
BS = 96
H = 224
W = 384
KW = 192
N_LAT = 32
N_CH = 8
ROWS = 7
FF_DEV = 384
MODES = KW // N_LAT
PLANES = 2 * MODES
LANES = PLANES * BS
GROUP = 384
EPSILON = 1e-05
BF16 = jnp.bfloat16
F32 = jnp.float32
VMEM_BYTES = 56 * 1024 * 1024


def halves(table):
    high = table.astype(ml_dtypes.bfloat16)
    low = (table - high.astype(np.float64)).astype(ml_dtypes.bfloat16)
    return high, low


def lon_table():
    mode = np.arange(MODES)[:, None] + MODES * np.arange(N_LAT)[None, :]
    angles = 2 * np.pi * ((mode[:, :, None] * np.arange(W)) % W) / W
    table = np.stack([np.cos(angles), -np.sin(angles)], 1) / math.sqrt(W)
    return table.reshape(PLANES * N_LAT, W)


def lat_tables():
    index = np.arange(H)
    angles = 2 * np.pi * ((index[:, None] * index[None, :]) % H) / H
    cosine = np.cos(angles) / math.sqrt(H)
    sine = np.sin(angles) / math.sqrt(H)
    forward = np.zeros((H, 2, N_LAT, 8))
    forward[:, 0, :, :ROWS] = cosine.reshape(H, N_LAT, ROWS)
    forward[:, 1, :, :ROWS] = sine.reshape(H, N_LAT, ROWS)
    inverse = np.zeros((N_LAT, 8, 2, H))
    inverse[:, :ROWS, 0] = cosine.reshape(N_LAT, ROWS, H)
    inverse[:, :ROWS, 1] = -sine.reshape(N_LAT, ROWS, H)
    return forward.reshape(H, 2 * N_LAT * 8), inverse.reshape(N_LAT * 8, 2 * H)


def swap_table():
    table = np.zeros((GROUP, GROUP))
    for mode in range(2):
        for c in range(BS):
            real = mode * 2 * BS + c
            table[real + BS, real] = 1
            table[real, real + BS] = -1
    return table.astype(ml_dtypes.bfloat16)


def dot(left, right):
    return lax.dot_general(left, right, (((1,), (0,)), ((), ())), preferred_element_type=F32)


def dot_nt(left, right):
    return lax.dot_general(left, right, (((1,), (1,)), ((), ())), preferred_element_type=F32)


def dot_tn(left, right):
    return lax.dot_general(left, right, (((0,), (0,)), ((), ())), preferred_element_type=F32)


def split(values):
    high = values.astype(BF16)
    return high, (values - high.astype(F32)).astype(BF16)


def dot3(kind, left, right):
    return kind(left[0], right[0]) + kind(left[1], right[0]) + kind(left[0], right[1])


def gelu_parts(values):
    cdf = 0.5 * (1.0 + lax.erf(values * 0.7071067811865476))
    return values * cdf, cdf + values * 0.3989422804014327 * jnp.exp(-0.5 * values * values)


def gelu_value(values):
    return 0.5 * values * (1.0 + lax.erf(values * 0.7071067811865476))


def norm_rows(stats):
    total = stats[0]
    for e in range(1, N_CH):
        total = total + stats[e]
    average = total[0:8] * (1.0 / C)
    squares = total[8:16] * (1.0 / C)
    return average, lax.rsqrt(squares - average * average + EPSILON)


def put_row(scratch, row, modes):
    wide = jnp.concatenate([modes[32 * k : 32 * k + 32] for k in range(PLANES)], axis=1)
    for t in range(LANES // 128):
        scratch[t, pl.ds(row, N_LAT, stride=8), :] = wide[:, 128 * t : 128 * t + 128]


def flush_rows(scratch, wire):
    for t in range(LANES // 128):
        scratch[t, pl.ds(ROWS, N_LAT, stride=8), :] = jnp.zeros((N_LAT, 128), F32)
        wire[:, 128 * t : 128 * t + 128] = scratch[t].astype(BF16)


def load_rows(wire, scratch):
    for t in range(LANES // 128):
        scratch[t] = wire[:, 128 * t : 128 * t + 128].astype(F32)


def load_packed(wire, scratch):
    for t in range(LANES // 128):
        block = wire[:, :, 128 * t : 128 * t + 128].astype(F32)
        scratch[t] = block[:, :8].reshape(8 * N_LAT, 128)


def get_row(scratch, row):
    wide = jnp.concatenate(
        [scratch[t, pl.ds(row, N_LAT, stride=8), :] for t in range(LANES // 128)], axis=1
    )
    return jnp.concatenate([wide[:, BS * k : BS * k + BS] for k in range(PLANES)], axis=0)


def to_chunk(rows, e):
    return jnp.concatenate(
        [
            jnp.concatenate(
                [values[48 * e + 8 * a : 48 * e + 8 * a + 8] for a in range(6)], axis=1
            )
            for values in rows
        ],
        axis=0,
    )


def from_chunks(chunks, row):
    return jnp.concatenate(
        [
            chunk[8 * row : 8 * row + 8, BS * a : BS * a + BS]
            for chunk in chunks
            for a in range(6)
        ],
        axis=0,
    )


def cot_kernel(cot, wire):
    rows = [cot[r].astype(F32).T for r in range(ROWS)]
    for e in range(N_CH):
        wire[e] = to_chunk(rows, e).astype(BF16)


def lon_kernel(x, stats, gain, t_high, t_low, wire, scratch):
    average, inv_std = norm_rows(stats)
    table = (t_high[...], t_low[...])
    for r in range(ROWS):
        normed = (x[r].astype(F32) - average[r : r + 1]) * inv_std[r : r + 1]
        lifted = split(normed * gain[...])
        put_row(scratch, r, dot3(dot_nt, table, lifted))
    flush_rows(scratch, wire)


def lat_forward(wire, lf_high, lf_low, swap):
    values = wire[...]
    swapped = dot(values, swap[...]).astype(BF16)
    both = jnp.concatenate([values, swapped], axis=0)
    return dot(lf_high[...], both) + dot(lf_low[...], both)


def lat_inverse(modes, li_high, li_low):
    both = split(jnp.concatenate([modes[:, :GROUP], modes[:, GROUP:]], axis=0))
    return dot3(dot, (li_high[...], li_low[...]), both)


def weight_sum(blocks):
    def block(part, other):
        pieces = [
            blocks[m + BS * part : m + BS * part + BS, m + BS * other : m + BS * other + BS]
            for m in (0, 2 * BS)
        ]
        return pieces[0] + pieces[1]

    return jnp.concatenate(
        [block(0, 0) + block(1, 1), block(1, 0) - block(0, 1)], axis=0
    )


def spectral_kernel(
    wire, lf_high, lf_low, swap, m1_high, m1_low, m2_high, m2_low, doubled, li_high, li_low,
    out, spectrum, pre_modes,
):
    modes = lat_forward(wire, lf_high, lf_low, swap)
    spectrum[...] = modes
    pre = dot3(dot, split(modes), (m1_high[...], m1_low[...]))
    pre_modes[...] = pre
    act = split(gelu_value(pre))
    scale = doubled[...]
    result = dot3(dot, act, (m2_high[...], m2_low[...])) * jnp.concatenate([scale, scale], axis=1)
    out[...] = lat_inverse(result, li_high, li_low).astype(BF16)


def spectral_back_kernel(
    wire, spectrum, pre_modes, lf_high, lf_low, swap, m1_high, m1_low, m2_high, m2_low, doubled,
    li_high, li_low, gain, gain_parts, out, small, grad_outer, grad_inner, gain_sum,
):
    @pl.when(pl.program_id(0) == 0)
    def _():
        grad_outer[...] = jnp.zeros_like(grad_outer)
        grad_inner[...] = jnp.zeros_like(grad_inner)
        gain_sum[...] = jnp.zeros_like(gain_sum)

    grad = split(lat_forward(wire, lf_high, lf_low, swap) * doubled[...])
    act, slope = gelu_parts(pre_modes[...])
    grad_act = dot3(dot_nt, grad, (m2_high[:, :GROUP], m2_low[:, :GROUP]))
    grad_outer[...] += dot3(dot_tn, grad, split(act))
    grad_pre = split(grad_act * slope)
    modes = spectrum[...]
    grad_inner[...] += dot3(dot_tn, grad_pre, split(modes))
    grad_spectrum = dot3(dot_nt, grad_pre, (m1_high[...], m1_low[...]))
    gain_row = jnp.sum(grad_spectrum[:, :GROUP] * modes, axis=0, keepdims=True)
    gain_row = sum(gain_row[:, BS * k : BS * k + BS] for k in range(4))
    gain_sum[0:1, :BS] += gain_row
    out[...] = lat_inverse(grad_spectrum, li_high, li_low).astype(BF16)

    @pl.when(pl.program_id(0) == 2)
    def _():
        first = gain_sum[0:1, :BS] / gain[...] + gain_parts[0:1, :BS]
        weights = [weight_sum(grad_inner[...]), weight_sum(grad_outer[...])]
        small[:N_LAT] = jnp.concatenate(
            [weight[32 * q : 32 * q + 32] for weight in weights for q in range(6)], axis=1
        )
        row = []
        for values in (first, gain_parts[1:2, :BS]):
            high = values.astype(BF16).astype(F32)
            row += [high, values - high]
        row = jnp.concatenate(row + [jnp.zeros((1, 8 * BS), F32)], axis=1)
        small[N_LAT:] = jnp.concatenate([row, jnp.zeros((7, LANES), F32)], axis=0)


def mix_kernel(wire, tt_high, tt_low, x, stats, gain, mixed, chunks, scratch):
    average, inv_std = norm_rows(stats)
    load_rows(wire, scratch)
    rows = []
    for r in range(ROWS):
        x_float = x[r].astype(F32)
        lifted = (x_float - average[r : r + 1]) * inv_std[r : r + 1] * gain[...]
        modes = get_row(scratch, r).astype(BF16)
        filtered = dot(tt_high[...], modes) + dot(tt_low[...], modes)
        values = filtered + (lifted + x_float).T
        mixed[r] = values
        rows.append(values)
    for e in range(N_CH):
        chunks[e] = to_chunk(rows, e)


def mlp_kernel(
    core, mixed, cot, gain, own_in, other_in, own_out, other_out,
    out_chunks, grad_chunks, grad_in_own, grad_in_other, grad_out_own, grad_out_other,
    normed, inputs, cots, inv_std, sum_out, sum_grad,
):
    step = pl.program_id(0)
    turn = 4 * core[0]
    cells = 6 * 8 * ROWS
    part = 8 * ROWS

    def gain_row():
        return jnp.concatenate([gain[e ^ turn] for e in range(N_CH)], axis=1)

    @pl.when(step == 0)
    def _():
        pieces = [mixed[e ^ turn] for e in range(N_CH)]
        values = jnp.concatenate(
            [
                jnp.concatenate([piece[:, BS * a : BS * a + BS] for piece in pieces], axis=1)
                for a in range(6)
            ],
            axis=0,
        )
        average = jnp.sum(values, axis=1, keepdims=True) * (1.0 / C)
        squares = jnp.sum(values * values, axis=1, keepdims=True) * (1.0 / C)
        inv = lax.rsqrt(squares - average * average + EPSILON)
        values = (values - average) * inv
        normed[...] = values
        inv_std[...] = jnp.broadcast_to(inv, (cells, 128))
        inputs[...] = (values * gain_row()).astype(BF16)
        pieces = [cot[e ^ turn].astype(F32) for e in range(N_CH)]
        cots[...] = jnp.concatenate(
            [
                jnp.concatenate([piece[:, BS * a : BS * a + BS] for piece in pieces], axis=1)
                for a in range(6)
            ],
            axis=0,
        ).astype(BF16)
        sum_out[...] = jnp.zeros_like(sum_out)
        sum_grad[...] = jnp.zeros_like(sum_grad)

    first, second = inputs[:, :384], inputs[:, 384:]
    cot_first, cot_second = cots[:, :384], cots[:, 384:]
    in_own, out_own = own_in[0], own_out[0]
    in_other, out_other = other_in[0], other_out[0]
    pre_act = dot(first, in_own) + dot(second, in_other)
    hidden, slope = gelu_parts(pre_act)
    hidden = hidden.astype(BF16)
    grad_hidden = dot_nt(cot_first, out_own) + dot_nt(cot_second, out_other)
    grad_pre = (grad_hidden * slope).astype(BF16)
    sum_out[:, :384] += dot(hidden, out_own)
    sum_out[:, 384:] += dot(hidden, out_other)
    sum_grad[:, :384] += dot_nt(grad_pre, in_own)
    sum_grad[:, 384:] += dot_nt(grad_pre, in_other)
    grad_in_own[0] = dot_tn(first, grad_pre)
    grad_in_other[0] = dot_tn(second, grad_pre).astype(BF16)
    grad_out_own[0] = dot_tn(hidden, cot_first)
    grad_out_other[0] = dot_tn(hidden, cot_second).astype(BF16)

    @pl.when(step == N_CH - 1)
    def _():
        grad_input = sum_grad[...]
        values = normed[...]
        gain_sum = jnp.sum(grad_input * values, axis=0, keepdims=True)
        scaled = grad_input * gain_row()
        leading = jnp.sum(scaled, axis=1, keepdims=True) * (1.0 / C)
        paired = jnp.sum(scaled * values, axis=1, keepdims=True) * (1.0 / C)
        grad_mixed = cots[...].astype(F32) + inv_std[:, :1] * (scaled - leading - values * paired)
        outputs = sum_out[...]

        def chunk(array, e):
            return jnp.concatenate(
                [array[part * a : part * a + part, BS * e : BS * e + BS] for a in range(6)],
                axis=1,
            )

        for e in range(N_CH):
            out_chunks[e ^ turn] = chunk(outputs, e).astype(BF16)
            gain_piece = gain_sum[:, BS * e : BS * e + BS]
            gain_high = gain_piece.astype(BF16).astype(F32)
            extra = jnp.concatenate(
                [gain_high, gain_piece - gain_high, jnp.zeros((1, 4 * BS), F32)], axis=1
            )
            extra = jnp.concatenate([extra, jnp.zeros((7, 6 * BS), F32)], axis=0)
            grad_chunks[e ^ turn] = jnp.concatenate(
                [chunk(grad_mixed, e), extra], axis=0
            ).astype(BF16)


def lon_back_kernel(chunks, x, stats, t_high, t_low, wire, grad_mixed, gains, scratch):
    average, inv_std = norm_rows(stats)
    pieces = [chunks[e].astype(F32) for e in range(N_CH)]
    gain_first = jnp.zeros((BS, 1), F32)
    for r in range(ROWS):
        values = from_chunks(pieces, r)
        rounded = values.astype(BF16)
        put_row(scratch, r, dot(t_high[...], rounded) + dot(t_low[...], rounded))
        turned = values.T
        grad_mixed[r] = turned.astype(BF16)
        normed = (x[r].astype(F32) - average[r : r + 1]) * inv_std[r : r + 1]
        gain_first = gain_first + jnp.sum(turned * normed, axis=1, keepdims=True)
    flush_rows(scratch, wire)
    gain_second = jnp.zeros((1, BS), F32)
    for piece in pieces:
        row = piece[8 * ROWS : 8 * ROWS + 1]
        gain_second = gain_second + row[:, :BS] + row[:, BS : 2 * BS]
    turned_first = jnp.broadcast_to(gain_first, (BS, 128)).T[0:1, :]
    gains[0:1, :BS] = turned_first
    gains[1:2, :BS] = gain_second


def unmix_kernel(wire, tt_high, tt_low, grad_mixed, x, stats, gain, scaled, sums, scratch):
    average, inv_std = norm_rows(stats)
    load_packed(wire, scratch)
    for r in range(ROWS):
        modes = get_row(scratch, r).astype(BF16)
        back = dot(tt_high[...], modes) + dot(tt_low[...], modes)
        values = (back.T + grad_mixed[r].astype(F32)) * gain[...]
        normed = (x[r].astype(F32) - average[r : r + 1]) * inv_std[r : r + 1]
        scaled[r] = values
        sums[r : r + 1] = jnp.sum(values, axis=0, keepdims=True)
        sums[8 + r : 9 + r] = jnp.sum(values * normed, axis=0, keepdims=True)
    sums[7:8] = jnp.zeros((1, W), F32)
    sums[15:16] = jnp.zeros((1, W), F32)


def final_kernel(scaled, grad_mixed, x, stats, *rest):
    average, inv_std = norm_rows(stats)
    out = rest[-1]
    total = rest[0][...]
    for part in rest[1:-1]:
        total = total + part[...]
    total = total * (1.0 / C)
    for r in range(ROWS):
        inv = inv_std[r : r + 1]
        normed = (x[r].astype(F32) - average[r : r + 1]) * inv
        change = scaled[r] - total[r : r + 1] - normed * total[8 + r : 9 + r]
        out[r] = (grad_mixed[r].astype(F32) + inv * change).astype(BF16)


def pack_kernel(wire, small, in_0, in_2, in_4, in_6, out_0, out_1, out):
    total_in = in_0[...] + in_2[...].astype(F32) + in_4[...].astype(F32) + in_6[...].astype(F32)
    total_out = out_0[...] + out_1[...].astype(F32)
    total = jnp.concatenate([total_in, total_out], axis=0)
    modes = wire[...].astype(F32).reshape(N_LAT, 8, LANES)
    weights = small[:N_LAT]
    row = lax.broadcasted_iota(jnp.int32, (N_LAT, 8, LANES), 1)
    modes = jnp.where(row == ROWS, weights[:, None, :], modes)
    grads = jnp.concatenate(
        [total[256 * g : 256 * g + 256].reshape(N_LAT, 8, GROUP) for g in range(3)], axis=2
    )
    out[...] = jnp.concatenate([modes, grads], axis=1).astype(BF16)


def spread_kernel(parts, small, out):
    sums = [parts[n].astype(F32) for n in (0, 1)]
    for n in range(2, N_LAT):
        sums[n % 2] = sums[n % 2] + parts[n].astype(F32)
    rows = [
        half[8:16, GROUP * g : GROUP * g + GROUP] for half in sums for g in range(3)
    ]
    weights = sums[0][ROWS : ROWS + 1] + sums[1][ROWS : ROWS + 1]
    last = [weights[:, GROUP * g : GROUP * g + GROUP] for g in range(3)]
    last += [small[N_LAT : N_LAT + 1, :GROUP], jnp.zeros((4, GROUP), F32)]
    total = jnp.concatenate(rows + [jnp.concatenate(last, axis=0)], axis=0).astype(BF16)
    for n in range(N_LAT // 2):
        out[n] = total


def finish_kernel(
    place, mine, theirs, grad_in, grad_out, grad_inner, grad_outer, gain_first, gain_second
):
    first = place[0] == 0
    one, two = mine[...].astype(F32), theirs[...].astype(F32)
    even, odd = jnp.where(first, one, two), jnp.where(first, two, one)

    def rows(start):
        parts = [part[:, start : start + 8][:, None] for part in (even, odd)]
        return jnp.concatenate(parts, axis=1).reshape(256, GROUP)

    for half in range(2):
        total = jnp.concatenate([rows(24 * half + 8 * g) for g in range(3)], axis=0)
        grad_in[384 * half : 384 * half + 384] = total[:384]
        grad_out[:, 384 * half : 384 * half + 384] = total[384:]
    last = rows(48)
    planes = [
        jnp.concatenate([last[8 * n + g : 8 * n + g + 1] for n in range(N_LAT)], axis=0)
        for g in range(4)
    ]
    weights = [
        plane[:, BS * q : BS * q + BS] for plane in planes[:3] for q in range(4)
    ]
    for part in range(2):
        grad_inner[part, 0] = jnp.concatenate(weights[3 * part : 3 * part + 3], axis=0)
        grad_outer[part, 0] = jnp.concatenate(weights[6 + 3 * part : 9 + 3 * part], axis=0)
    gains = jnp.sum(planes[3], axis=0, keepdims=True)
    gain_first[...] = gains[:, :BS] + gains[:, BS : 2 * BS]
    gain_second[...] = gains[:, 2 * BS : 3 * BS] + gains[:, 3 * BS :]


def output_kernel(chunks, mixed, out):
    pieces = [chunks[e].astype(F32) for e in range(N_CH)]
    for r in range(ROWS):
        out[r] = (from_chunks(pieces, r) + mixed[r]).T.astype(BF16)


def cost(micros):
    return pl.CostEstimate(
        flops=int(micros * 1.0e9), bytes_accessed=int(micros * 2.0e6), transcendentals=0
    )


def call(kernel, out_shape, *args, scratch=(), micros=3, place=None):
    specs = [pl.BlockSpec(memory_space=pltpu.VMEM)] * len(args)
    if place is not None:
        args = (place,) + args
        specs = [pl.BlockSpec(memory_space=pltpu.SMEM)] + specs
    return pl.pallas_call(
        kernel,
        out_shape=out_shape,
        in_specs=specs,
        scratch_shapes=scratch,
        compiler_params=pltpu.CompilerParams(vmem_limit_bytes=VMEM_BYTES),
        cost_estimate=cost(micros),
    )(*args)


def shaped(*shape, dtype=F32):
    return jax.ShapeDtypeStruct(shape, dtype)


def whole(shape):
    return pl.BlockSpec(shape, lambda g: (0,) * len(shape))


def lane_block(rows):
    return pl.BlockSpec((rows, GROUP), lambda g: (0, g))


def block_matrix(weight, swap_columns, swap_rows):
    real, imag = weight[0, 0].T, weight[1, 0].T
    base = [[real, imag], [-imag, real]]
    if swap_columns:
        base = [[imag, -real], [real, imag]]
    if swap_rows:
        base = [[-imag, real], [-real, -imag]]
    one = jnp.concatenate([jnp.concatenate(line, axis=1) for line in base], axis=0)
    zero = jnp.zeros_like(one)
    return jnp.concatenate(
        [jnp.concatenate([one, zero], axis=1), jnp.concatenate([zero, one], axis=1)], axis=0
    )


def to_all(values, axis, count, **kwargs):
    spread = jnp.broadcast_to(values[None], (count,) + values.shape)
    return lax.all_to_all(spread, axis, 0, 0, tiled=True, **kwargs)


def near(values, k):
    return lax.ppermute(values, "ch", [(i, i ^ k) for i in range(N_CH)])


def body(fields, gain_first, w_inner, w_outer, gain_second, fc_in, fc_out, cotangent):
    lat = lax.axis_index("lat")
    core = lat % 2
    core_place = core[None].astype(jnp.int32)
    siblings = [(i, i ^ 1) for i in range(N_LAT)]
    cores = [list(range(0, N_LAT, 2)), list(range(1, N_LAT, 2))]
    t_high, t_low = (jnp.asarray(t) for t in halves(lon_table()))
    tt_high, tt_low = (jnp.asarray(t) for t in halves(lon_table().T))
    forward, inverse = lat_tables()
    lf_high, lf_low = (jnp.asarray(t) for t in halves(forward))
    li_high, li_low = (jnp.asarray(t) for t in halves(inverse))
    swap = jnp.asarray(swap_table())

    x = fields.transpose(1, 0, 2)
    cot = cotangent.transpose(1, 0, 2)
    gain_column = gain_first[:, None]

    with jax.named_scope("weights"):
        half_in = lax.dynamic_slice_in_dim(fc_in, core * 384, 384, 0)
        half_out = lax.dynamic_slice_in_dim(fc_out, core * 384, 384, 1)
        near_in = near(half_in, 1)
        near_out = [near(half_out, k) for k in (2, 4, 6)]

    with jax.named_scope("cot"):
        cot_chunks = call(cot_kernel, shaped(N_CH, 8 * ROWS, 6 * BS, dtype=BF16), cot)

    with jax.named_scope("stats"):
        x_float = x.astype(F32)
        zero = jnp.zeros((1, W), F32)
        payload = jnp.concatenate(
            [
                jnp.sum(x_float, 1),
                zero,
                jnp.sum(x_float * x_float, 1),
                zero,
                jnp.pad(gain_second, (0, W - BS))[None],
                jnp.zeros((7, W), F32),
            ],
            axis=0,
        )
        gathered = to_all(payload, "ch", N_CH)
        near_in, *near_out, cot_chunks, gathered = lax.optimization_barrier(
            (near_in, *near_out, cot_chunks, gathered)
        )
        stats = gathered[:, :16]
        gains = gathered[:, 16:17, :BS]

    with jax.named_scope("weights"):
        pair = jnp.stack([half_in, near_in])
        own_in = [pair] + [near(pair, k) for k in (2, 4, 6)]
        quad = jnp.stack([half_out] + near_out)
        own_out = [quad, near(quad, 1)]

    scratch = pltpu.VMEM((LANES // 128, 8 * N_LAT, 128), F32)
    wire_shape = shaped(8 * N_LAT, LANES, dtype=BF16)
    with jax.named_scope("lon"):
        wire = call(
            lon_kernel, wire_shape, x, stats, gain_column, t_high, t_low, scratch=[scratch]
        )
        wire = lax.all_to_all(wire, "lat", 0, 0, tiled=True)

    with jax.named_scope("cot"):
        *weights, cot_chunks, wire = lax.optimization_barrier(
            (*own_in, *own_out, cot_chunks, wire)
        )
        cot_chunks = lax.all_to_all(cot_chunks, "ch", 0, 0, tiled=True)

    with jax.named_scope("matrices"):
        m1 = split(
            jnp.concatenate(
                [block_matrix(w_inner, False, False), block_matrix(w_inner, False, True)], axis=0
            )
        )
        m2 = split(
            jnp.concatenate(
                [block_matrix(w_outer, False, False), block_matrix(w_outer, True, False)], axis=1
            )
        )
        lane = jnp.arange(LANES, dtype=jnp.int32)[None]
        doubled = jnp.where((lat == 0) & (lane < 2 * BS), 1.0, 2.0).astype(F32)

    table_specs = [whole((H, 512)), whole((H, 512)), whole((GROUP, GROUP))]
    inverse_specs = [lane_block(1), whole((256, 448)), whole((256, 448))]
    params = pltpu.CompilerParams(vmem_limit_bytes=VMEM_BYTES)
    with jax.named_scope("spectral"):
        wire, spectrum, pre_modes = pl.pallas_call(
            spectral_kernel,
            grid=(3,),
            in_specs=[lane_block(256)]
            + table_specs
            + [whole((GROUP, GROUP))] * 2
            + [whole((GROUP, 2 * GROUP))] * 2
            + inverse_specs,
            out_specs=[lane_block(256), lane_block(H), lane_block(H)],
            out_shape=[wire_shape, shaped(H, LANES), shaped(H, LANES)],
            compiler_params=params,
            cost_estimate=cost(11),
        )(
            wire, lf_high, lf_low, swap, m1[0][:GROUP], m1[1][:GROUP], m2[0], m2[1], doubled,
            li_high, li_low,
        )
        *weights, wire, cot_chunks = lax.optimization_barrier((*weights, wire, cot_chunks))
        own_in = jnp.concatenate(weights[:4], axis=0)
        own_out = jnp.concatenate(weights[4:], axis=0)
        other_in = lax.ppermute(own_in, "lat", siblings)
        other_out = lax.ppermute(own_out, "lat", siblings)
        wire = lax.all_to_all(wire, "lat", 0, 0, tiled=True)

    with jax.named_scope("mix"):
        mixed, chunks = call(
            mix_kernel,
            [shaped(ROWS, W, BS), shaped(N_CH, 8 * ROWS, 6 * BS)],
            wire, tt_high, tt_low, x, stats, gain_column,
            scratch=[scratch],
        )
        chunks = lax.all_to_all(chunks, "ch", 0, 0, tiled=True)

    cells = 48 * ROWS
    direct = pl.BlockSpec((1, 384, 384), lambda e, place: (e, 0, 0))
    halved = pl.BlockSpec((1, 384, 384), lambda e, place: (e % 2 * 4 + e // 2, 0, 0))

    def all_of(shape):
        return pl.BlockSpec(shape, lambda e, place: (0,) * len(shape))

    with jax.named_scope("mlp"):
        out_chunks, grad_chunks, in_own, in_other, out_own, out_other = pl.pallas_call(
            mlp_kernel,
            grid_spec=pltpu.PrefetchScalarGridSpec(
                num_scalar_prefetch=1,
                grid=(N_CH,),
                in_specs=[
                    all_of((N_CH, 8 * ROWS, 6 * BS)),
                    all_of((N_CH, 8 * ROWS, 6 * BS)),
                    all_of((N_CH, 1, BS)),
                    direct,
                    direct,
                    halved,
                    halved,
                ],
                out_specs=[
                    all_of((N_CH, 8 * ROWS, 6 * BS)),
                    all_of((N_CH, 8 * ROWS + 8, 6 * BS)),
                    halved,
                    halved,
                    direct,
                    direct,
                ],
                scratch_shapes=[
                    pltpu.VMEM((cells, C), F32),
                    pltpu.VMEM((cells, C), BF16),
                    pltpu.VMEM((cells, C), BF16),
                    pltpu.VMEM((cells, 128), F32),
                    pltpu.VMEM((cells, C), F32),
                    pltpu.VMEM((cells, C), F32),
                ],
            ),
            out_shape=[
                shaped(N_CH, 8 * ROWS, 6 * BS, dtype=BF16),
                shaped(N_CH, 8 * ROWS + 8, 6 * BS, dtype=BF16),
                shaped(N_CH, 384, 384),
                shaped(N_CH, 384, 384, dtype=BF16),
                shaped(N_CH, 384, 384),
                shaped(N_CH, 384, 384, dtype=BF16),
            ],
            compiler_params=params,
            cost_estimate=cost(24),
        )(core_place, chunks, cot_chunks, gains,
          own_in, other_in, own_out, other_out)
        grad_chunks = lax.all_to_all(grad_chunks, "ch", 0, 0, tiled=True)

    with jax.named_scope("lon_back"):
        wire, grad_mixed, gain_parts = call(
            lon_back_kernel,
            [wire_shape, shaped(ROWS, BS, W, dtype=BF16), shaped(8, 128)],
            grad_chunks, x, stats, t_high, t_low,
            scratch=[scratch],
        )
        wire = lax.all_to_all(wire, "lat", 0, 0, tiled=True)

    with jax.named_scope("grads_ch"):
        theirs = lax.ppermute(in_other, "lat", siblings)
        odd = near((in_own[4:] + theirs[4:].astype(F32)).astype(BF16), 1)
        even = in_own[:4] + theirs[:4].astype(F32)
        theirs = lax.ppermute(out_other, "lat", siblings)
        pair = out_own[:2] + theirs[:2].astype(F32)
        pairs = [
            near((out_own[k : k + 2] + theirs[k : k + 2].astype(F32)).astype(BF16), k)
            for k in (2, 4, 6)
        ]
        odd, even, pair, *pairs, out_chunks, wire = lax.optimization_barrier(
            (odd, even, pair, *pairs, out_chunks, wire)
        )
        even = even + odd.astype(F32)
        for part in pairs:
            pair = pair + part.astype(F32)
        in_parts = [even[0]] + [near(even[k // 2].astype(BF16), k) for k in (2, 4, 6)]
        out_parts = [pair[0], near(pair[1].astype(BF16), 1)]

    with jax.named_scope("output"):
        out_chunks = lax.all_to_all(out_chunks, "ch", 0, 0, tiled=True)

    with jax.named_scope("spectral_back"):
        wire, small = pl.pallas_call(
            spectral_back_kernel,
            grid=(3,),
            in_specs=[lane_block(256), lane_block(H), lane_block(H)]
            + table_specs
            + [whole((2 * GROUP, GROUP))] * 2
            + [whole((GROUP, 2 * GROUP))] * 2
            + inverse_specs
            + [whole((1, BS)), whole((8, 128))],
            out_specs=[lane_block(256), whole((N_LAT + 8, LANES))],
            out_shape=[wire_shape, shaped(N_LAT + 8, LANES)],
            scratch_shapes=[
                pltpu.VMEM((GROUP, GROUP), F32),
                pltpu.VMEM((GROUP, GROUP), F32),
                pltpu.VMEM((8, 128), F32),
            ],
            compiler_params=params,
            cost_estimate=cost(14),
        )(
            wire, spectrum, pre_modes, lf_high, lf_low, swap, m1[0], m1[1], m2[0], m2[1], doubled,
            li_high, li_low, gain_first[None], gain_parts,
        )
        *grad_parts, out_chunks, wire = lax.optimization_barrier(
            (*in_parts, *out_parts, out_chunks, wire)
        )

    with jax.named_scope("pack"):
        wire = call(
            pack_kernel, shaped(N_LAT, 16, LANES, dtype=BF16), wire, small, *grad_parts
        )
        wire = lax.all_to_all(wire, "lat", 0, 0, tiled=True)

    with jax.named_scope("output_mix"):
        output = call(output_kernel, shaped(ROWS, BS, W, dtype=BF16), out_chunks, mixed)

    with jax.named_scope("unmix"):
        scaled, sums = call(
            unmix_kernel,
            [shaped(ROWS, BS, W), shaped(16, W)],
            wire, tt_high, tt_low, grad_mixed, x, stats, gain_column,
            scratch=[scratch],
        )
    with jax.named_scope("sums"):
        sums = [sums] + [near(sums, k) for k in range(1, N_CH)]

    with jax.named_scope("grads_lat"):
        payload = call(spread_kernel, shaped(N_LAT // 2, 56, GROUP, dtype=BF16), wire, small)
        mine = lax.all_to_all(payload, "lat", 0, 0, tiled=True, axis_index_groups=cores)
        mine, *sums = lax.optimization_barrier((mine, *sums))
        theirs = lax.ppermute(mine, "lat", siblings)
        weight_shape = shaped(2, 1, BS, BS)
        grad_fc_in, grad_fc_out, grad_w_inner, grad_w_outer, grad_first, grad_second = call(
            finish_kernel,
            [
                shaped(C, FF_DEV),
                shaped(FF_DEV, C),
                weight_shape,
                weight_shape,
                shaped(1, BS),
                shaped(1, BS),
            ],
            mine, theirs, place=core_place,
        )

    with jax.named_scope("final"):
        grad_fields = call(
            final_kernel, shaped(ROWS, BS, W, dtype=BF16), scaled, grad_mixed, x, stats, *sums
        )

    return (
        output.transpose(1, 0, 2),
        grad_fields.transpose(1, 0, 2),
        grad_first[0],
        grad_w_inner,
        grad_w_outer,
        grad_second[0],
        grad_fc_in,
        grad_fc_out,
    )


def solution(mesh):
    placed = (
        P("ch", "lat", None),
        P("ch"),
        P(None, "ch", None, None),
        P(None, "ch", None, None),
        P("ch"),
        P(None, "ch"),
        P("ch", None),
        P("ch", "lat", None),
    )
    return jax.shard_map(
        body,
        mesh=mesh,
        in_specs=placed,
        out_specs=(
            P("ch", "lat", None),
            P("ch", "lat", None),
            P("ch"),
            P(None, "ch", None, None),
            P(None, "ch", None, None),
            P("ch"),
            P(None, "ch"),
            P("ch", None),
        ),
        check_vma=False,
    )
```

```python
import math

import jax
import jax.numpy as jnp
import ml_dtypes
import numpy as np
from jax import lax
from jax.experimental import pallas as pl
from jax.experimental.pallas import tpu as pltpu
from jax.sharding import PartitionSpec as P

C = 768
BS = 96
H = 224
W = 384
KW = 192
N_LAT = 32
N_CH = 8
ROWS = 7
FF_DEV = 384
MODES = KW // N_LAT
PLANES = 2 * MODES
LANES = PLANES * BS
GROUP = 384
EPSILON = 1e-05
BF16 = jnp.bfloat16
F32 = jnp.float32
VMEM_BYTES = 56 * 1024 * 1024


def halves(table):
    high = table.astype(ml_dtypes.bfloat16)
    low = (table - high.astype(np.float64)).astype(ml_dtypes.bfloat16)
    return high, low


def lon_table():
    mode = np.arange(MODES)[:, None] + MODES * np.arange(N_LAT)[None, :]
    angles = 2 * np.pi * ((mode[:, :, None] * np.arange(W)) % W) / W
    table = np.stack([np.cos(angles), -np.sin(angles)], 1) / math.sqrt(W)
    return table.reshape(PLANES * N_LAT, W)


def lat_tables():
    index = np.arange(H)
    angles = 2 * np.pi * ((index[:, None] * index[None, :]) % H) / H
    cosine = np.cos(angles) / math.sqrt(H)
    sine = np.sin(angles) / math.sqrt(H)
    forward = np.zeros((H, 2, N_LAT, 8))
    forward[:, 0, :, :ROWS] = cosine.reshape(H, N_LAT, ROWS)
    forward[:, 1, :, :ROWS] = sine.reshape(H, N_LAT, ROWS)
    inverse = np.zeros((N_LAT, 8, 2, H))
    inverse[:, :ROWS, 0] = cosine.reshape(N_LAT, ROWS, H)
    inverse[:, :ROWS, 1] = -sine.reshape(N_LAT, ROWS, H)
    return forward.reshape(H, 2 * N_LAT * 8), inverse.reshape(N_LAT * 8, 2 * H)


def swap_table():
    table = np.zeros((GROUP, GROUP))
    for mode in range(2):
        for c in range(BS):
            real = mode * 2 * BS + c
            table[real + BS, real] = 1
            table[real, real + BS] = -1
    return table.astype(ml_dtypes.bfloat16)


def dot(left, right):
    return lax.dot_general(left, right, (((1,), (0,)), ((), ())), preferred_element_type=F32)


def dot_nt(left, right):
    return lax.dot_general(left, right, (((1,), (1,)), ((), ())), preferred_element_type=F32)


def dot_tn(left, right):
    return lax.dot_general(left, right, (((0,), (0,)), ((), ())), preferred_element_type=F32)


def split(values):
    high = values.astype(BF16)
    return high, (values - high.astype(F32)).astype(BF16)


def dot3(kind, left, right):
    return kind(left[0], right[0]) + kind(left[1], right[0]) + kind(left[0], right[1])


def gelu_parts(values):
    cdf = 0.5 * (1.0 + lax.erf(values * 0.7071067811865476))
    return values * cdf, cdf + values * 0.3989422804014327 * jnp.exp(-0.5 * values * values)


def gelu_value(values):
    return 0.5 * values * (1.0 + lax.erf(values * 0.7071067811865476))


def norm_rows(stats):
    total = stats[0]
    for e in range(1, N_CH):
        total = total + stats[e]
    average = total[0:8] * (1.0 / C)
    squares = total[8:16] * (1.0 / C)
    return average, lax.rsqrt(squares - average * average + EPSILON)


def put_row(scratch, row, modes):
    wide = jnp.concatenate([modes[32 * k : 32 * k + 32] for k in range(PLANES)], axis=1)
    for t in range(LANES // 128):
        scratch[t, pl.ds(row, N_LAT, stride=8), :] = wide[:, 128 * t : 128 * t + 128]


def flush_rows(scratch, wire):
    for t in range(LANES // 128):
        scratch[t, pl.ds(ROWS, N_LAT, stride=8), :] = jnp.zeros((N_LAT, 128), F32)
        wire[:, 128 * t : 128 * t + 128] = scratch[t].astype(BF16)


def load_rows(wire, scratch):
    for t in range(LANES // 128):
        scratch[t] = wire[:, 128 * t : 128 * t + 128].astype(F32)


def load_packed(wire, scratch):
    for t in range(LANES // 128):
        block = wire[:, :, 128 * t : 128 * t + 128].astype(F32)
        scratch[t] = block[:, :8].reshape(8 * N_LAT, 128)


def get_row(scratch, row):
    wide = jnp.concatenate(
        [scratch[t, pl.ds(row, N_LAT, stride=8), :] for t in range(LANES // 128)], axis=1
    )
    return jnp.concatenate([wide[:, BS * k : BS * k + BS] for k in range(PLANES)], axis=0)


def to_chunk(rows, e):
    return jnp.concatenate(
        [
            jnp.concatenate(
                [values[48 * e + 8 * a : 48 * e + 8 * a + 8] for a in range(6)], axis=1
            )
            for values in rows
        ],
        axis=0,
    )


def from_chunks(chunks, row):
    return jnp.concatenate(
        [
            chunk[8 * row : 8 * row + 8, BS * a : BS * a + BS]
            for chunk in chunks
            for a in range(6)
        ],
        axis=0,
    )


def cot_kernel(cot, wire):
    rows = [cot[r].astype(F32).T for r in range(ROWS)]
    for e in range(N_CH):
        wire[e] = to_chunk(rows, e).astype(BF16)


def lon_kernel(x, stats, gain, t_high, t_low, wire, scratch):
    average, inv_std = norm_rows(stats)
    table = (t_high[...], t_low[...])
    for r in range(ROWS):
        normed = (x[r].astype(F32) - average[r : r + 1]) * inv_std[r : r + 1]
        lifted = split(normed * gain[...])
        put_row(scratch, r, dot3(dot_nt, table, lifted))
    flush_rows(scratch, wire)


def lat_forward(wire, lf_high, lf_low, swap):
    values = wire[...]
    swapped = dot(values, swap[...]).astype(BF16)
    both = jnp.concatenate([values, swapped], axis=0)
    return dot(lf_high[...], both) + dot(lf_low[...], both)


def lat_inverse(modes, li_high, li_low):
    both = split(jnp.concatenate([modes[:, :GROUP], modes[:, GROUP:]], axis=0))
    return dot3(dot, (li_high[...], li_low[...]), both)


def weight_sum(blocks):
    def block(part, other):
        pieces = [
            blocks[m + BS * part : m + BS * part + BS, m + BS * other : m + BS * other + BS]
            for m in (0, 2 * BS)
        ]
        return pieces[0] + pieces[1]

    return jnp.concatenate(
        [block(0, 0) + block(1, 1), block(1, 0) - block(0, 1)], axis=0
    )


def spectral_kernel(
    wire, lf_high, lf_low, swap, m1_high, m1_low, m2_high, m2_low, doubled, li_high, li_low,
    out, spectrum, pre_modes,
):
    modes = lat_forward(wire, lf_high, lf_low, swap)
    spectrum[...] = modes
    pre = dot3(dot, split(modes), (m1_high[...], m1_low[...]))
    pre_modes[...] = pre
    act = split(gelu_value(pre))
    scale = doubled[...]
    result = dot3(dot, act, (m2_high[...], m2_low[...])) * jnp.concatenate([scale, scale], axis=1)
    out[...] = lat_inverse(result, li_high, li_low).astype(BF16)


def spectral_back_kernel(
    wire, spectrum, pre_modes, lf_high, lf_low, swap, m1_high, m1_low, m2_high, m2_low, doubled,
    li_high, li_low, gain, gain_parts, out, small, grad_outer, grad_inner, gain_sum,
):
    @pl.when(pl.program_id(0) == 0)
    def _():
        grad_outer[...] = jnp.zeros_like(grad_outer)
        grad_inner[...] = jnp.zeros_like(grad_inner)
        gain_sum[...] = jnp.zeros_like(gain_sum)

    grad = split(lat_forward(wire, lf_high, lf_low, swap) * doubled[...])
    act, slope = gelu_parts(pre_modes[...])
    grad_act = dot3(dot_nt, grad, (m2_high[:, :GROUP], m2_low[:, :GROUP]))
    grad_outer[...] += dot3(dot_tn, grad, split(act))
    grad_pre = split(grad_act * slope)
    modes = spectrum[...]
    grad_inner[...] += dot3(dot_tn, grad_pre, split(modes))
    grad_spectrum = dot3(dot_nt, grad_pre, (m1_high[...], m1_low[...]))
    gain_row = jnp.sum(grad_spectrum[:, :GROUP] * modes, axis=0, keepdims=True)
    gain_row = sum(gain_row[:, BS * k : BS * k + BS] for k in range(4))
    gain_sum[0:1, :BS] += gain_row
    out[...] = lat_inverse(grad_spectrum, li_high, li_low).astype(BF16)

    @pl.when(pl.program_id(0) == 2)
    def _():
        first = gain_sum[0:1, :BS] / gain[...] + gain_parts[0:1, :BS]
        weights = [weight_sum(grad_inner[...]), weight_sum(grad_outer[...])]
        small[:N_LAT] = jnp.concatenate(
            [weight[32 * q : 32 * q + 32] for weight in weights for q in range(6)], axis=1
        )
        row = []
        for values in (first, gain_parts[1:2, :BS]):
            high = values.astype(BF16).astype(F32)
            row += [high, values - high]
        row = jnp.concatenate(row + [jnp.zeros((1, 8 * BS), F32)], axis=1)
        small[N_LAT:] = jnp.concatenate([row, jnp.zeros((7, LANES), F32)], axis=0)


def mix_kernel(wire, tt_high, tt_low, x, stats, gain, mixed, chunks, scratch):
    average, inv_std = norm_rows(stats)
    load_rows(wire, scratch)
    rows = []
    for r in range(ROWS):
        x_float = x[r].astype(F32)
        lifted = (x_float - average[r : r + 1]) * inv_std[r : r + 1] * gain[...]
        modes = get_row(scratch, r).astype(BF16)
        filtered = dot(tt_high[...], modes) + dot(tt_low[...], modes)
        values = filtered + (lifted + x_float).T
        mixed[r] = values
        rows.append(values)
    for e in range(N_CH):
        chunks[e] = to_chunk(rows, e)


def mlp_kernel(core, mixed, cot, gain, *refs):
    weights, refs = refs[:12], refs[12:]
    out_chunks, grad_chunks, grad_in_own, grad_in_other, grad_out_own, grad_out_other = refs[:6]
    normed, inputs, cots, inv_std, sum_out, sum_grad, weight_in, weight_out, arrived = refs[6:]
    step = pl.program_id(0)
    turn = 4 * core[0]
    cells = 6 * 8 * ROWS
    part = 8 * ROWS

    def gain_row():
        return jnp.concatenate([gain[e ^ turn] for e in range(N_CH)], axis=1)

    def copies(p):
        found = []
        for half in range(2):
            parts = weights[6 * half : 6 * half + 6]
            rows = pl.ds(384 * half, 384)
            for b in range(2):
                units = pl.ds(384 * b, 384)
                found.append((parts[p].at[b], weight_in.at[p, rows, units]))
                found.append((parts[4 + b].at[p], weight_out.at[p, units, rows]))
        return [
            pltpu.make_async_copy(source, target, arrived.at[8 * p + n])
            for n, (source, target) in enumerate(found)
        ]

    @pl.when(step == 0)
    def _():
        for p in range(4):
            for copy in copies(p):
                copy.start()
        pieces = [mixed[e ^ turn] for e in range(N_CH)]
        values = jnp.concatenate(
            [
                jnp.concatenate([piece[:, BS * a : BS * a + BS] for piece in pieces], axis=1)
                for a in range(6)
            ],
            axis=0,
        )
        average = jnp.sum(values, axis=1, keepdims=True) * (1.0 / C)
        squares = jnp.sum(values * values, axis=1, keepdims=True) * (1.0 / C)
        inv = lax.rsqrt(squares - average * average + EPSILON)
        values = (values - average) * inv
        normed[...] = values
        inv_std[...] = jnp.broadcast_to(inv, (cells, 128))
        inputs[...] = (values * gain_row()).astype(BF16)
        pieces = [cot[e ^ turn].astype(F32) for e in range(N_CH)]
        cots[...] = jnp.concatenate(
            [
                jnp.concatenate([piece[:, BS * a : BS * a + BS] for piece in pieces], axis=1)
                for a in range(6)
            ],
            axis=0,
        ).astype(BF16)
        sum_out[...] = jnp.zeros_like(sum_out)
        sum_grad[...] = jnp.zeros_like(sum_grad)

    for p in range(4):

        @pl.when(step == p)
        def _():
            for copy in copies(p):
                copy.wait()

    own_in, own_out = weight_in[step], weight_out[step]
    values, given = inputs[...], cots[...]
    hidden, slope = gelu_parts(dot(values, own_in))
    hidden = hidden.astype(BF16)
    grad_pre = (dot_nt(given, own_out) * slope).astype(BF16)
    sum_out[...] += dot(hidden, own_out)
    sum_grad[...] += dot_nt(grad_pre, own_in)
    grad_in = dot_tn(values, grad_pre)
    grad_out = dot_tn(hidden, given)
    for b in range(2):
        units = slice(384 * b, 384 * b + 384)
        grad_in_own[b, 0] = grad_in[:384, units]
        grad_in_other[b, 0] = grad_in[384:, units].astype(BF16)
        grad_out_own[b] = grad_out[units, :384]
        grad_out_other[b] = grad_out[units, 384:].astype(BF16)

    @pl.when(step == 3)
    def _():
        grad_input = sum_grad[...]
        values = normed[...]
        gain_sum = jnp.sum(grad_input * values, axis=0, keepdims=True)
        scaled = grad_input * gain_row()
        leading = jnp.sum(scaled, axis=1, keepdims=True) * (1.0 / C)
        paired = jnp.sum(scaled * values, axis=1, keepdims=True) * (1.0 / C)
        grad_mixed = cots[...].astype(F32) + inv_std[:, :1] * (scaled - leading - values * paired)
        outputs = sum_out[...]

        def chunk(array, e):
            return jnp.concatenate(
                [array[part * a : part * a + part, BS * e : BS * e + BS] for a in range(6)],
                axis=1,
            )

        for e in range(N_CH):
            out_chunks[e ^ turn] = chunk(outputs, e).astype(BF16)
            gain_piece = gain_sum[:, BS * e : BS * e + BS]
            gain_high = gain_piece.astype(BF16).astype(F32)
            extra = jnp.concatenate(
                [gain_high, gain_piece - gain_high, jnp.zeros((1, 4 * BS), F32)], axis=1
            )
            extra = jnp.concatenate([extra, jnp.zeros((7, 6 * BS), F32)], axis=0)
            grad_chunks[e ^ turn] = jnp.concatenate(
                [chunk(grad_mixed, e), extra], axis=0
            ).astype(BF16)


def lon_back_kernel(chunks, x, stats, t_high, t_low, wire, grad_mixed, gains, scratch):
    average, inv_std = norm_rows(stats)
    pieces = [chunks[e].astype(F32) for e in range(N_CH)]
    gain_first = jnp.zeros((BS, 1), F32)
    for r in range(ROWS):
        values = from_chunks(pieces, r)
        rounded = values.astype(BF16)
        put_row(scratch, r, dot(t_high[...], rounded) + dot(t_low[...], rounded))
        turned = values.T
        grad_mixed[r] = turned.astype(BF16)
        normed = (x[r].astype(F32) - average[r : r + 1]) * inv_std[r : r + 1]
        gain_first = gain_first + jnp.sum(turned * normed, axis=1, keepdims=True)
    flush_rows(scratch, wire)
    gain_second = jnp.zeros((1, BS), F32)
    for piece in pieces:
        row = piece[8 * ROWS : 8 * ROWS + 1]
        gain_second = gain_second + row[:, :BS] + row[:, BS : 2 * BS]
    turned_first = jnp.broadcast_to(gain_first, (BS, 128)).T[0:1, :]
    gains[0:1, :BS] = turned_first
    gains[1:2, :BS] = gain_second


def unmix_kernel(wire, tt_high, tt_low, grad_mixed, x, stats, gain, scaled, sums, scratch):
    average, inv_std = norm_rows(stats)
    load_packed(wire, scratch)
    for r in range(ROWS):
        modes = get_row(scratch, r).astype(BF16)
        back = dot(tt_high[...], modes) + dot(tt_low[...], modes)
        values = (back.T + grad_mixed[r].astype(F32)) * gain[...]
        normed = (x[r].astype(F32) - average[r : r + 1]) * inv_std[r : r + 1]
        scaled[r] = values
        sums[r : r + 1] = jnp.sum(values, axis=0, keepdims=True)
        sums[8 + r : 9 + r] = jnp.sum(values * normed, axis=0, keepdims=True)
    sums[7:8] = jnp.zeros((1, W), F32)
    sums[15:16] = jnp.zeros((1, W), F32)


def final_kernel(scaled, grad_mixed, x, stats, *rest):
    average, inv_std = norm_rows(stats)
    out = rest[-1]
    total = rest[0][...]
    for part in rest[1:-1]:
        total = total + part[...]
    total = total * (1.0 / C)
    for r in range(ROWS):
        inv = inv_std[r : r + 1]
        normed = (x[r].astype(F32) - average[r : r + 1]) * inv
        change = scaled[r] - total[r : r + 1] - normed * total[8 + r : 9 + r]
        out[r] = (grad_mixed[r].astype(F32) + inv * change).astype(BF16)


def pack_kernel(wire, small, in_0, in_2, in_4, in_6, out_0, out_1, out):
    total_in = in_0[...] + in_2[...].astype(F32) + in_4[...].astype(F32) + in_6[...].astype(F32)
    total_out = out_0[...] + out_1[...].astype(F32)
    total = jnp.concatenate([total_in, total_out], axis=0)
    modes = wire[...].astype(F32).reshape(N_LAT, 8, LANES)
    weights = small[:N_LAT]
    row = lax.broadcasted_iota(jnp.int32, (N_LAT, 8, LANES), 1)
    modes = jnp.where(row == ROWS, weights[:, None, :], modes)
    grads = jnp.concatenate(
        [total[256 * g : 256 * g + 256].reshape(N_LAT, 8, GROUP) for g in range(3)], axis=2
    )
    out[...] = jnp.concatenate([modes, grads], axis=1).astype(BF16)


def spread_kernel(parts, small, out):
    sums = [parts[n].astype(F32) for n in (0, 1)]
    for n in range(2, N_LAT):
        sums[n % 2] = sums[n % 2] + parts[n].astype(F32)
    rows = [
        half[8:16, GROUP * g : GROUP * g + GROUP] for half in sums for g in range(3)
    ]
    weights = sums[0][ROWS : ROWS + 1] + sums[1][ROWS : ROWS + 1]
    last = [weights[:, GROUP * g : GROUP * g + GROUP] for g in range(3)]
    last += [small[N_LAT : N_LAT + 1, :GROUP], jnp.zeros((4, GROUP), F32)]
    total = jnp.concatenate(rows + [jnp.concatenate(last, axis=0)], axis=0).astype(BF16)
    for n in range(N_LAT // 2):
        out[n] = total


def finish_kernel(
    place, mine, theirs, grad_in, grad_out, grad_inner, grad_outer, gain_first, gain_second
):
    first = place[0] == 0
    one, two = mine[...].astype(F32), theirs[...].astype(F32)
    even, odd = jnp.where(first, one, two), jnp.where(first, two, one)

    def rows(start):
        parts = [part[:, start : start + 8][:, None] for part in (even, odd)]
        return jnp.concatenate(parts, axis=1).reshape(256, GROUP)

    for half in range(2):
        total = jnp.concatenate([rows(24 * half + 8 * g) for g in range(3)], axis=0)
        grad_in[384 * half : 384 * half + 384] = total[:384]
        grad_out[:, 384 * half : 384 * half + 384] = total[384:]
    last = rows(48)
    planes = [
        jnp.concatenate([last[8 * n + g : 8 * n + g + 1] for n in range(N_LAT)], axis=0)
        for g in range(4)
    ]
    weights = [
        plane[:, BS * q : BS * q + BS] for plane in planes[:3] for q in range(4)
    ]
    for part in range(2):
        grad_inner[part, 0] = jnp.concatenate(weights[3 * part : 3 * part + 3], axis=0)
        grad_outer[part, 0] = jnp.concatenate(weights[6 + 3 * part : 9 + 3 * part], axis=0)
    gains = jnp.sum(planes[3], axis=0, keepdims=True)
    gain_first[...] = gains[:, :BS] + gains[:, BS : 2 * BS]
    gain_second[...] = gains[:, 2 * BS : 3 * BS] + gains[:, 3 * BS :]


def output_kernel(chunks, mixed, out):
    pieces = [chunks[e].astype(F32) for e in range(N_CH)]
    for r in range(ROWS):
        out[r] = (from_chunks(pieces, r) + mixed[r]).T.astype(BF16)


def cost(micros):
    return pl.CostEstimate(
        flops=int(micros * 1.0e9), bytes_accessed=int(micros * 2.0e6), transcendentals=0
    )


def call(kernel, out_shape, *args, scratch=(), micros=3, place=None):
    specs = [pl.BlockSpec(memory_space=pltpu.VMEM)] * len(args)
    if place is not None:
        args = (place,) + args
        specs = [pl.BlockSpec(memory_space=pltpu.SMEM)] + specs
    return pl.pallas_call(
        kernel,
        out_shape=out_shape,
        in_specs=specs,
        scratch_shapes=scratch,
        compiler_params=pltpu.CompilerParams(vmem_limit_bytes=VMEM_BYTES),
        cost_estimate=cost(micros),
    )(*args)


def shaped(*shape, dtype=F32):
    return jax.ShapeDtypeStruct(shape, dtype)


def whole(shape):
    return pl.BlockSpec(shape, lambda g: (0,) * len(shape))


def lane_block(rows):
    return pl.BlockSpec((rows, GROUP), lambda g: (0, g))


def block_matrix(weight, swap_columns, swap_rows):
    real, imag = weight[0, 0].T, weight[1, 0].T
    base = [[real, imag], [-imag, real]]
    if swap_columns:
        base = [[imag, -real], [real, imag]]
    if swap_rows:
        base = [[-imag, real], [-real, -imag]]
    one = jnp.concatenate([jnp.concatenate(line, axis=1) for line in base], axis=0)
    zero = jnp.zeros_like(one)
    return jnp.concatenate(
        [jnp.concatenate([one, zero], axis=1), jnp.concatenate([zero, one], axis=1)], axis=0
    )


def to_all(values, axis, count, **kwargs):
    spread = jnp.broadcast_to(values[None], (count,) + values.shape)
    return lax.all_to_all(spread, axis, 0, 0, tiled=True, **kwargs)


def near(values, k):
    return lax.ppermute(values, "ch", [(i, i ^ k) for i in range(N_CH)])


def body(fields, gain_first, w_inner, w_outer, gain_second, fc_in, fc_out, cotangent):
    lat = lax.axis_index("lat")
    core = lat % 2
    core_place = core[None].astype(jnp.int32)
    siblings = [(i, i ^ 1) for i in range(N_LAT)]
    cores = [list(range(0, N_LAT, 2)), list(range(1, N_LAT, 2))]
    t_high, t_low = (jnp.asarray(t) for t in halves(lon_table()))
    tt_high, tt_low = (jnp.asarray(t) for t in halves(lon_table().T))
    forward, inverse = lat_tables()
    lf_high, lf_low = (jnp.asarray(t) for t in halves(forward))
    li_high, li_low = (jnp.asarray(t) for t in halves(inverse))
    swap = jnp.asarray(swap_table())

    x = fields.transpose(1, 0, 2)
    cot = cotangent.transpose(1, 0, 2)
    gain_column = gain_first[:, None]

    with jax.named_scope("stats"):
        x_float = x.astype(F32)
        zero = jnp.zeros((1, W), F32)
        payload = jnp.concatenate(
            [
                jnp.sum(x_float, 1),
                zero,
                jnp.sum(x_float * x_float, 1),
                zero,
                jnp.pad(gain_second, (0, W - BS))[None],
                jnp.zeros((7, W), F32),
            ],
            axis=0,
        )
        payload, fc_in, fc_out = lax.optimization_barrier((payload, fc_in, fc_out))
        gathered = to_all(payload, "ch", N_CH)

    with jax.named_scope("weights"):
        half_in = lax.dynamic_slice_in_dim(fc_in, core * 384, 384, 0)
        half_out = lax.dynamic_slice_in_dim(fc_out, core * 384, 384, 1)
        near_in = near(half_in, 1)
        near_out = [near(half_out, k) for k in (2, 4, 6)]

    with jax.named_scope("cot"):
        cot_chunks = call(cot_kernel, shaped(N_CH, 8 * ROWS, 6 * BS, dtype=BF16), cot)

    with jax.named_scope("stats"):
        near_in, *near_out, cot_chunks, gathered = lax.optimization_barrier(
            (near_in, *near_out, cot_chunks, gathered)
        )
        stats = gathered[:, :16]
        gains = gathered[:, 16:17, :BS]

    with jax.named_scope("weights"):
        pair = jnp.stack([half_in, near_in])
        own_in = [pair] + [near(pair, k) for k in (2, 4, 6)]
        quad = jnp.stack([half_out] + near_out)
        own_out = [quad, near(quad, 1)]

    scratch = pltpu.VMEM((LANES // 128, 8 * N_LAT, 128), F32)
    wire_shape = shaped(8 * N_LAT, LANES, dtype=BF16)
    with jax.named_scope("lon"):
        wire = call(
            lon_kernel, wire_shape, x, stats, gain_column, t_high, t_low, scratch=[scratch]
        )
        wire = lax.all_to_all(wire, "lat", 0, 0, tiled=True)

    with jax.named_scope("cot"):
        cot_chunks, wire = lax.optimization_barrier((cot_chunks, wire))
        cot_chunks = lax.all_to_all(cot_chunks, "ch", 0, 0, tiled=True)

    with jax.named_scope("matrices"):
        m1 = split(
            jnp.concatenate(
                [block_matrix(w_inner, False, False), block_matrix(w_inner, False, True)], axis=0
            )
        )
        m2 = split(
            jnp.concatenate(
                [block_matrix(w_outer, False, False), block_matrix(w_outer, True, False)], axis=1
            )
        )
        lane = jnp.arange(LANES, dtype=jnp.int32)[None]
        doubled = jnp.where((lat == 0) & (lane < 2 * BS), 1.0, 2.0).astype(F32)

    table_specs = [whole((H, 512)), whole((H, 512)), whole((GROUP, GROUP))]
    inverse_specs = [lane_block(1), whole((256, 448)), whole((256, 448))]
    params = pltpu.CompilerParams(vmem_limit_bytes=VMEM_BYTES)
    with jax.named_scope("spectral"):
        wire, spectrum, pre_modes = pl.pallas_call(
            spectral_kernel,
            grid=(3,),
            in_specs=[lane_block(256)]
            + table_specs
            + [whole((GROUP, GROUP))] * 2
            + [whole((GROUP, 2 * GROUP))] * 2
            + inverse_specs,
            out_specs=[lane_block(256), lane_block(H), lane_block(H)],
            out_shape=[wire_shape, shaped(H, LANES), shaped(H, LANES)],
            compiler_params=params,
            cost_estimate=cost(11),
        )(
            wire, lf_high, lf_low, swap, m1[0][:GROUP], m1[1][:GROUP], m2[0], m2[1], doubled,
            li_high, li_low,
        )
        *weights, wire, cot_chunks = lax.optimization_barrier(
            (*own_in, *own_out, wire, cot_chunks)
        )
        weights += [lax.ppermute(part, "lat", siblings) for part in weights]
        wire = lax.all_to_all(wire, "lat", 0, 0, tiled=True)

    with jax.named_scope("mix"):
        mixed, chunks = call(
            mix_kernel,
            [shaped(ROWS, W, BS), shaped(N_CH, 8 * ROWS, 6 * BS)],
            wire, tt_high, tt_low, x, stats, gain_column,
            scratch=[scratch],
        )
        chunks = lax.all_to_all(chunks, "ch", 0, 0, tiled=True)

    cells = 48 * ROWS
    halved = pl.BlockSpec((2, 1, 384, 384), lambda p, place: (0, p, 0, 0))
    direct = pl.BlockSpec((2, 384, 384), lambda p, place: (p, 0, 0))

    def all_of(shape):
        return pl.BlockSpec(shape, lambda e, place: (0,) * len(shape))

    with jax.named_scope("mlp"):
        out_chunks, grad_chunks, in_own, in_other, out_own, out_other = pl.pallas_call(
            mlp_kernel,
            grid_spec=pltpu.PrefetchScalarGridSpec(
                num_scalar_prefetch=1,
                grid=(4,),
                in_specs=[
                    all_of((N_CH, 8 * ROWS, 6 * BS)),
                    all_of((N_CH, 8 * ROWS, 6 * BS)),
                    all_of((N_CH, 1, BS)),
                ]
                + [pl.BlockSpec(memory_space=pl.ANY)] * 12,
                out_specs=[
                    all_of((N_CH, 8 * ROWS, 6 * BS)),
                    all_of((N_CH, 8 * ROWS + 8, 6 * BS)),
                    halved,
                    halved,
                    direct,
                    direct,
                ],
                scratch_shapes=[
                    pltpu.VMEM((cells, C), F32),
                    pltpu.VMEM((cells, C), BF16),
                    pltpu.VMEM((cells, C), BF16),
                    pltpu.VMEM((cells, 128), F32),
                    pltpu.VMEM((cells, C), F32),
                    pltpu.VMEM((cells, C), F32),
                    pltpu.VMEM((4, C, C), BF16),
                    pltpu.VMEM((4, C, C), BF16),
                    pltpu.SemaphoreType.DMA((32,)),
                ],
            ),
            out_shape=[
                shaped(N_CH, 8 * ROWS, 6 * BS, dtype=BF16),
                shaped(N_CH, 8 * ROWS + 8, 6 * BS, dtype=BF16),
                shaped(2, 4, 384, 384),
                shaped(2, 4, 384, 384, dtype=BF16),
                shaped(N_CH, 384, 384),
                shaped(N_CH, 384, 384, dtype=BF16),
            ],
            compiler_params=params,
            cost_estimate=cost(20),
        )(core_place, chunks, cot_chunks, gains, *weights)
        grad_chunks = lax.all_to_all(grad_chunks, "ch", 0, 0, tiled=True)

    with jax.named_scope("grads_ch"):
        theirs_in = lax.ppermute(in_other, "lat", siblings)
        theirs_out = lax.ppermute(out_other, "lat", siblings)
        odd = (in_own[1] + theirs_in[1].astype(F32)).astype(BF16)
        pairs = [
            (out_own[k : k + 2] + theirs_out[k : k + 2].astype(F32)).astype(BF16)
            for k in (2, 4, 6)
        ]
        odd, *pairs, grad_chunks = lax.optimization_barrier((odd, *pairs, grad_chunks))
        odd = near(odd, 1)
        pairs = [near(part, k) for part, k in zip(pairs, (2, 4, 6))]

    with jax.named_scope("lon_back"):
        wire, grad_mixed, gain_parts = call(
            lon_back_kernel,
            [wire_shape, shaped(ROWS, BS, W, dtype=BF16), shaped(8, 128)],
            grad_chunks, x, stats, t_high, t_low,
            scratch=[scratch],
        )
        wire = lax.all_to_all(wire, "lat", 0, 0, tiled=True)

    with jax.named_scope("grads_ch"):
        even = in_own[0] + theirs_in[0].astype(F32)
        pair = out_own[:2] + theirs_out[:2].astype(F32)
        odd, even, pair, *pairs, out_chunks, wire = lax.optimization_barrier(
            (odd, even, pair, *pairs, out_chunks, wire)
        )
        even = even + odd.astype(F32)
        for part in pairs:
            pair = pair + part.astype(F32)
        in_parts = [even[0]] + [near(even[k // 2].astype(BF16), k) for k in (2, 4, 6)]
        out_parts = [pair[0], near(pair[1].astype(BF16), 1)]

    with jax.named_scope("output"):
        out_chunks = lax.all_to_all(out_chunks, "ch", 0, 0, tiled=True)

    with jax.named_scope("spectral_back"):
        wire, small = pl.pallas_call(
            spectral_back_kernel,
            grid=(3,),
            in_specs=[lane_block(256), lane_block(H), lane_block(H)]
            + table_specs
            + [whole((2 * GROUP, GROUP))] * 2
            + [whole((GROUP, 2 * GROUP))] * 2
            + inverse_specs
            + [whole((1, BS)), whole((8, 128))],
            out_specs=[lane_block(256), whole((N_LAT + 8, LANES))],
            out_shape=[wire_shape, shaped(N_LAT + 8, LANES)],
            scratch_shapes=[
                pltpu.VMEM((GROUP, GROUP), F32),
                pltpu.VMEM((GROUP, GROUP), F32),
                pltpu.VMEM((8, 128), F32),
            ],
            compiler_params=params,
            cost_estimate=cost(14),
        )(
            wire, spectrum, pre_modes, lf_high, lf_low, swap, m1[0], m1[1], m2[0], m2[1], doubled,
            li_high, li_low, gain_first[None], gain_parts,
        )
        *grad_parts, out_chunks, wire = lax.optimization_barrier(
            (*in_parts, *out_parts, out_chunks, wire)
        )

    with jax.named_scope("pack"):
        wire = call(
            pack_kernel, shaped(N_LAT, 16, LANES, dtype=BF16), wire, small, *grad_parts
        )
        wire = lax.all_to_all(wire, "lat", 0, 0, tiled=True)

    with jax.named_scope("output_mix"):
        output = call(output_kernel, shaped(ROWS, BS, W, dtype=BF16), out_chunks, mixed)

    with jax.named_scope("unmix"):
        scaled, sums = call(
            unmix_kernel,
            [shaped(ROWS, BS, W), shaped(16, W)],
            wire, tt_high, tt_low, grad_mixed, x, stats, gain_column,
            scratch=[scratch],
        )
    with jax.named_scope("sums"):
        sums = [sums] + [near(sums, k) for k in range(1, N_CH)]

    with jax.named_scope("grads_lat"):
        payload = call(spread_kernel, shaped(N_LAT // 2, 56, GROUP, dtype=BF16), wire, small)
        mine = lax.all_to_all(payload, "lat", 0, 0, tiled=True, axis_index_groups=cores)
        mine, *sums = lax.optimization_barrier((mine, *sums))
        theirs = lax.ppermute(mine, "lat", siblings)
        weight_shape = shaped(2, 1, BS, BS)
        grad_fc_in, grad_fc_out, grad_w_inner, grad_w_outer, grad_first, grad_second = call(
            finish_kernel,
            [
                shaped(C, FF_DEV),
                shaped(FF_DEV, C),
                weight_shape,
                weight_shape,
                shaped(1, BS),
                shaped(1, BS),
            ],
            mine, theirs, place=core_place,
        )

    with jax.named_scope("final"):
        grad_fields = call(
            final_kernel, shaped(ROWS, BS, W, dtype=BF16), scaled, grad_mixed, x, stats, *sums
        )

    return (
        output.transpose(1, 0, 2),
        grad_fields.transpose(1, 0, 2),
        grad_first[0],
        grad_w_inner,
        grad_w_outer,
        grad_second[0],
        grad_fc_in,
        grad_fc_out,
    )


def solution(mesh):
    placed = (
        P("ch", "lat", None),
        P("ch"),
        P(None, "ch", None, None),
        P(None, "ch", None, None),
        P("ch"),
        P(None, "ch"),
        P("ch", None),
        P("ch", "lat", None),
    )
    return jax.shard_map(
        body,
        mesh=mesh,
        in_specs=placed,
        out_specs=(
            P("ch", "lat", None),
            P("ch", "lat", None),
            P("ch"),
            P(None, "ch", None, None),
            P(None, "ch", None, None),
            P("ch"),
            P(None, "ch"),
            P("ch", None),
        ),
        check_vma=False,
    )
```

```python
import math

import jax
import jax.numpy as jnp
import ml_dtypes
import numpy as np
from jax import lax
from jax.experimental import pallas as pl
from jax.experimental.pallas import tpu as pltpu
from jax.sharding import PartitionSpec as P

C = 768
BS = 96
H = 224
W = 384
KW = 192
N_LAT = 32
N_CH = 8
ROWS = 7
FF_DEV = 384
MODES = KW // N_LAT
PLANES = 2 * MODES
LANES = PLANES * BS
GROUP = 384
EPSILON = 1e-05
BF16 = jnp.bfloat16
F32 = jnp.float32
VMEM_BYTES = 56 * 1024 * 1024


def halves(table):
    high = table.astype(ml_dtypes.bfloat16)
    low = (table - high.astype(np.float64)).astype(ml_dtypes.bfloat16)
    return high, low


def lon_table():
    mode = np.arange(MODES)[:, None] + MODES * np.arange(N_LAT)[None, :]
    angles = 2 * np.pi * ((mode[:, :, None] * np.arange(W)) % W) / W
    table = np.stack([np.cos(angles), -np.sin(angles)], 1) / math.sqrt(W)
    return table.reshape(PLANES * N_LAT, W)


def lat_tables():
    index = np.arange(H)
    angles = 2 * np.pi * ((index[:, None] * index[None, :]) % H) / H
    cosine = np.cos(angles) / math.sqrt(H)
    sine = np.sin(angles) / math.sqrt(H)
    forward = np.zeros((H, 2, N_LAT, 8))
    forward[:, 0, :, :ROWS] = cosine.reshape(H, N_LAT, ROWS)
    forward[:, 1, :, :ROWS] = sine.reshape(H, N_LAT, ROWS)
    inverse = np.zeros((N_LAT, 8, 2, H))
    inverse[:, :ROWS, 0] = cosine.reshape(N_LAT, ROWS, H)
    inverse[:, :ROWS, 1] = -sine.reshape(N_LAT, ROWS, H)
    return forward.reshape(H, 2 * N_LAT * 8), inverse.reshape(N_LAT * 8, 2 * H)


def swap_table():
    table = np.zeros((GROUP, GROUP))
    for mode in range(2):
        for c in range(BS):
            real = mode * 2 * BS + c
            table[real + BS, real] = 1
            table[real, real + BS] = -1
    return table.astype(ml_dtypes.bfloat16)


def dot(left, right):
    return lax.dot_general(left, right, (((1,), (0,)), ((), ())), preferred_element_type=F32)


def dot_nt(left, right):
    return lax.dot_general(left, right, (((1,), (1,)), ((), ())), preferred_element_type=F32)


def dot_tn(left, right):
    return lax.dot_general(left, right, (((0,), (0,)), ((), ())), preferred_element_type=F32)


def split(values):
    high = values.astype(BF16)
    return high, (values - high.astype(F32)).astype(BF16)


def dot3(kind, left, right):
    return kind(left[0], right[0]) + kind(left[1], right[0]) + kind(left[0], right[1])


def gelu_parts(values):
    cdf = 0.5 * (1.0 + lax.erf(values * 0.7071067811865476))
    return values * cdf, cdf + values * 0.3989422804014327 * jnp.exp(-0.5 * values * values)


def gelu_value(values):
    return 0.5 * values * (1.0 + lax.erf(values * 0.7071067811865476))


def norm_rows(stats):
    total = stats[0]
    for e in range(1, N_CH):
        total = total + stats[e]
    average = total[0:8] * (1.0 / C)
    squares = total[8:16] * (1.0 / C)
    return average, lax.rsqrt(squares - average * average + EPSILON)


def put_row(scratch, row, modes):
    wide = jnp.concatenate([modes[32 * k : 32 * k + 32] for k in range(PLANES)], axis=1)
    for t in range(LANES // 128):
        scratch[t, pl.ds(row, N_LAT, stride=8), :] = wide[:, 128 * t : 128 * t + 128]


def flush_rows(scratch, wire):
    for t in range(LANES // 128):
        scratch[t, pl.ds(ROWS, N_LAT, stride=8), :] = jnp.zeros((N_LAT, 128), F32)
        wire[:, 128 * t : 128 * t + 128] = scratch[t].astype(BF16)


def load_rows(wire, scratch):
    for t in range(LANES // 128):
        scratch[t] = wire[:, 128 * t : 128 * t + 128].astype(F32)


def load_packed(wire, scratch):
    for t in range(LANES // 128):
        block = wire[:, :, 128 * t : 128 * t + 128].astype(F32)
        scratch[t] = block[:, :8].reshape(8 * N_LAT, 128)


def get_row(scratch, row):
    wide = jnp.concatenate(
        [scratch[t, pl.ds(row, N_LAT, stride=8), :] for t in range(LANES // 128)], axis=1
    )
    return jnp.concatenate([wide[:, BS * k : BS * k + BS] for k in range(PLANES)], axis=0)


def to_chunk(rows, e):
    return jnp.concatenate(
        [
            jnp.concatenate(
                [values[48 * e + 8 * a : 48 * e + 8 * a + 8] for a in range(6)], axis=1
            )
            for values in rows
        ],
        axis=0,
    )


def from_chunks(chunks, row):
    return jnp.concatenate(
        [
            chunk[8 * row : 8 * row + 8, BS * a : BS * a + BS]
            for chunk in chunks
            for a in range(6)
        ],
        axis=0,
    )


def cot_kernel(place, cot, *refs):
    chunks, scratch = refs[:N_CH], refs[N_CH]
    for r in range(ROWS):
        scratch[r] = cot[r].astype(F32).T
    for k in range(N_CH):
        cells = pl.ds(pl.multiple_of(48 * (place[1] ^ k), 8), 48)
        chunks[k][...] = to_chunk([scratch[r, cells] for r in range(ROWS)], 0).astype(BF16)


def lon_kernel(x, stats, gain, t_high, t_low, wire, scratch):
    average, inv_std = norm_rows(stats)
    table = (t_high[...], t_low[...])
    for r in range(ROWS):
        normed = (x[r].astype(F32) - average[r : r + 1]) * inv_std[r : r + 1]
        lifted = split(normed * gain[...])
        put_row(scratch, r, dot3(dot_nt, table, lifted))
    flush_rows(scratch, wire)


def lat_forward(wire, lf_high, lf_low, swap):
    values = wire[...]
    swapped = dot(values, swap[...]).astype(BF16)
    both = jnp.concatenate([values, swapped], axis=0)
    return dot(lf_high[...], both) + dot(lf_low[...], both)


def lat_inverse(modes, li_high, li_low):
    both = split(jnp.concatenate([modes[:, :GROUP], modes[:, GROUP:]], axis=0))
    return dot3(dot, (li_high[...], li_low[...]), both)


def weight_sum(blocks):
    def block(part, other):
        pieces = [
            blocks[m + BS * part : m + BS * part + BS, m + BS * other : m + BS * other + BS]
            for m in (0, 2 * BS)
        ]
        return pieces[0] + pieces[1]

    return jnp.concatenate(
        [block(0, 0) + block(1, 1), block(1, 0) - block(0, 1)], axis=0
    )


def spectral_kernel(
    wire, lf_high, lf_low, swap, m1_high, m1_low, m2_high, m2_low, doubled, li_high, li_low,
    out, spectrum, pre_modes,
):
    modes = lat_forward(wire, lf_high, lf_low, swap)
    spectrum[...] = modes
    pre = dot3(dot, split(modes), (m1_high[...], m1_low[...]))
    pre_modes[...] = pre
    act = split(gelu_value(pre))
    scale = doubled[...]
    result = dot3(dot, act, (m2_high[...], m2_low[...])) * jnp.concatenate([scale, scale], axis=1)
    out[...] = lat_inverse(result, li_high, li_low).astype(BF16)


def spectral_back_kernel(
    wire, spectrum, pre_modes, lf_high, lf_low, swap, m1_high, m1_low, m2_high, m2_low, doubled,
    li_high, li_low, gain, gain_parts, out, small, grad_outer, grad_inner, gain_sum,
):
    @pl.when(pl.program_id(0) == 0)
    def _():
        grad_outer[...] = jnp.zeros_like(grad_outer)
        grad_inner[...] = jnp.zeros_like(grad_inner)
        gain_sum[...] = jnp.zeros_like(gain_sum)

    grad = split(lat_forward(wire, lf_high, lf_low, swap) * doubled[...])
    act, slope = gelu_parts(pre_modes[...])
    grad_act = dot3(dot_nt, grad, (m2_high[:, :GROUP], m2_low[:, :GROUP]))
    grad_outer[...] += dot3(dot_tn, grad, split(act))
    grad_pre = split(grad_act * slope)
    modes = spectrum[...]
    grad_inner[...] += dot3(dot_tn, grad_pre, split(modes))
    grad_spectrum = dot3(dot_nt, grad_pre, (m1_high[...], m1_low[...]))
    gain_row = jnp.sum(grad_spectrum[:, :GROUP] * modes, axis=0, keepdims=True)
    gain_row = sum(gain_row[:, BS * k : BS * k + BS] for k in range(4))
    gain_sum[0:1, :BS] += gain_row
    out[...] = lat_inverse(grad_spectrum, li_high, li_low).astype(BF16)

    @pl.when(pl.program_id(0) == 2)
    def _():
        first = gain_sum[0:1, :BS] / gain[...] + gain_parts[0:1, :BS]
        weights = [weight_sum(grad_inner[...]), weight_sum(grad_outer[...])]
        small[:N_LAT] = jnp.concatenate(
            [weight[32 * q : 32 * q + 32] for weight in weights for q in range(6)], axis=1
        )
        row = []
        for values in (first, gain_parts[1:2, :BS]):
            high = values.astype(BF16).astype(F32)
            row += [high, values - high]
        row = jnp.concatenate(row + [jnp.zeros((1, 8 * BS), F32)], axis=1)
        small[N_LAT:] = jnp.concatenate([row, jnp.zeros((7, LANES), F32)], axis=0)


def mix_kernel(wire, tt_high, tt_low, x, stats, gain, mixed, chunks, scratch):
    average, inv_std = norm_rows(stats)
    load_rows(wire, scratch)
    rows = []
    for r in range(ROWS):
        x_float = x[r].astype(F32)
        lifted = (x_float - average[r : r + 1]) * inv_std[r : r + 1] * gain[...]
        modes = get_row(scratch, r).astype(BF16)
        filtered = dot(tt_high[...], modes) + dot(tt_low[...], modes)
        values = filtered + (lifted + x_float).T
        mixed[r] = values
        rows.append(values)
    for e in range(N_CH):
        chunks[e] = to_chunk(rows, e)


def mlp_kernel(core, mixed, gain, *refs):
    given_cots, weights, refs = refs[:8], refs[8:20], refs[20:]
    out_chunks, refs = refs[:8], refs[8:]
    grad_chunks, grad_in_own, grad_in_other, grad_out_own, grad_out_other = refs[:5]
    (
        normed, inputs, cots, inv_std, sum_out, sum_grad, weight_in, weight_out, chunk_rows, arrived,
    ) = refs[5:]
    step = pl.program_id(0)
    turn = 4 * core[0]
    cells = 6 * 8 * ROWS
    part = 8 * ROWS

    def gain_row():
        return jnp.concatenate([gain[e ^ turn] for e in range(N_CH)], axis=1)

    def copies(p):
        found = []
        for half in range(2):
            parts = weights[6 * half : 6 * half + 6]
            rows = pl.ds(384 * half, 384)
            for b in range(2):
                units = pl.ds(384 * b, 384)
                found.append((parts[p].at[b], weight_in.at[p, rows, units]))
                found.append((parts[4 + b].at[p], weight_out.at[p, units, rows]))
        return [
            pltpu.make_async_copy(source, target, arrived.at[8 * p + n])
            for n, (source, target) in enumerate(found)
        ]

    @pl.when(step == 0)
    def _():
        for p in range(4):
            for copy in copies(p):
                copy.start()
        pieces = [mixed[e ^ turn] for e in range(N_CH)]
        values = jnp.concatenate(
            [
                jnp.concatenate([piece[:, BS * a : BS * a + BS] for piece in pieces], axis=1)
                for a in range(6)
            ],
            axis=0,
        )
        average = jnp.sum(values, axis=1, keepdims=True) * (1.0 / C)
        squares = jnp.sum(values * values, axis=1, keepdims=True) * (1.0 / C)
        inv = lax.rsqrt(squares - average * average + EPSILON)
        values = (values - average) * inv
        normed[...] = values
        inv_std[...] = jnp.broadcast_to(inv, (cells, 128))
        inputs[...] = (values * gain_row()).astype(BF16)
        for k in range(N_CH):
            chunk_rows[k] = given_cots[k][...].astype(F32)
        pieces = [chunk_rows[e ^ turn ^ core[1]] for e in range(N_CH)]
        cots[...] = jnp.concatenate(
            [
                jnp.concatenate([piece[:, BS * a : BS * a + BS] for piece in pieces], axis=1)
                for a in range(6)
            ],
            axis=0,
        ).astype(BF16)
        sum_out[...] = jnp.zeros_like(sum_out)
        sum_grad[...] = jnp.zeros_like(sum_grad)

    for p in range(4):

        @pl.when(step == p)
        def _():
            for copy in copies(p):
                copy.wait()

    own_in, own_out = weight_in[step], weight_out[step]
    values, given = inputs[...], cots[...]
    hidden, slope = gelu_parts(dot(values, own_in))
    hidden = hidden.astype(BF16)
    grad_pre = (dot_nt(given, own_out) * slope).astype(BF16)
    sum_out[...] += dot(hidden, own_out)
    sum_grad[...] += dot_nt(grad_pre, own_in)
    grad_in = dot_tn(values, grad_pre)
    grad_out = dot_tn(hidden, given)
    for b in range(2):
        units = slice(384 * b, 384 * b + 384)
        grad_in_own[b, 0] = grad_in[:384, units]
        grad_in_other[b, 0] = grad_in[384:, units].astype(BF16)
        grad_out_own[b] = grad_out[units, :384]
        grad_out_other[b] = grad_out[units, 384:].astype(BF16)

    @pl.when(step == 3)
    def _():
        grad_input = sum_grad[...]
        values = normed[...]
        gain_sum = jnp.sum(grad_input * values, axis=0, keepdims=True)
        scaled = grad_input * gain_row()
        leading = jnp.sum(scaled, axis=1, keepdims=True) * (1.0 / C)
        paired = jnp.sum(scaled * values, axis=1, keepdims=True) * (1.0 / C)
        grad_mixed = cots[...].astype(F32) + inv_std[:, :1] * (scaled - leading - values * paired)
        outputs = sum_out[...]

        def chunk(array, e):
            return jnp.concatenate(
                [array[part * a : part * a + part, BS * e : BS * e + BS] for a in range(6)],
                axis=1,
            )

        for e in range(N_CH):
            chunk_rows[e ^ turn ^ core[1]] = chunk(outputs, e)
            gain_piece = gain_sum[:, BS * e : BS * e + BS]
            gain_high = gain_piece.astype(BF16).astype(F32)
            extra = jnp.concatenate(
                [gain_high, gain_piece - gain_high, jnp.zeros((1, 4 * BS), F32)], axis=1
            )
            extra = jnp.concatenate([extra, jnp.zeros((7, 6 * BS), F32)], axis=0)
            grad_chunks[e ^ turn] = jnp.concatenate(
                [chunk(grad_mixed, e), extra], axis=0
            ).astype(BF16)
        for k in range(N_CH):
            out_chunks[k][...] = chunk_rows[k].astype(BF16)


def lon_back_kernel(chunks, x, stats, t_high, t_low, wire, grad_mixed, gains, scratch):
    average, inv_std = norm_rows(stats)
    pieces = [chunks[e].astype(F32) for e in range(N_CH)]
    gain_first = jnp.zeros((BS, 1), F32)
    for r in range(ROWS):
        values = from_chunks(pieces, r)
        rounded = values.astype(BF16)
        put_row(scratch, r, dot(t_high[...], rounded) + dot(t_low[...], rounded))
        turned = values.T
        grad_mixed[r] = turned.astype(BF16)
        normed = (x[r].astype(F32) - average[r : r + 1]) * inv_std[r : r + 1]
        gain_first = gain_first + jnp.sum(turned * normed, axis=1, keepdims=True)
    flush_rows(scratch, wire)
    gain_second = jnp.zeros((1, BS), F32)
    for piece in pieces:
        row = piece[8 * ROWS : 8 * ROWS + 1]
        gain_second = gain_second + row[:, :BS] + row[:, BS : 2 * BS]
    turned_first = jnp.broadcast_to(gain_first, (BS, 128)).T[0:1, :]
    gains[0:1, :BS] = turned_first
    gains[1:2, :BS] = gain_second


def unmix_kernel(wire, tt_high, tt_low, grad_mixed, x, stats, gain, scaled, sums, scratch):
    average, inv_std = norm_rows(stats)
    load_packed(wire, scratch)
    for r in range(ROWS):
        modes = get_row(scratch, r).astype(BF16)
        back = dot(tt_high[...], modes) + dot(tt_low[...], modes)
        values = (back.T + grad_mixed[r].astype(F32)) * gain[...]
        normed = (x[r].astype(F32) - average[r : r + 1]) * inv_std[r : r + 1]
        scaled[r] = values
        sums[r : r + 1] = jnp.sum(values, axis=0, keepdims=True)
        sums[8 + r : 9 + r] = jnp.sum(values * normed, axis=0, keepdims=True)
    sums[7:8] = jnp.zeros((1, W), F32)
    sums[15:16] = jnp.zeros((1, W), F32)


def final_kernel(scaled, grad_mixed, x, stats, *rest):
    average, inv_std = norm_rows(stats)
    out = rest[-1]
    total = rest[0][...]
    for part in rest[1:-1]:
        total = total + part[...]
    total = total * (1.0 / C)
    for r in range(ROWS):
        inv = inv_std[r : r + 1]
        normed = (x[r].astype(F32) - average[r : r + 1]) * inv
        change = scaled[r] - total[r : r + 1] - normed * total[8 + r : 9 + r]
        out[r] = (grad_mixed[r].astype(F32) + inv * change).astype(BF16)


def pack_kernel(wire, small, in_0, in_2, in_4, in_6, out_0, out_1, out):
    total_in = in_0[0] + in_2[...].astype(F32) + in_4[...].astype(F32) + in_6[...].astype(F32)
    total_out = out_0[0] + out_1[...].astype(F32)
    total = jnp.concatenate([total_in, total_out], axis=0)
    modes = wire[...].astype(F32).reshape(N_LAT, 8, LANES)
    weights = small[:N_LAT]
    row = lax.broadcasted_iota(jnp.int32, (N_LAT, 8, LANES), 1)
    modes = jnp.where(row == ROWS, weights[:, None, :], modes)
    grads = jnp.concatenate(
        [total[256 * g : 256 * g + 256].reshape(N_LAT, 8, GROUP) for g in range(3)], axis=2
    )
    out[...] = jnp.concatenate([modes, grads], axis=1).astype(BF16)


def spread_kernel(parts, small, out):
    sums = [parts[n].astype(F32) for n in (0, 1)]
    for n in range(2, N_LAT):
        sums[n % 2] = sums[n % 2] + parts[n].astype(F32)
    rows = [
        half[8:16, GROUP * g : GROUP * g + GROUP] for half in sums for g in range(3)
    ]
    weights = sums[0][ROWS : ROWS + 1] + sums[1][ROWS : ROWS + 1]
    last = [weights[:, GROUP * g : GROUP * g + GROUP] for g in range(3)]
    last += [small[N_LAT : N_LAT + 1, :GROUP], jnp.zeros((4, GROUP), F32)]
    total = jnp.concatenate(rows + [jnp.concatenate(last, axis=0)], axis=0).astype(BF16)
    for n in range(N_LAT // 2):
        out[n] = total


def finish_kernel(
    place, mine, theirs, grad_in, grad_out, grad_inner, grad_outer, gain_first, gain_second
):
    first = place[0] == 0
    one, two = mine[...].astype(F32), theirs[...].astype(F32)
    even, odd = jnp.where(first, one, two), jnp.where(first, two, one)

    def rows(start):
        parts = [part[:, start : start + 8][:, None] for part in (even, odd)]
        return jnp.concatenate(parts, axis=1).reshape(256, GROUP)

    for half in range(2):
        total = jnp.concatenate([rows(24 * half + 8 * g) for g in range(3)], axis=0)
        grad_in[384 * half : 384 * half + 384] = total[:384]
        grad_out[:, 384 * half : 384 * half + 384] = total[384:]
    last = rows(48)
    planes = [
        jnp.concatenate([last[8 * n + g : 8 * n + g + 1] for n in range(N_LAT)], axis=0)
        for g in range(4)
    ]
    weights = [
        plane[:, BS * q : BS * q + BS] for plane in planes[:3] for q in range(4)
    ]
    for part in range(2):
        grad_inner[part, 0] = jnp.concatenate(weights[3 * part : 3 * part + 3], axis=0)
        grad_outer[part, 0] = jnp.concatenate(weights[6 + 3 * part : 9 + 3 * part], axis=0)
    gains = jnp.sum(planes[3], axis=0, keepdims=True)
    gain_first[...] = gains[:, :BS] + gains[:, BS : 2 * BS]
    gain_second[...] = gains[:, 2 * BS : 3 * BS] + gains[:, 3 * BS :]


def output_kernel(place, mixed, *refs):
    chunks, out, chunk_rows = refs[:N_CH], refs[N_CH], refs[N_CH + 1]
    for k in range(N_CH):
        chunk_rows[k] = chunks[k][...].astype(F32)
    pieces = [chunk_rows[e ^ place[1]] for e in range(N_CH)]
    for r in range(ROWS):
        out[r] = (from_chunks(pieces, r) + mixed[r]).T.astype(BF16)


def cost(micros):
    return pl.CostEstimate(
        flops=int(micros * 1.0e9), bytes_accessed=int(micros * 2.0e6), transcendentals=0
    )


def call(kernel, out_shape, *args, scratch=(), micros=3, place=None):
    specs = [pl.BlockSpec(memory_space=pltpu.VMEM)] * len(args)
    if place is not None:
        args = (place,) + args
        specs = [pl.BlockSpec(memory_space=pltpu.SMEM)] + specs
    return pl.pallas_call(
        kernel,
        out_shape=out_shape,
        in_specs=specs,
        scratch_shapes=scratch,
        compiler_params=pltpu.CompilerParams(vmem_limit_bytes=VMEM_BYTES),
        cost_estimate=cost(micros),
    )(*args)


def shaped(*shape, dtype=F32):
    return jax.ShapeDtypeStruct(shape, dtype)


def whole(shape):
    return pl.BlockSpec(shape, lambda g: (0,) * len(shape))


def lane_block(rows):
    return pl.BlockSpec((rows, GROUP), lambda g: (0, g))


def block_matrix(weight, swap_columns, swap_rows):
    real, imag = weight[0, 0].T, weight[1, 0].T
    base = [[real, imag], [-imag, real]]
    if swap_columns:
        base = [[imag, -real], [real, imag]]
    if swap_rows:
        base = [[-imag, real], [-real, -imag]]
    one = jnp.concatenate([jnp.concatenate(line, axis=1) for line in base], axis=0)
    zero = jnp.zeros_like(one)
    return jnp.concatenate(
        [jnp.concatenate([one, zero], axis=1), jnp.concatenate([zero, one], axis=1)], axis=0
    )


def to_all(values, axis, count, **kwargs):
    spread = jnp.broadcast_to(values[None], (count,) + values.shape)
    return lax.all_to_all(spread, axis, 0, 0, tiled=True, **kwargs)


def near(values, k):
    return lax.ppermute(values, "ch", [(i, i ^ k) for i in range(N_CH)])


def body(fields, gain_first, w_inner, w_outer, gain_second, fc_in, fc_out, cotangent):
    lat = lax.axis_index("lat")
    core = lat % 2
    me = lax.axis_index("ch")
    place = jnp.stack([core, me]).astype(jnp.int32)
    siblings = [(i, i ^ 1) for i in range(N_LAT)]
    cores = [list(range(0, N_LAT, 2)), list(range(1, N_LAT, 2))]
    t_high, t_low = (jnp.asarray(t) for t in halves(lon_table()))
    tt_high, tt_low = (jnp.asarray(t) for t in halves(lon_table().T))
    forward, inverse = lat_tables()
    lf_high, lf_low = (jnp.asarray(t) for t in halves(forward))
    li_high, li_low = (jnp.asarray(t) for t in halves(inverse))
    swap = jnp.asarray(swap_table())

    x = fields.transpose(1, 0, 2)
    cot = cotangent.transpose(1, 0, 2)
    gain_column = gain_first[:, None]

    with jax.named_scope("stats"):
        x_float = x.astype(F32)
        zero = jnp.zeros((1, W), F32)
        payload = jnp.concatenate(
            [
                jnp.sum(x_float, 1),
                zero,
                jnp.sum(x_float * x_float, 1),
                zero,
                jnp.pad(gain_second, (0, W - BS))[None],
                jnp.zeros((7, W), F32),
            ],
            axis=0,
        )
        gathered = to_all(payload, "ch", N_CH)
        gathered, fc_in, fc_out, cot = lax.optimization_barrier((gathered, fc_in, fc_out, cot))

    with jax.named_scope("weights"):
        half_in = lax.dynamic_slice_in_dim(fc_in, core * 384, 384, 0)
        half_out = lax.dynamic_slice_in_dim(fc_out, core * 384, 384, 1)
        near_in = near(half_in, 1)
        near_out = [near(half_out, k) for k in (2, 4, 6)]

    with jax.named_scope("cot"):
        chunk_shape = shaped(8 * ROWS, 6 * BS, dtype=BF16)
        first, *others = call(
            cot_kernel, [chunk_shape] * N_CH, cot, place=place,
            scratch=[pltpu.VMEM((ROWS, W, BS), F32)],
        )
        cot_chunks = [first] + [near(part, k + 1) for k, part in enumerate(others)]

    with jax.named_scope("stats"):
        stats = gathered[:, :16]
        gains = gathered[:, 16:17, :BS]

    scratch = pltpu.VMEM((LANES // 128, 8 * N_LAT, 128), F32)
    wire_shape = shaped(8 * N_LAT, LANES, dtype=BF16)
    with jax.named_scope("lon"):
        wire = call(
            lon_kernel, wire_shape, x, stats, gain_column, t_high, t_low, scratch=[scratch]
        )
        wire = lax.all_to_all(wire, "lat", 0, 0, tiled=True)

    with jax.named_scope("weights"):
        near_in, *near_out, wire = lax.optimization_barrier((near_in, *near_out, wire))
        *cot_chunks, wire = lax.optimization_barrier((*cot_chunks, wire))
        pair = jnp.stack([half_in, near_in])
        own_in = [pair] + [near(pair, k) for k in (2, 4, 6)]
        quad = jnp.stack([half_out] + near_out)
        own_out = [quad, near(quad, 1)]

    with jax.named_scope("matrices"):
        m1 = split(
            jnp.concatenate(
                [block_matrix(w_inner, False, False), block_matrix(w_inner, False, True)], axis=0
            )
        )
        m2 = split(
            jnp.concatenate(
                [block_matrix(w_outer, False, False), block_matrix(w_outer, True, False)], axis=1
            )
        )
        lane = jnp.arange(LANES, dtype=jnp.int32)[None]
        doubled = jnp.where((lat == 0) & (lane < 2 * BS), 1.0, 2.0).astype(F32)

    table_specs = [whole((H, 512)), whole((H, 512)), whole((GROUP, GROUP))]
    inverse_specs = [lane_block(1), whole((256, 448)), whole((256, 448))]
    params = pltpu.CompilerParams(vmem_limit_bytes=VMEM_BYTES)
    with jax.named_scope("spectral"):
        wire, spectrum, pre_modes = pl.pallas_call(
            spectral_kernel,
            grid=(3,),
            in_specs=[lane_block(256)]
            + table_specs
            + [whole((GROUP, GROUP))] * 2
            + [whole((GROUP, 2 * GROUP))] * 2
            + inverse_specs,
            out_specs=[lane_block(256), lane_block(H), lane_block(H)],
            out_shape=[wire_shape, shaped(H, LANES), shaped(H, LANES)],
            compiler_params=params,
            cost_estimate=cost(11),
        )(
            wire, lf_high, lf_low, swap, m1[0][:GROUP], m1[1][:GROUP], m2[0], m2[1], doubled,
            li_high, li_low,
        )
        wire = lax.all_to_all(wire, "lat", 0, 0, tiled=True)
        *weights, wire = lax.optimization_barrier((*own_in, *own_out, wire))
        weights += [lax.ppermute(part, "lat", siblings) for part in weights]

    with jax.named_scope("mix"):
        mixed, chunks = call(
            mix_kernel,
            [shaped(ROWS, W, BS), shaped(N_CH, 8 * ROWS, 6 * BS)],
            wire, tt_high, tt_low, x, stats, gain_column,
            scratch=[scratch],
        )
        chunks = lax.all_to_all(chunks, "ch", 0, 0, tiled=True)

    cells = 48 * ROWS
    halved = pl.BlockSpec((2, 1, 384, 384), lambda p, place: (0, p, 0, 0))
    direct = pl.BlockSpec((2, 384, 384), lambda p, place: (p, 0, 0))

    def all_of(shape):
        return pl.BlockSpec(shape, lambda e, place: (0,) * len(shape))

    with jax.named_scope("mlp"):
        *out_chunks, grad_chunks, in_own, in_other, out_own, out_other = pl.pallas_call(
            mlp_kernel,
            grid_spec=pltpu.PrefetchScalarGridSpec(
                num_scalar_prefetch=1,
                grid=(4,),
                in_specs=[
                    all_of((N_CH, 8 * ROWS, 6 * BS)),
                    all_of((N_CH, 1, BS)),
                ]
                + [all_of((8 * ROWS, 6 * BS))] * N_CH
                + [pl.BlockSpec(memory_space=pl.ANY)] * 12,
                out_specs=[all_of((8 * ROWS, 6 * BS))] * N_CH
                + [
                    all_of((N_CH, 8 * ROWS + 8, 6 * BS)),
                    halved,
                    halved,
                    direct,
                    direct,
                ],
                scratch_shapes=[
                    pltpu.VMEM((cells, C), F32),
                    pltpu.VMEM((cells, C), BF16),
                    pltpu.VMEM((cells, C), BF16),
                    pltpu.VMEM((cells, 128), F32),
                    pltpu.VMEM((cells, C), F32),
                    pltpu.VMEM((cells, C), F32),
                    pltpu.VMEM((4, C, C), BF16),
                    pltpu.VMEM((4, C, C), BF16),
                    pltpu.VMEM((N_CH, 8 * ROWS, 6 * BS), F32),
                    pltpu.SemaphoreType.DMA((32,)),
                ],
            ),
            out_shape=[chunk_shape] * N_CH
            + [
                shaped(N_CH, 8 * ROWS + 8, 6 * BS, dtype=BF16),
                shaped(2, 4, 384, 384),
                shaped(2, 4, 384, 384, dtype=BF16),
                shaped(N_CH, 384, 384),
                shaped(N_CH, 384, 384, dtype=BF16),
            ],
            compiler_params=params,
            cost_estimate=cost(20),
        )(place, chunks, gains, *cot_chunks, *weights)
        grad_chunks = lax.all_to_all(grad_chunks, "ch", 0, 0, tiled=True)

    with jax.named_scope("grads_ch"):
        theirs_in = lax.ppermute(in_other, "lat", siblings)
        theirs_out = lax.ppermute(out_other, "lat", siblings)
        odd = (in_own[1] + theirs_in[1].astype(F32)).astype(BF16)
        pairs = [
            (out_own[k : k + 2] + theirs_out[k : k + 2].astype(F32)).astype(BF16)
            for k in (2, 4, 6)
        ]
        odd, *pairs, grad_chunks = lax.optimization_barrier((odd, *pairs, grad_chunks))
        odd = near(odd, 1)
        pairs = [near(part, k) for part, k in zip(pairs, (2, 4, 6))]

    with jax.named_scope("lon_back"):
        wire, grad_mixed, gain_parts = call(
            lon_back_kernel,
            [wire_shape, shaped(ROWS, BS, W, dtype=BF16), shaped(8, 128)],
            grad_chunks, x, stats, t_high, t_low,
            scratch=[scratch],
        )
        wire = lax.all_to_all(wire, "lat", 0, 0, tiled=True)

    with jax.named_scope("grads_ch"):
        even = in_own[0] + theirs_in[0].astype(F32)
        pair = out_own[:2] + theirs_out[:2].astype(F32)
        odd, even, pair, *pairs, wire = lax.optimization_barrier((odd, even, pair, *pairs, wire))
        even = even + odd.astype(F32)
        for part in pairs:
            pair = pair + part.astype(F32)
        in_parts = [even] + [near(even[k // 2].astype(BF16), k) for k in (2, 4, 6)]
        out_parts = [pair, near(pair[1].astype(BF16), 1)]

    with jax.named_scope("spectral_back"):
        wire, small = pl.pallas_call(
            spectral_back_kernel,
            grid=(3,),
            in_specs=[lane_block(256), lane_block(H), lane_block(H)]
            + table_specs
            + [whole((2 * GROUP, GROUP))] * 2
            + [whole((GROUP, 2 * GROUP))] * 2
            + inverse_specs
            + [whole((1, BS)), whole((8, 128))],
            out_specs=[lane_block(256), whole((N_LAT + 8, LANES))],
            out_shape=[wire_shape, shaped(N_LAT + 8, LANES)],
            scratch_shapes=[
                pltpu.VMEM((GROUP, GROUP), F32),
                pltpu.VMEM((GROUP, GROUP), F32),
                pltpu.VMEM((8, 128), F32),
            ],
            compiler_params=params,
            cost_estimate=cost(14),
        )(
            wire, spectrum, pre_modes, lf_high, lf_low, swap, m1[0], m1[1], m2[0], m2[1], doubled,
            li_high, li_low, gain_first[None], gain_parts,
        )
        *grad_parts, wire = lax.optimization_barrier((*in_parts, *out_parts, wire))

    with jax.named_scope("pack"):
        corner = pl.BlockSpec((1, 384, 384), lambda g: (0, 0, 0))
        flat = whole((384, 384))
        wire = pl.pallas_call(
            pack_kernel,
            grid=(1,),
            in_specs=[whole((256, LANES)), whole((N_LAT + 8, LANES)), corner, flat, flat, flat]
            + [corner, flat],
            out_specs=whole((N_LAT, 16, LANES)),
            out_shape=shaped(N_LAT, 16, LANES, dtype=BF16),
            compiler_params=params,
            cost_estimate=cost(3),
        )(wire, small, *grad_parts)
        *out_chunks, wire = lax.optimization_barrier((*out_chunks, wire))
        wire = lax.all_to_all(wire, "lat", 0, 0, tiled=True)

    with jax.named_scope("output"):
        first, *others = out_chunks
        out_chunks = [first] + [near(part, k + 1) for k, part in enumerate(others)]
        output = call(
            output_kernel, shaped(ROWS, BS, W, dtype=BF16), mixed, *out_chunks, place=place,
            scratch=[pltpu.VMEM((N_CH, 8 * ROWS, 6 * BS), F32)],
        )
        output, wire = lax.optimization_barrier((output, wire))

    with jax.named_scope("unmix"):
        scaled, sums = call(
            unmix_kernel,
            [shaped(ROWS, BS, W), shaped(16, W)],
            wire, tt_high, tt_low, grad_mixed, x, stats, gain_column,
            scratch=[scratch],
        )
    with jax.named_scope("sums"):
        sums = [sums] + [near(sums, k) for k in range(1, N_CH)]

    with jax.named_scope("grads_lat"):
        payload = call(spread_kernel, shaped(N_LAT // 2, 56, GROUP, dtype=BF16), wire, small)
        mine = lax.all_to_all(payload, "lat", 0, 0, tiled=True, axis_index_groups=cores)
        mine, *sums = lax.optimization_barrier((mine, *sums))
        theirs = lax.ppermute(mine, "lat", siblings)
        weight_shape = shaped(2, 1, BS, BS)
        grad_fc_in, grad_fc_out, grad_w_inner, grad_w_outer, grad_first, grad_second = call(
            finish_kernel,
            [
                shaped(C, FF_DEV),
                shaped(FF_DEV, C),
                weight_shape,
                weight_shape,
                shaped(1, BS),
                shaped(1, BS),
            ],
            mine, theirs, place=place,
        )

    with jax.named_scope("final"):
        grad_fields = call(
            final_kernel, shaped(ROWS, BS, W, dtype=BF16), scaled, grad_mixed, x, stats, *sums
        )

    return (
        output.transpose(1, 0, 2),
        grad_fields.transpose(1, 0, 2),
        grad_first[0],
        grad_w_inner,
        grad_w_outer,
        grad_second[0],
        grad_fc_in,
        grad_fc_out,
    )


def solution(mesh):
    placed = (
        P("ch", "lat", None),
        P("ch"),
        P(None, "ch", None, None),
        P(None, "ch", None, None),
        P("ch"),
        P(None, "ch"),
        P("ch", None),
        P("ch", "lat", None),
    )
    return jax.shard_map(
        body,
        mesh=mesh,
        in_specs=placed,
        out_specs=(
            P("ch", "lat", None),
            P("ch", "lat", None),
            P("ch"),
            P(None, "ch", None, None),
            P(None, "ch", None, None),
            P("ch"),
            P(None, "ch"),
            P("ch", None),
        ),
        check_vma=False,
    )
```

```python
import math

import jax
import jax.numpy as jnp
import ml_dtypes
import numpy as np
from jax import lax
from jax.experimental import pallas as pl
from jax.experimental.pallas import tpu as pltpu
from jax.sharding import PartitionSpec as P

C = 768
BS = 96
H = 224
W = 384
KW = 192
N_LAT = 32
N_CH = 8
ROWS = 7
FF_DEV = 384
MODES = KW // N_LAT
PLANES = 2 * MODES
LANES = PLANES * BS
GROUP = 384
EPSILON = 1e-05
BF16 = jnp.bfloat16
F32 = jnp.float32
VMEM_BYTES = 56 * 1024 * 1024


def halves(table):
    high = table.astype(ml_dtypes.bfloat16)
    low = (table - high.astype(np.float64)).astype(ml_dtypes.bfloat16)
    return high, low


def lon_table():
    mode = np.arange(MODES)[:, None] + MODES * np.arange(N_LAT)[None, :]
    angles = 2 * np.pi * ((mode[:, :, None] * np.arange(W)) % W) / W
    table = np.stack([np.cos(angles), -np.sin(angles)], 1) / math.sqrt(W)
    return table.reshape(PLANES * N_LAT, W)


def lat_tables():
    index = np.arange(H)
    angles = 2 * np.pi * ((index[:, None] * index[None, :]) % H) / H
    cosine = np.cos(angles) / math.sqrt(H)
    sine = np.sin(angles) / math.sqrt(H)
    forward = np.zeros((H, 2, N_LAT, 8))
    forward[:, 0, :, :ROWS] = cosine.reshape(H, N_LAT, ROWS)
    forward[:, 1, :, :ROWS] = sine.reshape(H, N_LAT, ROWS)
    inverse = np.zeros((N_LAT, 8, 2, H))
    inverse[:, :ROWS, 0] = cosine.reshape(N_LAT, ROWS, H)
    inverse[:, :ROWS, 1] = -sine.reshape(N_LAT, ROWS, H)
    return forward.reshape(H, 2 * N_LAT * 8), inverse.reshape(N_LAT * 8, 2 * H)


def swap_table():
    table = np.zeros((GROUP, GROUP))
    for mode in range(2):
        for c in range(BS):
            real = mode * 2 * BS + c
            table[real + BS, real] = 1
            table[real, real + BS] = -1
    return table.astype(ml_dtypes.bfloat16)


def dot(left, right):
    return lax.dot_general(left, right, (((1,), (0,)), ((), ())), preferred_element_type=F32)


def dot_nt(left, right):
    return lax.dot_general(left, right, (((1,), (1,)), ((), ())), preferred_element_type=F32)


def dot_tn(left, right):
    return lax.dot_general(left, right, (((0,), (0,)), ((), ())), preferred_element_type=F32)


def split(values):
    high = values.astype(BF16)
    return high, (values - high.astype(F32)).astype(BF16)


def dot3(kind, left, right):
    return kind(left[0], right[0]) + kind(left[1], right[0]) + kind(left[0], right[1])


def gelu_parts(values):
    cdf = 0.5 * (1.0 + lax.erf(values * 0.7071067811865476))
    return values * cdf, cdf + values * 0.3989422804014327 * jnp.exp(-0.5 * values * values)


def gelu_value(values):
    return 0.5 * values * (1.0 + lax.erf(values * 0.7071067811865476))


def norm_rows(stats):
    total = stats[0]
    for e in range(1, N_CH):
        total = total + stats[e]
    average = total[0:8] * (1.0 / C)
    squares = total[8:16] * (1.0 / C)
    return average, lax.rsqrt(squares - average * average + EPSILON)


def put_row(scratch, row, modes):
    wide = jnp.concatenate([modes[32 * k : 32 * k + 32] for k in range(PLANES)], axis=1)
    for t in range(LANES // 128):
        scratch[t, pl.ds(row, N_LAT, stride=8), :] = wide[:, 128 * t : 128 * t + 128]


def flush_rows(scratch, wire):
    for t in range(LANES // 128):
        scratch[t, pl.ds(ROWS, N_LAT, stride=8), :] = jnp.zeros((N_LAT, 128), F32)
        wire[:, 128 * t : 128 * t + 128] = scratch[t].astype(BF16)


def load_rows(wire, scratch):
    for t in range(LANES // 128):
        scratch[t] = wire[:, 128 * t : 128 * t + 128].astype(F32)


def load_packed(wire, scratch):
    for t in range(LANES // 128):
        block = wire[:, :, 128 * t : 128 * t + 128].astype(F32)
        scratch[t] = block[:, :8].reshape(8 * N_LAT, 128)


def get_row(scratch, row):
    wide = jnp.concatenate(
        [scratch[t, pl.ds(row, N_LAT, stride=8), :] for t in range(LANES // 128)], axis=1
    )
    return jnp.concatenate([wide[:, BS * k : BS * k + BS] for k in range(PLANES)], axis=0)


def to_chunk(rows, e):
    return jnp.concatenate(
        [
            jnp.concatenate(
                [values[48 * e + 8 * a : 48 * e + 8 * a + 8] for a in range(6)], axis=1
            )
            for values in rows
        ],
        axis=0,
    )


def from_chunks(chunks, row):
    return jnp.concatenate(
        [
            chunk[8 * row : 8 * row + 8, BS * a : BS * a + BS]
            for chunk in chunks
            for a in range(6)
        ],
        axis=0,
    )


def cot_kernel(place, cot, *refs):
    chunks, scratch = refs[:N_CH], refs[N_CH]
    for r in range(ROWS):
        scratch[r] = cot[r].astype(F32).T
    for k in range(N_CH):
        cells = pl.ds(pl.multiple_of(48 * (place[1] ^ k), 8), 48)
        chunks[k][...] = to_chunk([scratch[r, cells] for r in range(ROWS)], 0).astype(BF16)


def lon_kernel(x, stats, gain, t_high, t_low, wire, scratch):
    average, inv_std = norm_rows(stats)
    table = (t_high[...], t_low[...])
    for r in range(ROWS):
        normed = (x[r].astype(F32) - average[r : r + 1]) * inv_std[r : r + 1]
        lifted = split(normed * gain[...])
        put_row(scratch, r, dot3(dot_nt, table, lifted))
    flush_rows(scratch, wire)


def lat_forward(wire, lf_high, lf_low, swap):
    values = wire[...]
    swapped = dot(values, swap[...]).astype(BF16)
    both = jnp.concatenate([values, swapped], axis=0)
    return dot(lf_high[...], both) + dot(lf_low[...], both)


def lat_inverse(modes, li_high, li_low):
    both = split(jnp.concatenate([modes[:, :GROUP], modes[:, GROUP:]], axis=0))
    return dot3(dot, (li_high[...], li_low[...]), both)


def weight_sum(blocks):
    def block(part, other):
        pieces = [
            blocks[m + BS * part : m + BS * part + BS, m + BS * other : m + BS * other + BS]
            for m in (0, 2 * BS)
        ]
        return pieces[0] + pieces[1]

    return jnp.concatenate(
        [block(0, 0) + block(1, 1), block(1, 0) - block(0, 1)], axis=0
    )


def spectral_kernel(
    wire, lf_high, lf_low, swap, m1_high, m1_low, m2_high, m2_low, doubled, li_high, li_low,
    out, spectrum, pre_modes,
):
    modes = lat_forward(wire, lf_high, lf_low, swap)
    spectrum[...] = modes
    pre = dot3(dot, split(modes), (m1_high[...], m1_low[...]))
    pre_modes[...] = pre
    act = split(gelu_value(pre))
    scale = doubled[...]
    result = dot3(dot, act, (m2_high[...], m2_low[...])) * jnp.concatenate([scale, scale], axis=1)
    out[...] = lat_inverse(result, li_high, li_low).astype(BF16)


def spectral_back_kernel(
    wire, spectrum, pre_modes, lf_high, lf_low, swap, m1_high, m1_low, m2_high, m2_low, doubled,
    li_high, li_low, gain, gain_parts, out, small, grad_outer, grad_inner, gain_sum,
):
    @pl.when(pl.program_id(0) == 0)
    def _():
        grad_outer[...] = jnp.zeros_like(grad_outer)
        grad_inner[...] = jnp.zeros_like(grad_inner)
        gain_sum[...] = jnp.zeros_like(gain_sum)

    grad = split(lat_forward(wire, lf_high, lf_low, swap) * doubled[...])
    act, slope = gelu_parts(pre_modes[...])
    grad_act = dot3(dot_nt, grad, (m2_high[:, :GROUP], m2_low[:, :GROUP]))
    grad_outer[...] += dot3(dot_tn, grad, split(act))
    grad_pre = split(grad_act * slope)
    modes = spectrum[...]
    grad_inner[...] += dot3(dot_tn, grad_pre, split(modes))
    grad_spectrum = dot3(dot_nt, grad_pre, (m1_high[...], m1_low[...]))
    gain_row = jnp.sum(grad_spectrum[:, :GROUP] * modes, axis=0, keepdims=True)
    gain_row = sum(gain_row[:, BS * k : BS * k + BS] for k in range(4))
    gain_sum[0:1, :BS] += gain_row
    out[...] = lat_inverse(grad_spectrum, li_high, li_low).astype(BF16)

    @pl.when(pl.program_id(0) == 2)
    def _():
        first = gain_sum[0:1, :BS] / gain[...] + gain_parts[0:1, :BS]
        weights = [weight_sum(grad_inner[...]), weight_sum(grad_outer[...])]
        small[:N_LAT] = jnp.concatenate(
            [weight[32 * q : 32 * q + 32] for weight in weights for q in range(6)], axis=1
        )
        row = []
        for values in (first, gain_parts[1:2, :BS]):
            high = values.astype(BF16).astype(F32)
            row += [high, values - high]
        row = jnp.concatenate(row + [jnp.zeros((1, 8 * BS), F32)], axis=1)
        small[N_LAT:] = jnp.concatenate([row, jnp.zeros((7, LANES), F32)], axis=0)


def mix_kernel(wire, tt_high, tt_low, x, stats, gain, mixed, chunks, scratch):
    average, inv_std = norm_rows(stats)
    load_rows(wire, scratch)
    rows = []
    for r in range(ROWS):
        x_float = x[r].astype(F32)
        lifted = (x_float - average[r : r + 1]) * inv_std[r : r + 1] * gain[...]
        modes = get_row(scratch, r).astype(BF16)
        filtered = dot(tt_high[...], modes) + dot(tt_low[...], modes)
        values = filtered + (lifted + x_float).T
        mixed[r] = values
        rows.append(values)
    for e in range(N_CH):
        chunks[e] = to_chunk(rows, e)


def mlp_kernel(core, mixed, gain, *refs):
    given_cots, weights, refs = refs[:8], refs[8:20], refs[20:]
    out_chunks, refs = refs[:8], refs[8:]
    grad_chunks, grad_in_own, grad_in_other, grad_out_own, grad_out_other = refs[:5]
    (
        normed, inputs, cots, inv_std, sum_out, sum_grad, weight_in, weight_out, chunk_rows, arrived,
    ) = refs[5:]
    step = pl.program_id(0)
    turn = 4 * core[0]
    cells = 6 * 8 * ROWS
    part = 8 * ROWS

    def gain_row():
        return jnp.concatenate([gain[e ^ turn] for e in range(N_CH)], axis=1)

    def copies(p):
        found = []
        for half in range(2):
            parts = weights[6 * half : 6 * half + 6]
            rows = pl.ds(384 * half, 384)
            for b in range(2):
                units = pl.ds(384 * b, 384)
                found.append((parts[p].at[b], weight_in.at[p, rows, units]))
                found.append((parts[4 + b].at[p], weight_out.at[p, units, rows]))
        return [
            pltpu.make_async_copy(source, target, arrived.at[8 * p + n])
            for n, (source, target) in enumerate(found)
        ]

    @pl.when(step == 0)
    def _():
        for p in range(4):
            for copy in copies(p):
                copy.start()
        pieces = [mixed[e ^ turn] for e in range(N_CH)]
        values = jnp.concatenate(
            [
                jnp.concatenate([piece[:, BS * a : BS * a + BS] for piece in pieces], axis=1)
                for a in range(6)
            ],
            axis=0,
        )
        average = jnp.sum(values, axis=1, keepdims=True) * (1.0 / C)
        squares = jnp.sum(values * values, axis=1, keepdims=True) * (1.0 / C)
        inv = lax.rsqrt(squares - average * average + EPSILON)
        values = (values - average) * inv
        normed[...] = values
        inv_std[...] = jnp.broadcast_to(inv, (cells, 128))
        inputs[...] = (values * gain_row()).astype(BF16)
        for k in range(N_CH):
            chunk_rows[k] = given_cots[k][...].astype(F32)
        pieces = [chunk_rows[e ^ turn ^ core[1]] for e in range(N_CH)]
        cots[...] = jnp.concatenate(
            [
                jnp.concatenate([piece[:, BS * a : BS * a + BS] for piece in pieces], axis=1)
                for a in range(6)
            ],
            axis=0,
        ).astype(BF16)
        sum_out[...] = jnp.zeros_like(sum_out)
        sum_grad[...] = jnp.zeros_like(sum_grad)

    for p in range(4):

        @pl.when(step == p)
        def _():
            for copy in copies(p):
                copy.wait()

    own_in, own_out = weight_in[step], weight_out[step]
    values, given = inputs[...], cots[...]
    hidden, slope = gelu_parts(dot(values, own_in))
    hidden = hidden.astype(BF16)
    grad_pre = (dot_nt(given, own_out) * slope).astype(BF16)
    sum_out[...] += dot(hidden, own_out)
    sum_grad[...] += dot_nt(grad_pre, own_in)
    grad_in = dot_tn(values, grad_pre)
    grad_out = dot_tn(hidden, given)
    for b in range(2):
        units = slice(384 * b, 384 * b + 384)
        grad_in_own[b, 0] = grad_in[:384, units]
        grad_in_other[b, 0] = grad_in[384:, units].astype(BF16)
        grad_out_own[b] = grad_out[units, :384]
        grad_out_other[b] = grad_out[units, 384:].astype(BF16)

    @pl.when(step == 3)
    def _():
        grad_input = sum_grad[...]
        values = normed[...]
        gain_sum = jnp.sum(grad_input * values, axis=0, keepdims=True)
        scaled = grad_input * gain_row()
        leading = jnp.sum(scaled, axis=1, keepdims=True) * (1.0 / C)
        paired = jnp.sum(scaled * values, axis=1, keepdims=True) * (1.0 / C)
        grad_mixed = cots[...].astype(F32) + inv_std[:, :1] * (scaled - leading - values * paired)
        outputs = sum_out[...]

        def chunk(array, e):
            return jnp.concatenate(
                [array[part * a : part * a + part, BS * e : BS * e + BS] for a in range(6)],
                axis=1,
            )

        for e in range(N_CH):
            chunk_rows[e ^ turn ^ core[1]] = chunk(outputs, e)
            gain_piece = gain_sum[:, BS * e : BS * e + BS]
            gain_high = gain_piece.astype(BF16).astype(F32)
            extra = jnp.concatenate(
                [gain_high, gain_piece - gain_high, jnp.zeros((1, 4 * BS), F32)], axis=1
            )
            extra = jnp.concatenate([extra, jnp.zeros((7, 6 * BS), F32)], axis=0)
            grad_chunks[e ^ turn] = jnp.concatenate(
                [chunk(grad_mixed, e), extra], axis=0
            ).astype(BF16)
        for k in range(N_CH):
            out_chunks[k][...] = chunk_rows[k].astype(BF16)


def lon_back_kernel(chunks, x, stats, t_high, t_low, wire, grad_mixed, gains, scratch):
    average, inv_std = norm_rows(stats)
    pieces = [chunks[e].astype(F32) for e in range(N_CH)]
    gain_first = jnp.zeros((BS, 1), F32)
    for r in range(ROWS):
        values = from_chunks(pieces, r)
        rounded = values.astype(BF16)
        put_row(scratch, r, dot(t_high[...], rounded) + dot(t_low[...], rounded))
        turned = values.T
        grad_mixed[r] = turned.astype(BF16)
        normed = (x[r].astype(F32) - average[r : r + 1]) * inv_std[r : r + 1]
        gain_first = gain_first + jnp.sum(turned * normed, axis=1, keepdims=True)
    flush_rows(scratch, wire)
    gain_second = jnp.zeros((1, BS), F32)
    for piece in pieces:
        row = piece[8 * ROWS : 8 * ROWS + 1]
        gain_second = gain_second + row[:, :BS] + row[:, BS : 2 * BS]
    turned_first = jnp.broadcast_to(gain_first, (BS, 128)).T[0:1, :]
    gains[0:1, :BS] = turned_first
    gains[1:2, :BS] = gain_second


def unmix_kernel(wire, tt_high, tt_low, grad_mixed, x, stats, gain, scaled, sums, scratch):
    average, inv_std = norm_rows(stats)
    load_packed(wire, scratch)
    for r in range(ROWS):
        modes = get_row(scratch, r).astype(BF16)
        back = dot(tt_high[...], modes) + dot(tt_low[...], modes)
        values = (back.T + grad_mixed[r].astype(F32)) * gain[...]
        normed = (x[r].astype(F32) - average[r : r + 1]) * inv_std[r : r + 1]
        scaled[r] = values
        sums[r : r + 1] = jnp.sum(values, axis=0, keepdims=True)
        sums[8 + r : 9 + r] = jnp.sum(values * normed, axis=0, keepdims=True)
    sums[7:8] = jnp.zeros((1, W), F32)
    sums[15:16] = jnp.zeros((1, W), F32)


def final_kernel(scaled, grad_mixed, x, stats, *rest):
    average, inv_std = norm_rows(stats)
    out = rest[-1]
    total = rest[0][...]
    for part in rest[1:-1]:
        total = total + part[...]
    total = total * (1.0 / C)
    for r in range(ROWS):
        inv = inv_std[r : r + 1]
        normed = (x[r].astype(F32) - average[r : r + 1]) * inv
        change = scaled[r] - total[r : r + 1] - normed * total[8 + r : 9 + r]
        out[r] = (grad_mixed[r].astype(F32) + inv * change).astype(BF16)


def pack_kernel(wire, small, *refs):
    out = refs[12]

    def add(parts):
        total = parts[0].astype(F32)
        for part in parts[1:]:
            total = total + part.astype(F32)
        return total

    total_in = add([refs[0][0, 0], refs[1][0, 0], refs[2][0]] + [part[...] for part in refs[3:6]])
    total_out = add([part[0] for part in refs[6:11]] + [refs[11][...]])
    total = jnp.concatenate([total_in, total_out], axis=0)
    modes = wire[...].astype(F32).reshape(N_LAT, 8, LANES)
    weights = small[:N_LAT]
    row = lax.broadcasted_iota(jnp.int32, (N_LAT, 8, LANES), 1)
    modes = jnp.where(row == ROWS, weights[:, None, :], modes)
    grads = jnp.concatenate(
        [total[256 * g : 256 * g + 256].reshape(N_LAT, 8, GROUP) for g in range(3)], axis=2
    )
    out[...] = jnp.concatenate([modes, grads], axis=1).astype(BF16)


def spread_kernel(parts, small, out):
    sums = [parts[n].astype(F32) for n in (0, 1)]
    for n in range(2, N_LAT):
        sums[n % 2] = sums[n % 2] + parts[n].astype(F32)
    rows = [
        half[8:16, GROUP * g : GROUP * g + GROUP] for half in sums for g in range(3)
    ]
    weights = sums[0][ROWS : ROWS + 1] + sums[1][ROWS : ROWS + 1]
    last = [weights[:, GROUP * g : GROUP * g + GROUP] for g in range(3)]
    last += [small[N_LAT : N_LAT + 1, :GROUP], jnp.zeros((4, GROUP), F32)]
    total = jnp.concatenate(rows + [jnp.concatenate(last, axis=0)], axis=0).astype(BF16)
    for n in range(N_LAT // 2):
        out[n] = total


def finish_kernel(
    place, mine, theirs, grad_in, grad_out, grad_inner, grad_outer, gain_first, gain_second
):
    first = place[0] == 0
    one, two = mine[...].astype(F32), theirs[...].astype(F32)
    even, odd = jnp.where(first, one, two), jnp.where(first, two, one)

    def rows(start):
        parts = [part[:, start : start + 8][:, None] for part in (even, odd)]
        return jnp.concatenate(parts, axis=1).reshape(256, GROUP)

    for half in range(2):
        total = jnp.concatenate([rows(24 * half + 8 * g) for g in range(3)], axis=0)
        grad_in[384 * half : 384 * half + 384] = total[:384]
        grad_out[:, 384 * half : 384 * half + 384] = total[384:]
    last = rows(48)
    planes = [
        jnp.concatenate([last[8 * n + g : 8 * n + g + 1] for n in range(N_LAT)], axis=0)
        for g in range(4)
    ]
    weights = [
        plane[:, BS * q : BS * q + BS] for plane in planes[:3] for q in range(4)
    ]
    for part in range(2):
        grad_inner[part, 0] = jnp.concatenate(weights[3 * part : 3 * part + 3], axis=0)
        grad_outer[part, 0] = jnp.concatenate(weights[6 + 3 * part : 9 + 3 * part], axis=0)
    gains = jnp.sum(planes[3], axis=0, keepdims=True)
    gain_first[...] = gains[:, :BS] + gains[:, BS : 2 * BS]
    gain_second[...] = gains[:, 2 * BS : 3 * BS] + gains[:, 3 * BS :]


def output_kernel(place, mixed, *refs):
    chunks, out, chunk_rows = refs[:N_CH], refs[N_CH], refs[N_CH + 1]
    for k in range(N_CH):
        chunk_rows[k] = chunks[k][...].astype(F32)
    pieces = [chunk_rows[e ^ place[1]] for e in range(N_CH)]
    for r in range(ROWS):
        out[r] = (from_chunks(pieces, r) + mixed[r]).T.astype(BF16)


def cost(micros):
    return pl.CostEstimate(
        flops=int(micros * 1.0e9), bytes_accessed=int(micros * 2.0e6), transcendentals=0
    )


def call(kernel, out_shape, *args, scratch=(), micros=3, place=None):
    specs = [pl.BlockSpec(memory_space=pltpu.VMEM)] * len(args)
    if place is not None:
        args = (place,) + args
        specs = [pl.BlockSpec(memory_space=pltpu.SMEM)] + specs
    return pl.pallas_call(
        kernel,
        out_shape=out_shape,
        in_specs=specs,
        scratch_shapes=scratch,
        compiler_params=pltpu.CompilerParams(vmem_limit_bytes=VMEM_BYTES),
        cost_estimate=cost(micros),
    )(*args)


def shaped(*shape, dtype=F32):
    return jax.ShapeDtypeStruct(shape, dtype)


def whole(shape):
    return pl.BlockSpec(shape, lambda g: (0,) * len(shape))


def lane_block(rows):
    return pl.BlockSpec((rows, GROUP), lambda g: (0, g))


def block_matrix(weight, swap_columns, swap_rows):
    real, imag = weight[0, 0].T, weight[1, 0].T
    base = [[real, imag], [-imag, real]]
    if swap_columns:
        base = [[imag, -real], [real, imag]]
    if swap_rows:
        base = [[-imag, real], [-real, -imag]]
    one = jnp.concatenate([jnp.concatenate(line, axis=1) for line in base], axis=0)
    zero = jnp.zeros_like(one)
    return jnp.concatenate(
        [jnp.concatenate([one, zero], axis=1), jnp.concatenate([zero, one], axis=1)], axis=0
    )


def to_all(values, axis, count, **kwargs):
    spread = jnp.broadcast_to(values[None], (count,) + values.shape)
    return lax.all_to_all(spread, axis, 0, 0, tiled=True, **kwargs)


def near(values, k):
    return lax.ppermute(values, "ch", [(i, i ^ k) for i in range(N_CH)])


def body(fields, gain_first, w_inner, w_outer, gain_second, fc_in, fc_out, cotangent):
    lat = lax.axis_index("lat")
    core = lat % 2
    me = lax.axis_index("ch")
    place = jnp.stack([core, me]).astype(jnp.int32)
    siblings = [(i, i ^ 1) for i in range(N_LAT)]
    cores = [list(range(0, N_LAT, 2)), list(range(1, N_LAT, 2))]
    t_high, t_low = (jnp.asarray(t) for t in halves(lon_table()))
    tt_high, tt_low = (jnp.asarray(t) for t in halves(lon_table().T))
    forward, inverse = lat_tables()
    lf_high, lf_low = (jnp.asarray(t) for t in halves(forward))
    li_high, li_low = (jnp.asarray(t) for t in halves(inverse))
    swap = jnp.asarray(swap_table())

    x = fields.transpose(1, 0, 2)
    cot = cotangent.transpose(1, 0, 2)
    gain_column = gain_first[:, None]

    with jax.named_scope("stats"):
        x_float = x.astype(F32)
        zero = jnp.zeros((1, W), F32)
        payload = jnp.concatenate(
            [
                jnp.sum(x_float, 1),
                zero,
                jnp.sum(x_float * x_float, 1),
                zero,
                jnp.pad(gain_second, (0, W - BS))[None],
                jnp.zeros((7, W), F32),
            ],
            axis=0,
        )
        gathered = to_all(payload, "ch", N_CH)
        gathered, fc_in, fc_out, cot = lax.optimization_barrier((gathered, fc_in, fc_out, cot))

    with jax.named_scope("weights"):
        half_in = lax.dynamic_slice_in_dim(fc_in, core * 384, 384, 0)
        half_out = lax.dynamic_slice_in_dim(fc_out, core * 384, 384, 1)
        near_in = near(half_in, 1)
        near_out = [near(half_out, k) for k in (2, 4, 6)]

    with jax.named_scope("cot"):
        chunk_shape = shaped(8 * ROWS, 6 * BS, dtype=BF16)
        first, *others = call(
            cot_kernel, [chunk_shape] * N_CH, cot, place=place,
            scratch=[pltpu.VMEM((ROWS, W, BS), F32)],
        )
        cot_chunks = [first] + [near(part, k + 1) for k, part in enumerate(others)]

    with jax.named_scope("stats"):
        stats = gathered[:, :16]
        gains = gathered[:, 16:17, :BS]

    scratch = pltpu.VMEM((LANES // 128, 8 * N_LAT, 128), F32)
    wire_shape = shaped(8 * N_LAT, LANES, dtype=BF16)
    with jax.named_scope("lon"):
        wire = call(
            lon_kernel, wire_shape, x, stats, gain_column, t_high, t_low, scratch=[scratch]
        )
        wire = lax.all_to_all(wire, "lat", 0, 0, tiled=True)

    with jax.named_scope("weights"):
        pair = jnp.stack([half_in, near_in])
        own_in = [pair] + [near(pair, k) for k in (2, 4, 6)]
        quad = jnp.stack([half_out] + near_out)
        own_out = [quad, near(quad, 1)]

    with jax.named_scope("matrices"):
        m1 = split(
            jnp.concatenate(
                [block_matrix(w_inner, False, False), block_matrix(w_inner, False, True)], axis=0
            )
        )
        m2 = split(
            jnp.concatenate(
                [block_matrix(w_outer, False, False), block_matrix(w_outer, True, False)], axis=1
            )
        )
        lane = jnp.arange(LANES, dtype=jnp.int32)[None]
        doubled = jnp.where((lat == 0) & (lane < 2 * BS), 1.0, 2.0).astype(F32)

    table_specs = [whole((H, 512)), whole((H, 512)), whole((GROUP, GROUP))]
    inverse_specs = [lane_block(1), whole((256, 448)), whole((256, 448))]
    params = pltpu.CompilerParams(vmem_limit_bytes=VMEM_BYTES)
    with jax.named_scope("spectral"):
        wire, spectrum, pre_modes = pl.pallas_call(
            spectral_kernel,
            grid=(3,),
            in_specs=[lane_block(256)]
            + table_specs
            + [whole((GROUP, GROUP))] * 2
            + [whole((GROUP, 2 * GROUP))] * 2
            + inverse_specs,
            out_specs=[lane_block(256), lane_block(H), lane_block(H)],
            out_shape=[wire_shape, shaped(H, LANES), shaped(H, LANES)],
            compiler_params=params,
            cost_estimate=cost(11),
        )(
            wire, lf_high, lf_low, swap, m1[0][:GROUP], m1[1][:GROUP], m2[0], m2[1], doubled,
            li_high, li_low,
        )
        *weights, wire = lax.optimization_barrier((*own_in, *own_out, wire))
        wire = lax.all_to_all(wire, "lat", 0, 0, tiled=True)
        *cot_chunks, wire = lax.optimization_barrier((*cot_chunks, wire))
        weights += [lax.ppermute(part, "lat", siblings) for part in weights]

    with jax.named_scope("mix"):
        mixed, chunks = call(
            mix_kernel,
            [shaped(ROWS, W, BS), shaped(N_CH, 8 * ROWS, 6 * BS)],
            wire, tt_high, tt_low, x, stats, gain_column,
            scratch=[scratch],
        )
        chunks = lax.all_to_all(chunks, "ch", 0, 0, tiled=True)

    cells = 48 * ROWS
    halved = pl.BlockSpec((2, 1, 384, 384), lambda p, place: (0, p, 0, 0))
    direct = pl.BlockSpec((2, 384, 384), lambda p, place: (p, 0, 0))

    def all_of(shape):
        return pl.BlockSpec(shape, lambda e, place: (0,) * len(shape))

    with jax.named_scope("mlp"):
        *out_chunks, grad_chunks, in_own, in_other, out_own, out_other = pl.pallas_call(
            mlp_kernel,
            grid_spec=pltpu.PrefetchScalarGridSpec(
                num_scalar_prefetch=1,
                grid=(4,),
                in_specs=[
                    all_of((N_CH, 8 * ROWS, 6 * BS)),
                    all_of((N_CH, 1, BS)),
                ]
                + [all_of((8 * ROWS, 6 * BS))] * N_CH
                + [pl.BlockSpec(memory_space=pl.ANY)] * 12,
                out_specs=[all_of((8 * ROWS, 6 * BS))] * N_CH
                + [
                    all_of((N_CH, 8 * ROWS + 8, 6 * BS)),
                    halved,
                    halved,
                    direct,
                    direct,
                ],
                scratch_shapes=[
                    pltpu.VMEM((cells, C), F32),
                    pltpu.VMEM((cells, C), BF16),
                    pltpu.VMEM((cells, C), BF16),
                    pltpu.VMEM((cells, 128), F32),
                    pltpu.VMEM((cells, C), F32),
                    pltpu.VMEM((cells, C), F32),
                    pltpu.VMEM((4, C, C), BF16),
                    pltpu.VMEM((4, C, C), BF16),
                    pltpu.VMEM((N_CH, 8 * ROWS, 6 * BS), F32),
                    pltpu.SemaphoreType.DMA((32,)),
                ],
            ),
            out_shape=[chunk_shape] * N_CH
            + [
                shaped(N_CH, 8 * ROWS + 8, 6 * BS, dtype=BF16),
                shaped(2, 4, 384, 384),
                shaped(2, 4, 384, 384, dtype=BF16),
                shaped(N_CH, 384, 384),
                shaped(N_CH, 384, 384, dtype=BF16),
            ],
            compiler_params=params,
            cost_estimate=cost(20),
        )(place, chunks, gains, *cot_chunks, *weights)
        grad_chunks = lax.all_to_all(grad_chunks, "ch", 0, 0, tiled=True)

    with jax.named_scope("grads_ch"):
        theirs_in = lax.ppermute(in_other, "lat", siblings)
        theirs_out = lax.ppermute(out_other, "lat", siblings)
        odd = (in_own[1] + theirs_in[1].astype(F32)).astype(BF16)
        pairs = [
            (out_own[k : k + 2] + theirs_out[k : k + 2].astype(F32)).astype(BF16)
            for k in (2, 4, 6)
        ]
        early = near(pairs[0], 2)
        odd, *pairs, grad_chunks = lax.optimization_barrier((odd, *pairs, grad_chunks))
        odd = near(odd, 1)
        pairs = [near(part, k) for part, k in zip(pairs[1:], (4, 6))]

    with jax.named_scope("lon_back"):
        wire, grad_mixed, gain_parts = call(
            lon_back_kernel,
            [wire_shape, shaped(ROWS, BS, W, dtype=BF16), shaped(8, 128)],
            grad_chunks, x, stats, t_high, t_low,
            scratch=[scratch],
        )
        early, wire = lax.optimization_barrier((early, wire))
        wire = lax.all_to_all(wire, "lat", 0, 0, tiled=True)

    with jax.named_scope("grads_ch"):
        odd, early, *pairs, wire = lax.optimization_barrier((odd, early, *pairs, wire))
        pairs.append(early)
        even = in_own[0, 1:] + theirs_in[0, 1:].astype(F32) + odd[1:].astype(F32)
        even = even.astype(BF16)
        far = out_own[1] + theirs_out[1].astype(F32)
        for part in pairs:
            far = far + part[1].astype(F32)
        in_parts = [near(even[k // 2 - 1], k) for k in (2, 4, 6)]
        out_part = near(far.astype(BF16), 1)

    with jax.named_scope("spectral_back"):
        wire, small = pl.pallas_call(
            spectral_back_kernel,
            grid=(3,),
            in_specs=[lane_block(256), lane_block(H), lane_block(H)]
            + table_specs
            + [whole((2 * GROUP, GROUP))] * 2
            + [whole((GROUP, 2 * GROUP))] * 2
            + inverse_specs
            + [whole((1, BS)), whole((8, 128))],
            out_specs=[lane_block(256), whole((N_LAT + 8, LANES))],
            out_shape=[wire_shape, shaped(N_LAT + 8, LANES)],
            scratch_shapes=[
                pltpu.VMEM((GROUP, GROUP), F32),
                pltpu.VMEM((GROUP, GROUP), F32),
                pltpu.VMEM((8, 128), F32),
            ],
            compiler_params=params,
            cost_estimate=cost(14),
        )(
            wire, spectrum, pre_modes, lf_high, lf_low, swap, m1[0], m1[1], m2[0], m2[1], doubled,
            li_high, li_low, gain_first[None], gain_parts,
        )
        *in_parts, out_part, wire = lax.optimization_barrier((*in_parts, out_part, wire))

    with jax.named_scope("pack"):
        corner = pl.BlockSpec((1, 1, 384, 384), lambda g: (0, 0, 0, 0))
        front = pl.BlockSpec((1, 384, 384), lambda g: (0, 0, 0))
        flat = whole((384, 384))
        wire = pl.pallas_call(
            pack_kernel,
            grid=(1,),
            in_specs=[whole((256, LANES)), whole((N_LAT + 8, LANES))]
            + [corner, corner, front, flat, flat, flat]
            + [front, front, front, front, front, flat],
            out_specs=whole((N_LAT, 16, LANES)),
            out_shape=shaped(N_LAT, 16, LANES, dtype=BF16),
            compiler_params=params,
            cost_estimate=cost(3),
        )(
            wire, small, in_own, theirs_in, odd, *in_parts, out_own, theirs_out, *pairs, out_part
        )
        *out_chunks, wire = lax.optimization_barrier((*out_chunks, wire))
        wire = lax.all_to_all(wire, "lat", 0, 0, tiled=True)

    with jax.named_scope("output"):
        first, *others = out_chunks
        out_chunks = [first] + [near(part, k + 1) for k, part in enumerate(others)]
        output = call(
            output_kernel, shaped(ROWS, BS, W, dtype=BF16), mixed, *out_chunks, place=place,
            scratch=[pltpu.VMEM((N_CH, 8 * ROWS, 6 * BS), F32)],
        )
        output, wire = lax.optimization_barrier((output, wire))

    with jax.named_scope("unmix"):
        scaled, sums = call(
            unmix_kernel,
            [shaped(ROWS, BS, W), shaped(16, W)],
            wire, tt_high, tt_low, grad_mixed, x, stats, gain_column,
            scratch=[scratch],
        )
    with jax.named_scope("sums"):
        sums = [sums] + [near(sums, k) for k in range(1, N_CH)]

    with jax.named_scope("grads_lat"):
        payload = call(spread_kernel, shaped(N_LAT // 2, 56, GROUP, dtype=BF16), wire, small)
        mine = lax.all_to_all(payload, "lat", 0, 0, tiled=True, axis_index_groups=cores)
        mine, *sums = lax.optimization_barrier((mine, *sums))
        theirs = lax.ppermute(mine, "lat", siblings)
        weight_shape = shaped(2, 1, BS, BS)
        grad_fc_in, grad_fc_out, grad_w_inner, grad_w_outer, grad_first, grad_second = call(
            finish_kernel,
            [
                shaped(C, FF_DEV),
                shaped(FF_DEV, C),
                weight_shape,
                weight_shape,
                shaped(1, BS),
                shaped(1, BS),
            ],
            mine, theirs, place=place,
        )

    with jax.named_scope("final"):
        grad_fields = call(
            final_kernel, shaped(ROWS, BS, W, dtype=BF16), scaled, grad_mixed, x, stats, *sums
        )

    return (
        output.transpose(1, 0, 2),
        grad_fields.transpose(1, 0, 2),
        grad_first[0],
        grad_w_inner,
        grad_w_outer,
        grad_second[0],
        grad_fc_in,
        grad_fc_out,
    )


def solution(mesh):
    placed = (
        P("ch", "lat", None),
        P("ch"),
        P(None, "ch", None, None),
        P(None, "ch", None, None),
        P("ch"),
        P(None, "ch"),
        P("ch", None),
        P("ch", "lat", None),
    )
    return jax.shard_map(
        body,
        mesh=mesh,
        in_specs=placed,
        out_specs=(
            P("ch", "lat", None),
            P("ch", "lat", None),
            P("ch"),
            P(None, "ch", None, None),
            P(None, "ch", None, None),
            P("ch"),
            P(None, "ch"),
            P("ch", None),
        ),
        check_vma=False,
    )
```

```python
import math

import jax
import jax.numpy as jnp
import ml_dtypes
import numpy as np
from jax import lax
from jax.experimental import pallas as pl
from jax.experimental.pallas import tpu as pltpu
from jax.sharding import PartitionSpec as P

C = 768
BS = 96
H = 224
W = 384
KW = 192
N_LAT = 32
N_CH = 8
ROWS = 7
FF_DEV = 384
MODES = KW // N_LAT
PLANES = 2 * MODES
LANES = PLANES * BS
GROUP = 384
EPSILON = 1e-05
BF16 = jnp.bfloat16
F32 = jnp.float32
VMEM_BYTES = 56 * 1024 * 1024


def halves(table):
    high = table.astype(ml_dtypes.bfloat16)
    low = (table - high.astype(np.float64)).astype(ml_dtypes.bfloat16)
    return high, low


def lon_table():
    mode = np.arange(MODES)[:, None] + MODES * np.arange(N_LAT)[None, :]
    angles = 2 * np.pi * ((mode[:, :, None] * np.arange(W)) % W) / W
    table = np.stack([np.cos(angles), -np.sin(angles)], 1) / math.sqrt(W)
    return table.reshape(PLANES * N_LAT, W)


def lat_tables():
    index = np.arange(H)
    angles = 2 * np.pi * ((index[:, None] * index[None, :]) % H) / H
    cosine = np.cos(angles) / math.sqrt(H)
    sine = np.sin(angles) / math.sqrt(H)
    forward = np.zeros((H, 2, N_LAT, 8))
    forward[:, 0, :, :ROWS] = cosine.reshape(H, N_LAT, ROWS)
    forward[:, 1, :, :ROWS] = sine.reshape(H, N_LAT, ROWS)
    inverse = np.zeros((N_LAT, 8, 2, H))
    inverse[:, :ROWS, 0] = cosine.reshape(N_LAT, ROWS, H)
    inverse[:, :ROWS, 1] = -sine.reshape(N_LAT, ROWS, H)
    return forward.reshape(H, 2 * N_LAT * 8), inverse.reshape(N_LAT * 8, 2 * H)


def swap_table():
    table = np.zeros((GROUP, GROUP))
    for mode in range(2):
        for c in range(BS):
            real = mode * 2 * BS + c
            table[real + BS, real] = 1
            table[real, real + BS] = -1
    return table.astype(ml_dtypes.bfloat16)


def dot(left, right):
    return lax.dot_general(left, right, (((1,), (0,)), ((), ())), preferred_element_type=F32)


def dot_nt(left, right):
    return lax.dot_general(left, right, (((1,), (1,)), ((), ())), preferred_element_type=F32)


def dot_tn(left, right):
    return lax.dot_general(left, right, (((0,), (0,)), ((), ())), preferred_element_type=F32)


def split(values):
    high = values.astype(BF16)
    return high, (values - high.astype(F32)).astype(BF16)


def dot3(kind, left, right):
    return kind(left[0], right[0]) + kind(left[1], right[0]) + kind(left[0], right[1])


def gelu_parts(values):
    cdf = 0.5 * (1.0 + lax.erf(values * 0.7071067811865476))
    return values * cdf, cdf + values * 0.3989422804014327 * jnp.exp(-0.5 * values * values)


def gelu_value(values):
    return 0.5 * values * (1.0 + lax.erf(values * 0.7071067811865476))


def norm_rows(stats):
    total = stats[0]
    for e in range(1, N_CH):
        total = total + stats[e]
    average = total[0:8] * (1.0 / C)
    squares = total[8:16] * (1.0 / C)
    return average, lax.rsqrt(squares - average * average + EPSILON)


def put_row(scratch, row, modes):
    wide = jnp.concatenate([modes[32 * k : 32 * k + 32] for k in range(PLANES)], axis=1)
    for t in range(LANES // 128):
        scratch[t, pl.ds(row, N_LAT, stride=8), :] = wide[:, 128 * t : 128 * t + 128]


def flush_rows(scratch, wire):
    for t in range(LANES // 128):
        scratch[t, pl.ds(ROWS, N_LAT, stride=8), :] = jnp.zeros((N_LAT, 128), F32)
        wire[:, 128 * t : 128 * t + 128] = scratch[t].astype(BF16)


def load_rows(wire, scratch):
    for t in range(LANES // 128):
        scratch[t] = wire[:, 128 * t : 128 * t + 128].astype(F32)


def load_packed(wire, scratch):
    for t in range(LANES // 128):
        block = wire[:, :, 128 * t : 128 * t + 128].astype(F32)
        scratch[t] = block[:, :8].reshape(8 * N_LAT, 128)


def get_row(scratch, row):
    wide = jnp.concatenate(
        [scratch[t, pl.ds(row, N_LAT, stride=8), :] for t in range(LANES // 128)], axis=1
    )
    return jnp.concatenate([wide[:, BS * k : BS * k + BS] for k in range(PLANES)], axis=0)


def to_chunk(rows, e):
    return jnp.concatenate(
        [
            jnp.concatenate(
                [values[48 * e + 8 * a : 48 * e + 8 * a + 8] for a in range(6)], axis=1
            )
            for values in rows
        ],
        axis=0,
    )


def from_chunks(chunks, row):
    return jnp.concatenate(
        [
            chunk[8 * row : 8 * row + 8, BS * a : BS * a + BS]
            for chunk in chunks
            for a in range(6)
        ],
        axis=0,
    )


def cot_kernel(place, cot, *refs):
    chunks, scratch = refs[:N_CH], refs[N_CH]
    for r in range(ROWS):
        scratch[r] = cot[r].astype(F32).T
    for k in range(N_CH):
        cells = pl.ds(pl.multiple_of(48 * (place[1] ^ k), 8), 48)
        chunks[k][...] = to_chunk([scratch[r, cells] for r in range(ROWS)], 0).astype(BF16)


def lon_kernel(x, stats, gain, t_high, t_low, wire, scratch):
    average, inv_std = norm_rows(stats)
    table = (t_high[...], t_low[...])
    for r in range(ROWS):
        normed = (x[r].astype(F32) - average[r : r + 1]) * inv_std[r : r + 1]
        lifted = split(normed * gain[...])
        put_row(scratch, r, dot3(dot_nt, table, lifted))
    flush_rows(scratch, wire)


def lat_forward(wire, lf_high, lf_low, swap):
    values = wire[...]
    swapped = dot(values, swap[...]).astype(BF16)
    both = jnp.concatenate([values, swapped], axis=0)
    return dot(lf_high[...], both) + dot(lf_low[...], both)


def lat_inverse(modes, li_high, li_low):
    both = split(jnp.concatenate([modes[:, :GROUP], modes[:, GROUP:]], axis=0))
    return dot3(dot, (li_high[...], li_low[...]), both)


def weight_sum(blocks):
    def block(part, other):
        pieces = [
            blocks[m + BS * part : m + BS * part + BS, m + BS * other : m + BS * other + BS]
            for m in (0, 2 * BS)
        ]
        return pieces[0] + pieces[1]

    return jnp.concatenate(
        [block(0, 0) + block(1, 1), block(1, 0) - block(0, 1)], axis=0
    )


def spectral_kernel(
    wire, lf_high, lf_low, swap, m1_high, m1_low, m2_high, m2_low, doubled, li_high, li_low,
    out, spectrum, pre_modes,
):
    modes = lat_forward(wire, lf_high, lf_low, swap)
    spectrum[...] = modes
    pre = dot3(dot, split(modes), (m1_high[...], m1_low[...]))
    pre_modes[...] = pre
    act = split(gelu_value(pre))
    scale = doubled[...]
    result = dot3(dot, act, (m2_high[...], m2_low[...])) * jnp.concatenate([scale, scale], axis=1)
    out[...] = lat_inverse(result, li_high, li_low).astype(BF16)


def spectral_back_kernel(
    wire, spectrum, pre_modes, lf_high, lf_low, swap, m1_high, m1_low, m2_high, m2_low, doubled,
    li_high, li_low, gain, gain_parts, out, small, grad_outer, grad_inner, gain_sum,
):
    @pl.when(pl.program_id(0) == 0)
    def _():
        grad_outer[...] = jnp.zeros_like(grad_outer)
        grad_inner[...] = jnp.zeros_like(grad_inner)
        gain_sum[...] = jnp.zeros_like(gain_sum)

    grad = split(lat_forward(wire, lf_high, lf_low, swap) * doubled[...])
    act, slope = gelu_parts(pre_modes[...])
    grad_act = dot3(dot_nt, grad, (m2_high[:, :GROUP], m2_low[:, :GROUP]))
    grad_outer[...] += dot3(dot_tn, grad, split(act))
    grad_pre = split(grad_act * slope)
    modes = spectrum[...]
    grad_inner[...] += dot3(dot_tn, grad_pre, split(modes))
    grad_spectrum = dot3(dot_nt, grad_pre, (m1_high[...], m1_low[...]))
    gain_row = jnp.sum(grad_spectrum[:, :GROUP] * modes, axis=0, keepdims=True)
    gain_row = sum(gain_row[:, BS * k : BS * k + BS] for k in range(4))
    gain_sum[0:1, :BS] += gain_row
    out[...] = lat_inverse(grad_spectrum, li_high, li_low).astype(BF16)

    @pl.when(pl.program_id(0) == 2)
    def _():
        first = gain_sum[0:1, :BS] / gain[...] + gain_parts[0:1, :BS]
        weights = [weight_sum(grad_inner[...]), weight_sum(grad_outer[...])]
        small[:N_LAT] = jnp.concatenate(
            [weight[32 * q : 32 * q + 32] for weight in weights for q in range(6)], axis=1
        )
        row = []
        for values in (first, gain_parts[1:2, :BS]):
            high = values.astype(BF16).astype(F32)
            row += [high, values - high]
        row = jnp.concatenate(row + [jnp.zeros((1, 8 * BS), F32)], axis=1)
        small[N_LAT:] = jnp.concatenate([row, jnp.zeros((7, LANES), F32)], axis=0)


def mix_kernel(wire, tt_high, tt_low, x, stats, gain, mixed, chunks, scratch):
    average, inv_std = norm_rows(stats)
    load_rows(wire, scratch)
    rows = []
    for r in range(ROWS):
        x_float = x[r].astype(F32)
        lifted = (x_float - average[r : r + 1]) * inv_std[r : r + 1] * gain[...]
        modes = get_row(scratch, r).astype(BF16)
        filtered = dot(tt_high[...], modes) + dot(tt_low[...], modes)
        values = filtered + (lifted + x_float).T
        mixed[r] = values
        rows.append(values)
    for e in range(N_CH):
        chunks[e] = to_chunk(rows, e)


def mlp_kernel(core, mixed, gain, *refs):
    given_cots, weights, refs = refs[:8], refs[8:20], refs[20:]
    out_chunks, refs = refs[:8], refs[8:]
    grad_chunks, grad_in_own, grad_in_other, grad_out_own, grad_out_other = refs[:5]
    (
        normed, inputs, cots, inv_std, sum_out, sum_grad, weight_in, weight_out, chunk_rows, arrived,
    ) = refs[5:]
    step = pl.program_id(0)
    turn = 4 * core[0]
    cells = 6 * 8 * ROWS
    part = 8 * ROWS

    def gain_row():
        return jnp.concatenate([gain[e ^ turn] for e in range(N_CH)], axis=1)

    def copies(p):
        found = []
        for half in range(2):
            parts = weights[6 * half : 6 * half + 6]
            rows = pl.ds(384 * half, 384)
            for b in range(2):
                units = pl.ds(384 * b, 384)
                found.append((parts[p].at[b], weight_in.at[p, rows, units]))
                found.append((parts[4 + b].at[p], weight_out.at[p, units, rows]))
        return [
            pltpu.make_async_copy(source, target, arrived.at[8 * p + n])
            for n, (source, target) in enumerate(found)
        ]

    @pl.when(step == 0)
    def _():
        for p in range(4):
            for copy in copies(p):
                copy.start()
        pieces = [mixed[e ^ turn] for e in range(N_CH)]
        values = jnp.concatenate(
            [
                jnp.concatenate([piece[:, BS * a : BS * a + BS] for piece in pieces], axis=1)
                for a in range(6)
            ],
            axis=0,
        )
        average = jnp.sum(values, axis=1, keepdims=True) * (1.0 / C)
        squares = jnp.sum(values * values, axis=1, keepdims=True) * (1.0 / C)
        inv = lax.rsqrt(squares - average * average + EPSILON)
        values = (values - average) * inv
        normed[...] = values
        inv_std[...] = jnp.broadcast_to(inv, (cells, 128))
        inputs[...] = (values * gain_row()).astype(BF16)
        for k in range(N_CH):
            chunk_rows[k] = given_cots[k][...].astype(F32)
        pieces = [chunk_rows[e ^ turn ^ core[1]] for e in range(N_CH)]
        cots[...] = jnp.concatenate(
            [
                jnp.concatenate([piece[:, BS * a : BS * a + BS] for piece in pieces], axis=1)
                for a in range(6)
            ],
            axis=0,
        ).astype(BF16)
        sum_out[...] = jnp.zeros_like(sum_out)
        sum_grad[...] = jnp.zeros_like(sum_grad)

    for p in range(4):

        @pl.when(step == p)
        def _():
            for copy in copies(p):
                copy.wait()

    own_in, own_out = weight_in[step], weight_out[step]
    values, given = inputs[...], cots[...]
    hidden, slope = gelu_parts(dot(values, own_in))
    hidden = hidden.astype(BF16)
    grad_pre = (dot_nt(given, own_out) * slope).astype(BF16)
    sum_out[...] += dot(hidden, own_out)
    sum_grad[...] += dot_nt(grad_pre, own_in)
    grad_in = dot_tn(values, grad_pre)
    grad_out = dot_tn(hidden, given)
    for b in range(2):
        units = slice(384 * b, 384 * b + 384)
        grad_in_own[b, 0] = grad_in[:384, units]
        grad_in_other[b, 0] = grad_in[384:, units].astype(BF16)
        grad_out_own[b, 0] = grad_out[units, :384]
        grad_out_other[b, 0] = grad_out[units, 384:].astype(BF16)

    @pl.when(step == 3)
    def _():
        grad_input = sum_grad[...]
        values = normed[...]
        gain_sum = jnp.sum(grad_input * values, axis=0, keepdims=True)
        scaled = grad_input * gain_row()
        leading = jnp.sum(scaled, axis=1, keepdims=True) * (1.0 / C)
        paired = jnp.sum(scaled * values, axis=1, keepdims=True) * (1.0 / C)
        grad_mixed = cots[...].astype(F32) + inv_std[:, :1] * (scaled - leading - values * paired)
        outputs = sum_out[...]

        def chunk(array, e):
            return jnp.concatenate(
                [array[part * a : part * a + part, BS * e : BS * e + BS] for a in range(6)],
                axis=1,
            )

        for e in range(N_CH):
            chunk_rows[e ^ turn ^ core[1]] = chunk(outputs, e)
            gain_piece = gain_sum[:, BS * e : BS * e + BS]
            gain_high = gain_piece.astype(BF16).astype(F32)
            extra = jnp.concatenate(
                [gain_high, gain_piece - gain_high, jnp.zeros((1, 4 * BS), F32)], axis=1
            )
            extra = jnp.concatenate([extra, jnp.zeros((7, 6 * BS), F32)], axis=0)
            grad_chunks[e ^ turn] = jnp.concatenate(
                [chunk(grad_mixed, e), extra], axis=0
            ).astype(BF16)
        for k in range(N_CH):
            out_chunks[k][...] = chunk_rows[k].astype(BF16)


def lon_back_kernel(chunks, x, stats, t_high, t_low, wire, grad_mixed, gains, scratch):
    average, inv_std = norm_rows(stats)
    pieces = [chunks[e].astype(F32) for e in range(N_CH)]
    gain_first = jnp.zeros((BS, 1), F32)
    for r in range(ROWS):
        values = from_chunks(pieces, r)
        rounded = values.astype(BF16)
        put_row(scratch, r, dot(t_high[...], rounded) + dot(t_low[...], rounded))
        turned = values.T
        grad_mixed[r] = turned.astype(BF16)
        normed = (x[r].astype(F32) - average[r : r + 1]) * inv_std[r : r + 1]
        gain_first = gain_first + jnp.sum(turned * normed, axis=1, keepdims=True)
    flush_rows(scratch, wire)
    gain_second = jnp.zeros((1, BS), F32)
    for piece in pieces:
        row = piece[8 * ROWS : 8 * ROWS + 1]
        gain_second = gain_second + row[:, :BS] + row[:, BS : 2 * BS]
    turned_first = jnp.broadcast_to(gain_first, (BS, 128)).T[0:1, :]
    gains[0:1, :BS] = turned_first
    gains[1:2, :BS] = gain_second


def unmix_kernel(wire, tt_high, tt_low, grad_mixed, x, stats, gain, scaled, sums, scratch):
    average, inv_std = norm_rows(stats)
    load_packed(wire, scratch)
    for r in range(ROWS):
        modes = get_row(scratch, r).astype(BF16)
        back = dot(tt_high[...], modes) + dot(tt_low[...], modes)
        values = (back.T + grad_mixed[r].astype(F32)) * gain[...]
        normed = (x[r].astype(F32) - average[r : r + 1]) * inv_std[r : r + 1]
        scaled[r] = values
        sums[r : r + 1] = jnp.sum(values, axis=0, keepdims=True)
        sums[8 + r : 9 + r] = jnp.sum(values * normed, axis=0, keepdims=True)
    sums[7:8] = jnp.zeros((1, W), F32)
    sums[15:16] = jnp.zeros((1, W), F32)


def final_kernel(scaled, grad_mixed, x, stats, *rest):
    average, inv_std = norm_rows(stats)
    out = rest[-1]
    total = rest[0][...]
    for part in rest[1:-1]:
        total = total + part[...]
    total = total * (1.0 / C)
    for r in range(ROWS):
        inv = inv_std[r : r + 1]
        normed = (x[r].astype(F32) - average[r : r + 1]) * inv
        change = scaled[r] - total[r : r + 1] - normed * total[8 + r : 9 + r]
        out[r] = (grad_mixed[r].astype(F32) + inv * change).astype(BF16)


def pack_kernel(wire, small, *refs):
    out = refs[11]

    def add(parts):
        total = parts[0].astype(F32)
        for part in parts[1:]:
            total = total + part.astype(F32)
        return total

    total_in = add([refs[0][0, 0], refs[1][0, 0], refs[2][0]] + [part[...] for part in refs[3:6]])
    total_out = add([refs[6][0, 0], refs[7][0, 0], refs[8][0], refs[9][...], refs[10][...]])
    total = jnp.concatenate([total_in, total_out], axis=0)
    modes = wire[...].astype(F32).reshape(N_LAT, 8, LANES)
    weights = small[:N_LAT]
    row = lax.broadcasted_iota(jnp.int32, (N_LAT, 8, LANES), 1)
    modes = jnp.where(row == ROWS, weights[:, None, :], modes)
    grads = jnp.concatenate(
        [total[256 * g : 256 * g + 256].reshape(N_LAT, 8, GROUP) for g in range(3)], axis=2
    )
    out[...] = jnp.concatenate([modes, grads], axis=1).astype(BF16)


def spread_kernel(parts, small, out):
    sums = [parts[n].astype(F32) for n in (0, 1)]
    for n in range(2, N_LAT):
        sums[n % 2] = sums[n % 2] + parts[n].astype(F32)
    rows = [
        half[8:16, GROUP * g : GROUP * g + GROUP] for half in sums for g in range(3)
    ]
    weights = sums[0][ROWS : ROWS + 1] + sums[1][ROWS : ROWS + 1]
    last = [weights[:, GROUP * g : GROUP * g + GROUP] for g in range(3)]
    last += [small[N_LAT : N_LAT + 1, :GROUP], jnp.zeros((4, GROUP), F32)]
    total = jnp.concatenate(rows + [jnp.concatenate(last, axis=0)], axis=0).astype(BF16)
    for n in range(N_LAT // 2):
        out[n] = total


def finish_kernel(
    place, mine, theirs, grad_in, grad_out, grad_inner, grad_outer, gain_first, gain_second
):
    first = place[0] == 0
    one, two = mine[...].astype(F32), theirs[...].astype(F32)
    even, odd = jnp.where(first, one, two), jnp.where(first, two, one)

    def rows(start):
        parts = [part[:, start : start + 8][:, None] for part in (even, odd)]
        return jnp.concatenate(parts, axis=1).reshape(256, GROUP)

    for half in range(2):
        total = jnp.concatenate([rows(24 * half + 8 * g) for g in range(3)], axis=0)
        grad_in[384 * half : 384 * half + 384] = total[:384]
        grad_out[:, 384 * half : 384 * half + 384] = total[384:]
    last = rows(48)
    planes = [
        jnp.concatenate([last[8 * n + g : 8 * n + g + 1] for n in range(N_LAT)], axis=0)
        for g in range(4)
    ]
    weights = [
        plane[:, BS * q : BS * q + BS] for plane in planes[:3] for q in range(4)
    ]
    for part in range(2):
        grad_inner[part, 0] = jnp.concatenate(weights[3 * part : 3 * part + 3], axis=0)
        grad_outer[part, 0] = jnp.concatenate(weights[6 + 3 * part : 9 + 3 * part], axis=0)
    gains = jnp.sum(planes[3], axis=0, keepdims=True)
    gain_first[...] = gains[:, :BS] + gains[:, BS : 2 * BS]
    gain_second[...] = gains[:, 2 * BS : 3 * BS] + gains[:, 3 * BS :]


def output_kernel(place, mixed, *refs):
    chunks, out, chunk_rows = refs[:N_CH], refs[N_CH], refs[N_CH + 1]
    for k in range(N_CH):
        chunk_rows[k] = chunks[k][...].astype(F32)
    pieces = [chunk_rows[e ^ place[1]] for e in range(N_CH)]
    for r in range(ROWS):
        out[r] = (from_chunks(pieces, r) + mixed[r]).T.astype(BF16)


def cost(micros):
    return pl.CostEstimate(
        flops=int(micros * 1.0e9), bytes_accessed=int(micros * 2.0e6), transcendentals=0
    )


def call(kernel, out_shape, *args, scratch=(), micros=3, place=None):
    specs = [pl.BlockSpec(memory_space=pltpu.VMEM)] * len(args)
    if place is not None:
        args = (place,) + args
        specs = [pl.BlockSpec(memory_space=pltpu.SMEM)] + specs
    return pl.pallas_call(
        kernel,
        out_shape=out_shape,
        in_specs=specs,
        scratch_shapes=scratch,
        compiler_params=pltpu.CompilerParams(vmem_limit_bytes=VMEM_BYTES),
        cost_estimate=cost(micros),
    )(*args)


def shaped(*shape, dtype=F32):
    return jax.ShapeDtypeStruct(shape, dtype)


def whole(shape):
    return pl.BlockSpec(shape, lambda g: (0,) * len(shape))


def lane_block(rows):
    return pl.BlockSpec((rows, GROUP), lambda g: (0, g))


def block_matrix(weight, swap_columns, swap_rows):
    real, imag = weight[0, 0].T, weight[1, 0].T
    base = [[real, imag], [-imag, real]]
    if swap_columns:
        base = [[imag, -real], [real, imag]]
    if swap_rows:
        base = [[-imag, real], [-real, -imag]]
    one = jnp.concatenate([jnp.concatenate(line, axis=1) for line in base], axis=0)
    zero = jnp.zeros_like(one)
    return jnp.concatenate(
        [jnp.concatenate([one, zero], axis=1), jnp.concatenate([zero, one], axis=1)], axis=0
    )


def to_all(values, axis, count, **kwargs):
    spread = jnp.broadcast_to(values[None], (count,) + values.shape)
    return lax.all_to_all(spread, axis, 0, 0, tiled=True, **kwargs)


def near(values, k):
    return lax.ppermute(values, "ch", [(i, i ^ k) for i in range(N_CH)])


def body(fields, gain_first, w_inner, w_outer, gain_second, fc_in, fc_out, cotangent):
    lat = lax.axis_index("lat")
    core = lat % 2
    me = lax.axis_index("ch")
    place = jnp.stack([core, me]).astype(jnp.int32)
    siblings = [(i, i ^ 1) for i in range(N_LAT)]
    cores = [list(range(0, N_LAT, 2)), list(range(1, N_LAT, 2))]
    t_high, t_low = (jnp.asarray(t) for t in halves(lon_table()))
    tt_high, tt_low = (jnp.asarray(t) for t in halves(lon_table().T))
    forward, inverse = lat_tables()
    lf_high, lf_low = (jnp.asarray(t) for t in halves(forward))
    li_high, li_low = (jnp.asarray(t) for t in halves(inverse))
    swap = jnp.asarray(swap_table())

    x = fields.transpose(1, 0, 2)
    cot = cotangent.transpose(1, 0, 2)
    gain_column = gain_first[:, None]

    with jax.named_scope("stats"):
        x_float = x.astype(F32)
        zero = jnp.zeros((1, W), F32)
        payload = jnp.concatenate(
            [
                jnp.sum(x_float, 1),
                zero,
                jnp.sum(x_float * x_float, 1),
                zero,
                jnp.pad(gain_second, (0, W - BS))[None],
                jnp.zeros((7, W), F32),
            ],
            axis=0,
        )
        gathered = to_all(payload, "ch", N_CH)
        gathered, fc_in, fc_out, cot = lax.optimization_barrier((gathered, fc_in, fc_out, cot))

    with jax.named_scope("weights"):
        half_in = lax.dynamic_slice_in_dim(fc_in, core * 384, 384, 0)
        half_out = lax.dynamic_slice_in_dim(fc_out, core * 384, 384, 1)
        near_in = near(half_in, 1)
        near_out = [near(half_out, k) for k in (2, 4, 6)]

    with jax.named_scope("cot"):
        chunk_shape = shaped(8 * ROWS, 6 * BS, dtype=BF16)
        first, *others = call(
            cot_kernel, [chunk_shape] * N_CH, cot, place=place,
            scratch=[pltpu.VMEM((ROWS, W, BS), F32)],
        )
        cot_chunks = [first] + [near(part, k + 1) for k, part in enumerate(others)]

    with jax.named_scope("stats"):
        stats = gathered[:, :16]
        gains = gathered[:, 16:17, :BS]

    scratch = pltpu.VMEM((LANES // 128, 8 * N_LAT, 128), F32)
    wire_shape = shaped(8 * N_LAT, LANES, dtype=BF16)
    with jax.named_scope("lon"):
        wire = call(
            lon_kernel, wire_shape, x, stats, gain_column, t_high, t_low, scratch=[scratch]
        )
        wire = lax.all_to_all(wire, "lat", 0, 0, tiled=True)

    with jax.named_scope("weights"):
        pair = jnp.stack([half_in, near_in])
        own_in = [pair] + [near(pair, k) for k in (2, 4, 6)]
        quad = jnp.stack([half_out] + near_out)
        own_out = [quad, near(quad, 1)]

    with jax.named_scope("matrices"):
        m1 = split(
            jnp.concatenate(
                [block_matrix(w_inner, False, False), block_matrix(w_inner, False, True)], axis=0
            )
        )
        m2 = split(
            jnp.concatenate(
                [block_matrix(w_outer, False, False), block_matrix(w_outer, True, False)], axis=1
            )
        )
        lane = jnp.arange(LANES, dtype=jnp.int32)[None]
        doubled = jnp.where((lat == 0) & (lane < 2 * BS), 1.0, 2.0).astype(F32)

    table_specs = [whole((H, 512)), whole((H, 512)), whole((GROUP, GROUP))]
    inverse_specs = [lane_block(1), whole((256, 448)), whole((256, 448))]
    params = pltpu.CompilerParams(vmem_limit_bytes=VMEM_BYTES)
    with jax.named_scope("spectral"):
        wire, spectrum, pre_modes = pl.pallas_call(
            spectral_kernel,
            grid=(3,),
            in_specs=[lane_block(256)]
            + table_specs
            + [whole((GROUP, GROUP))] * 2
            + [whole((GROUP, 2 * GROUP))] * 2
            + inverse_specs,
            out_specs=[lane_block(256), lane_block(H), lane_block(H)],
            out_shape=[wire_shape, shaped(H, LANES), shaped(H, LANES)],
            compiler_params=params,
            cost_estimate=cost(11),
        )(
            wire, lf_high, lf_low, swap, m1[0][:GROUP], m1[1][:GROUP], m2[0], m2[1], doubled,
            li_high, li_low,
        )
        own_in[1], own_in[3], wire = lax.optimization_barrier((own_in[1], own_in[3], wire))
        wire = lax.all_to_all(wire, "lat", 0, 0, tiled=True)
        own_in[2], own_out[1], *cot_chunks, wire = lax.optimization_barrier(
            (own_in[2], own_out[1], *cot_chunks, wire)
        )
        weights = own_in + own_out
        weights += [lax.ppermute(part, "lat", siblings) for part in weights]

    with jax.named_scope("mix"):
        mixed, chunks = call(
            mix_kernel,
            [shaped(ROWS, W, BS), shaped(N_CH, 8 * ROWS, 6 * BS)],
            wire, tt_high, tt_low, x, stats, gain_column,
            scratch=[scratch],
        )
        chunks = lax.all_to_all(chunks, "ch", 0, 0, tiled=True)

    cells = 48 * ROWS
    halved = pl.BlockSpec((2, 1, 384, 384), lambda p, place: (0, p, 0, 0))

    def all_of(shape):
        return pl.BlockSpec(shape, lambda e, place: (0,) * len(shape))

    with jax.named_scope("mlp"):
        *out_chunks, grad_chunks, in_own, in_other, out_own, out_other = pl.pallas_call(
            mlp_kernel,
            grid_spec=pltpu.PrefetchScalarGridSpec(
                num_scalar_prefetch=1,
                grid=(4,),
                in_specs=[
                    all_of((N_CH, 8 * ROWS, 6 * BS)),
                    all_of((N_CH, 1, BS)),
                ]
                + [all_of((8 * ROWS, 6 * BS))] * N_CH
                + [pl.BlockSpec(memory_space=pl.ANY)] * 12,
                out_specs=[all_of((8 * ROWS, 6 * BS))] * N_CH
                + [
                    all_of((N_CH, 8 * ROWS + 8, 6 * BS)),
                    halved,
                    halved,
                    halved,
                    halved,
                ],
                scratch_shapes=[
                    pltpu.VMEM((cells, C), F32),
                    pltpu.VMEM((cells, C), BF16),
                    pltpu.VMEM((cells, C), BF16),
                    pltpu.VMEM((cells, 128), F32),
                    pltpu.VMEM((cells, C), F32),
                    pltpu.VMEM((cells, C), F32),
                    pltpu.VMEM((4, C, C), BF16),
                    pltpu.VMEM((4, C, C), BF16),
                    pltpu.VMEM((N_CH, 8 * ROWS, 6 * BS), F32),
                    pltpu.SemaphoreType.DMA((32,)),
                ],
            ),
            out_shape=[chunk_shape] * N_CH
            + [
                shaped(N_CH, 8 * ROWS + 8, 6 * BS, dtype=BF16),
                shaped(2, 4, 384, 384),
                shaped(2, 4, 384, 384, dtype=BF16),
                shaped(2, 4, 384, 384),
                shaped(2, 4, 384, 384, dtype=BF16),
            ],
            compiler_params=params,
            cost_estimate=cost(20),
        )(place, chunks, gains, *cot_chunks, *weights)
        grad_chunks = lax.all_to_all(grad_chunks, "ch", 0, 0, tiled=True)

    with jax.named_scope("grads_ch"):
        theirs_in = lax.ppermute(in_other, "lat", siblings)
        theirs_out = lax.ppermute(out_other, "lat", siblings)

        def merged(part, rows):
            own, theirs = (in_own, theirs_in) if part == 2 else (out_own[part], theirs_out[part])
            own, theirs = (own[1], theirs[1]) if part == 2 else (own[rows], theirs[rows])
            return own + theirs.astype(F32)

        odd = merged(2, None).astype(BF16)
        one = merged(0, slice(1, 3)).astype(BF16)
        two = merged(1, slice(2, 4)).astype(BF16)
        *_, grad_chunks = lax.optimization_barrier((odd, one, two, grad_chunks))
        odd, one, two = near(odd, 1), near(one, 2), near(two, 6)

    with jax.named_scope("lon_back"):
        wire, grad_mixed, gain_parts = call(
            lon_back_kernel,
            [wire_shape, shaped(ROWS, BS, W, dtype=BF16), shaped(8, 128)],
            grad_chunks, x, stats, t_high, t_low,
            scratch=[scratch],
        )
        wire = lax.all_to_all(wire, "lat", 0, 0, tiled=True)

    with jax.named_scope("grads_ch"):
        one_next = near((merged(0, 3) + one[1].astype(F32)).astype(BF16), 6)
        two_next = near((merged(1, 1) + two[0].astype(F32)).astype(BF16), 2)
        odd, one, two, one_next, two_next, wire = lax.optimization_barrier(
            (odd, one, two, one_next, two_next, wire)
        )
        even = in_own[0, 1:] + theirs_in[0, 1:].astype(F32) + odd[1:].astype(F32)
        even = even.astype(BF16)
        in_parts = [near(even[k // 2 - 1], k) for k in (2, 4, 6)]
        far = merged(1, 0) + two[1].astype(F32) + two_next.astype(F32)
        out_part = near(far.astype(BF16), 1)

    with jax.named_scope("spectral_back"):
        wire, small = pl.pallas_call(
            spectral_back_kernel,
            grid=(3,),
            in_specs=[lane_block(256), lane_block(H), lane_block(H)]
            + table_specs
            + [whole((2 * GROUP, GROUP))] * 2
            + [whole((GROUP, 2 * GROUP))] * 2
            + inverse_specs
            + [whole((1, BS)), whole((8, 128))],
            out_specs=[lane_block(256), whole((N_LAT + 8, LANES))],
            out_shape=[wire_shape, shaped(N_LAT + 8, LANES)],
            scratch_shapes=[
                pltpu.VMEM((GROUP, GROUP), F32),
                pltpu.VMEM((GROUP, GROUP), F32),
                pltpu.VMEM((8, 128), F32),
            ],
            compiler_params=params,
            cost_estimate=cost(14),
        )(
            wire, spectrum, pre_modes, lf_high, lf_low, swap, m1[0], m1[1], m2[0], m2[1], doubled,
            li_high, li_low, gain_first[None], gain_parts,
        )
        *in_parts, out_part, wire = lax.optimization_barrier((*in_parts, out_part, wire))

    with jax.named_scope("pack"):
        corner = pl.BlockSpec((1, 1, 384, 384), lambda g: (0, 0, 0, 0))
        front = pl.BlockSpec((1, 384, 384), lambda g: (0, 0, 0))
        flat = whole((384, 384))
        wire = pl.pallas_call(
            pack_kernel,
            grid=(1,),
            in_specs=[whole((256, LANES)), whole((N_LAT + 8, LANES))]
            + [corner, corner, front, flat, flat, flat]
            + [corner, corner, front, flat, flat],
            out_specs=whole((N_LAT, 16, LANES)),
            out_shape=shaped(N_LAT, 16, LANES, dtype=BF16),
            compiler_params=params,
            cost_estimate=cost(3),
        )(
            wire, small, in_own, theirs_in, odd, *in_parts, out_own, theirs_out, one, one_next,
            out_part,
        )
        *out_chunks, wire = lax.optimization_barrier((*out_chunks, wire))
        wire = lax.all_to_all(wire, "lat", 0, 0, tiled=True)

    with jax.named_scope("output"):
        first, *others = out_chunks
        out_chunks = [first] + [near(part, k + 1) for k, part in enumerate(others)]
        output = call(
            output_kernel, shaped(ROWS, BS, W, dtype=BF16), mixed, *out_chunks, place=place,
            scratch=[pltpu.VMEM((N_CH, 8 * ROWS, 6 * BS), F32)],
        )
        output, wire = lax.optimization_barrier((output, wire))

    with jax.named_scope("unmix"):
        scaled, sums = call(
            unmix_kernel,
            [shaped(ROWS, BS, W), shaped(16, W)],
            wire, tt_high, tt_low, grad_mixed, x, stats, gain_column,
            scratch=[scratch],
        )
    with jax.named_scope("sums"):
        sums = [sums] + [near(sums, k) for k in range(1, N_CH)]

    with jax.named_scope("grads_lat"):
        payload = call(spread_kernel, shaped(N_LAT // 2, 56, GROUP, dtype=BF16), wire, small)
        mine = lax.all_to_all(payload, "lat", 0, 0, tiled=True, axis_index_groups=cores)
        mine, *sums = lax.optimization_barrier((mine, *sums))
        theirs = lax.ppermute(mine, "lat", siblings)
        weight_shape = shaped(2, 1, BS, BS)
        grad_fc_in, grad_fc_out, grad_w_inner, grad_w_outer, grad_first, grad_second = call(
            finish_kernel,
            [
                shaped(C, FF_DEV),
                shaped(FF_DEV, C),
                weight_shape,
                weight_shape,
                shaped(1, BS),
                shaped(1, BS),
            ],
            mine, theirs, place=place,
        )

    with jax.named_scope("final"):
        grad_fields = call(
            final_kernel, shaped(ROWS, BS, W, dtype=BF16), scaled, grad_mixed, x, stats, *sums
        )

    return (
        output.transpose(1, 0, 2),
        grad_fields.transpose(1, 0, 2),
        grad_first[0],
        grad_w_inner,
        grad_w_outer,
        grad_second[0],
        grad_fc_in,
        grad_fc_out,
    )


def solution(mesh):
    placed = (
        P("ch", "lat", None),
        P("ch"),
        P(None, "ch", None, None),
        P(None, "ch", None, None),
        P("ch"),
        P(None, "ch"),
        P("ch", None),
        P("ch", "lat", None),
    )
    return jax.shard_map(
        body,
        mesh=mesh,
        in_specs=placed,
        out_specs=(
            P("ch", "lat", None),
            P("ch", "lat", None),
            P("ch"),
            P(None, "ch", None, None),
            P(None, "ch", None, None),
            P("ch"),
            P(None, "ch"),
            P("ch", None),
        ),
        check_vma=False,
    )
```

```python
import math

import jax
import jax.numpy as jnp
import ml_dtypes
import numpy as np
from jax import lax
from jax.experimental import pallas as pl
from jax.experimental.pallas import tpu as pltpu
from jax.sharding import PartitionSpec as P

C = 768
BS = 96
H = 224
W = 384
KW = 192
N_LAT = 32
N_CH = 8
ROWS = 7
FF_DEV = 384
MODES = KW // N_LAT
PLANES = 2 * MODES
LANES = PLANES * BS
GROUP = 384
EPSILON = 1e-05
BF16 = jnp.bfloat16
F32 = jnp.float32
VMEM_BYTES = 56 * 1024 * 1024


def halves(table):
    high = table.astype(ml_dtypes.bfloat16)
    low = (table - high.astype(np.float64)).astype(ml_dtypes.bfloat16)
    return high, low


def lon_table():
    mode = np.arange(MODES)[:, None] + MODES * np.arange(N_LAT)[None, :]
    angles = 2 * np.pi * ((mode[:, :, None] * np.arange(W)) % W) / W
    table = np.stack([np.cos(angles), -np.sin(angles)], 1) / math.sqrt(W)
    return table.reshape(PLANES * N_LAT, W)


def lat_tables():
    index = np.arange(H)
    angles = 2 * np.pi * ((index[:, None] * index[None, :]) % H) / H
    cosine = np.cos(angles) / math.sqrt(H)
    sine = np.sin(angles) / math.sqrt(H)
    forward = np.zeros((H, 2, N_LAT, 8))
    forward[:, 0, :, :ROWS] = cosine.reshape(H, N_LAT, ROWS)
    forward[:, 1, :, :ROWS] = sine.reshape(H, N_LAT, ROWS)
    inverse = np.zeros((N_LAT, 8, 2, H))
    inverse[:, :ROWS, 0] = cosine.reshape(N_LAT, ROWS, H)
    inverse[:, :ROWS, 1] = -sine.reshape(N_LAT, ROWS, H)
    return forward.reshape(H, 2 * N_LAT * 8), inverse.reshape(N_LAT * 8, 2 * H)


def swap_table():
    table = np.zeros((GROUP, GROUP))
    for mode in range(2):
        for c in range(BS):
            real = mode * 2 * BS + c
            table[real + BS, real] = 1
            table[real, real + BS] = -1
    return table.astype(ml_dtypes.bfloat16)


def dot(left, right):
    return lax.dot_general(left, right, (((1,), (0,)), ((), ())), preferred_element_type=F32)


def dot_nt(left, right):
    return lax.dot_general(left, right, (((1,), (1,)), ((), ())), preferred_element_type=F32)


def dot_tn(left, right):
    return lax.dot_general(left, right, (((0,), (0,)), ((), ())), preferred_element_type=F32)


def split(values):
    high = values.astype(BF16)
    return high, (values - high.astype(F32)).astype(BF16)


def dot3(kind, left, right):
    return kind(left[0], right[0]) + kind(left[1], right[0]) + kind(left[0], right[1])


def gelu_parts(values):
    cdf = 0.5 * (1.0 + lax.erf(values * 0.7071067811865476))
    return values * cdf, cdf + values * 0.3989422804014327 * jnp.exp(-0.5 * values * values)


def gelu_value(values):
    return 0.5 * values * (1.0 + lax.erf(values * 0.7071067811865476))


def norm_rows(stats):
    total = stats[0]
    for e in range(1, N_CH):
        total = total + stats[e]
    average = total[0:8] * (1.0 / C)
    squares = total[8:16] * (1.0 / C)
    return average, lax.rsqrt(squares - average * average + EPSILON)


def put_row(scratch, row, modes):
    wide = jnp.concatenate([modes[32 * k : 32 * k + 32] for k in range(PLANES)], axis=1)
    for t in range(LANES // 128):
        scratch[t, pl.ds(row, N_LAT, stride=8), :] = wide[:, 128 * t : 128 * t + 128]


def flush_rows(scratch, wire):
    for t in range(LANES // 128):
        scratch[t, pl.ds(ROWS, N_LAT, stride=8), :] = jnp.zeros((N_LAT, 128), F32)
        wire[:, 128 * t : 128 * t + 128] = scratch[t].astype(BF16)


def load_rows(wire, scratch):
    for t in range(LANES // 128):
        scratch[t] = wire[:, 128 * t : 128 * t + 128].astype(F32)


def load_packed(wire, scratch):
    for t in range(LANES // 128):
        block = wire[:, :, 128 * t : 128 * t + 128].astype(F32)
        scratch[t] = block[:, :8].reshape(8 * N_LAT, 128)


def get_row(scratch, row):
    wide = jnp.concatenate(
        [scratch[t, pl.ds(row, N_LAT, stride=8), :] for t in range(LANES // 128)], axis=1
    )
    return jnp.concatenate([wide[:, BS * k : BS * k + BS] for k in range(PLANES)], axis=0)


def to_chunk(rows, e):
    return jnp.concatenate(
        [
            jnp.concatenate(
                [values[48 * e + 8 * a : 48 * e + 8 * a + 8] for a in range(6)], axis=1
            )
            for values in rows
        ],
        axis=0,
    )


def from_chunks(chunks, row):
    return jnp.concatenate(
        [
            chunk[8 * row : 8 * row + 8, BS * a : BS * a + BS]
            for chunk in chunks
            for a in range(6)
        ],
        axis=0,
    )


def cot_kernel(place, cot, *refs):
    chunks, scratch = refs[:N_CH], refs[N_CH]
    for r in range(ROWS):
        scratch[r] = cot[r].astype(F32).T
    for k in range(N_CH):
        cells = pl.ds(pl.multiple_of(48 * (place[1] ^ k), 8), 48)
        chunks[k][...] = to_chunk([scratch[r, cells] for r in range(ROWS)], 0).astype(BF16)


def lon_kernel(x, stats, gain, t_high, t_low, wire, scratch):
    average, inv_std = norm_rows(stats)
    table = (t_high[...], t_low[...])
    for r in range(ROWS):
        normed = (x[r].astype(F32) - average[r : r + 1]) * inv_std[r : r + 1]
        lifted = split(normed * gain[...])
        put_row(scratch, r, dot3(dot_nt, table, lifted))
    flush_rows(scratch, wire)


def lat_forward(wire, lf_high, lf_low, swap):
    values = wire[...]
    swapped = dot(values, swap[...]).astype(BF16)
    both = jnp.concatenate([values, swapped], axis=0)
    return dot(lf_high[...], both) + dot(lf_low[...], both)


def lat_inverse(modes, li_high, li_low):
    both = split(jnp.concatenate([modes[:, :GROUP], modes[:, GROUP:]], axis=0))
    return dot3(dot, (li_high[...], li_low[...]), both)


def weight_sum(blocks):
    def block(part, other):
        pieces = [
            blocks[m + BS * part : m + BS * part + BS, m + BS * other : m + BS * other + BS]
            for m in (0, 2 * BS)
        ]
        return pieces[0] + pieces[1]

    return jnp.concatenate(
        [block(0, 0) + block(1, 1), block(1, 0) - block(0, 1)], axis=0
    )


def spectral_kernel(
    wire, lf_high, lf_low, swap, m1_high, m1_low, m2_high, m2_low, doubled, li_high, li_low,
    out, spectrum, pre_modes,
):
    modes = lat_forward(wire, lf_high, lf_low, swap)
    spectrum[...] = modes
    pre = dot3(dot, split(modes), (m1_high[...], m1_low[...]))
    pre_modes[...] = pre
    act = split(gelu_value(pre))
    scale = doubled[...]
    result = dot3(dot, act, (m2_high[...], m2_low[...])) * jnp.concatenate([scale, scale], axis=1)
    out[...] = lat_inverse(result, li_high, li_low).astype(BF16)


def spectral_back_kernel(
    wire, spectrum, pre_modes, lf_high, lf_low, swap, m1_high, m1_low, m2_high, m2_low, doubled,
    li_high, li_low, gain, gain_parts, out, small, grad_outer, grad_inner, gain_sum,
):
    @pl.when(pl.program_id(0) == 0)
    def _():
        grad_outer[...] = jnp.zeros_like(grad_outer)
        grad_inner[...] = jnp.zeros_like(grad_inner)
        gain_sum[...] = jnp.zeros_like(gain_sum)

    grad = split(lat_forward(wire, lf_high, lf_low, swap) * doubled[...])
    act, slope = gelu_parts(pre_modes[...])
    grad_act = dot3(dot_nt, grad, (m2_high[:, :GROUP], m2_low[:, :GROUP]))
    grad_outer[...] += dot3(dot_tn, grad, split(act))
    grad_pre = split(grad_act * slope)
    modes = spectrum[...]
    grad_inner[...] += dot3(dot_tn, grad_pre, split(modes))
    grad_spectrum = dot3(dot_nt, grad_pre, (m1_high[...], m1_low[...]))
    gain_row = jnp.sum(grad_spectrum[:, :GROUP] * modes, axis=0, keepdims=True)
    gain_row = sum(gain_row[:, BS * k : BS * k + BS] for k in range(4))
    gain_sum[0:1, :BS] += gain_row
    out[...] = lat_inverse(grad_spectrum, li_high, li_low).astype(BF16)

    @pl.when(pl.program_id(0) == 2)
    def _():
        first = gain_sum[0:1, :BS] / gain[...] + gain_parts[0:1, :BS]
        weights = [weight_sum(grad_inner[...]), weight_sum(grad_outer[...])]
        small[:N_LAT] = jnp.concatenate(
            [weight[32 * q : 32 * q + 32] for weight in weights for q in range(6)], axis=1
        )
        row = []
        for values in (first, gain_parts[1:2, :BS]):
            high = values.astype(BF16).astype(F32)
            row += [high, values - high]
        row = jnp.concatenate(row + [jnp.zeros((1, 8 * BS), F32)], axis=1)
        small[N_LAT:] = jnp.concatenate([row, jnp.zeros((7, LANES), F32)], axis=0)


def mix_kernel(wire, tt_high, tt_low, x, stats, gain, mixed, chunks, scratch):
    average, inv_std = norm_rows(stats)
    load_rows(wire, scratch)
    rows = []
    for r in range(ROWS):
        x_float = x[r].astype(F32)
        lifted = (x_float - average[r : r + 1]) * inv_std[r : r + 1] * gain[...]
        modes = get_row(scratch, r).astype(BF16)
        filtered = dot(tt_high[...], modes) + dot(tt_low[...], modes)
        values = filtered + (lifted + x_float).T
        mixed[r] = values
        rows.append(values)
    for e in range(N_CH):
        chunks[e] = to_chunk(rows, e)


def mlp_kernel(core, mixed, gain, *refs):
    given_cots, weights, refs = refs[:8], refs[8:20], refs[20:]
    out_chunks, refs = refs[:8], refs[8:]
    grad_chunks, grad_in_own, grad_in_other, grad_out_own, grad_out_other = refs[:5]
    (
        normed, inputs, cots, inv_std, sum_out, sum_grad, weight_in, weight_out, chunk_rows, arrived,
    ) = refs[5:]
    step = pl.program_id(0)
    turn = 4 * core[0]
    cells = 6 * 8 * ROWS
    part = 8 * ROWS

    def gain_row():
        return jnp.concatenate([gain[e ^ turn] for e in range(N_CH)], axis=1)

    def copies(p):
        found = []
        for half in range(2):
            parts = weights[6 * half : 6 * half + 6]
            rows = pl.ds(384 * half, 384)
            for b in range(2):
                units = pl.ds(384 * b, 384)
                found.append((parts[p].at[b], weight_in.at[p, rows, units]))
                found.append((parts[4 + b].at[p], weight_out.at[p, units, rows]))
        return [
            pltpu.make_async_copy(source, target, arrived.at[8 * p + n])
            for n, (source, target) in enumerate(found)
        ]

    @pl.when(step == 0)
    def _():
        for p in range(4):
            for copy in copies(p):
                copy.start()
        pieces = [mixed[e ^ turn] for e in range(N_CH)]
        values = jnp.concatenate(
            [
                jnp.concatenate([piece[:, BS * a : BS * a + BS] for piece in pieces], axis=1)
                for a in range(6)
            ],
            axis=0,
        )
        average = jnp.sum(values, axis=1, keepdims=True) * (1.0 / C)
        squares = jnp.sum(values * values, axis=1, keepdims=True) * (1.0 / C)
        inv = lax.rsqrt(squares - average * average + EPSILON)
        values = (values - average) * inv
        normed[...] = values
        inv_std[...] = jnp.broadcast_to(inv, (cells, 128))
        inputs[...] = (values * gain_row()).astype(BF16)
        for k in range(N_CH):
            chunk_rows[k] = given_cots[k][...].astype(F32)
        pieces = [chunk_rows[e ^ turn ^ core[1]] for e in range(N_CH)]
        cots[...] = jnp.concatenate(
            [
                jnp.concatenate([piece[:, BS * a : BS * a + BS] for piece in pieces], axis=1)
                for a in range(6)
            ],
            axis=0,
        ).astype(BF16)
        sum_out[...] = jnp.zeros_like(sum_out)
        sum_grad[...] = jnp.zeros_like(sum_grad)

    for p in range(4):

        @pl.when(step == p)
        def _():
            for copy in copies(p):
                copy.wait()

    own_in, own_out = weight_in[step], weight_out[step]
    values, given = inputs[...], cots[...]
    hidden, slope = gelu_parts(dot(values, own_in))
    hidden = hidden.astype(BF16)
    grad_pre = (dot_nt(given, own_out) * slope).astype(BF16)
    sum_out[...] += dot(hidden, own_out)
    sum_grad[...] += dot_nt(grad_pre, own_in)
    grad_in = dot_tn(values, grad_pre)
    grad_out = dot_tn(hidden, given)
    for b in range(2):
        units = slice(384 * b, 384 * b + 384)
        grad_in_own[b, 0] = grad_in[:384, units]
        grad_in_other[b, 0] = grad_in[384:, units].astype(BF16)
        grad_out_own[b, 0] = grad_out[units, :384]
        grad_out_other[b, 0] = grad_out[units, 384:].astype(BF16)

    @pl.when(step == 3)
    def _():
        grad_input = sum_grad[...]
        values = normed[...]
        gain_sum = jnp.sum(grad_input * values, axis=0, keepdims=True)
        scaled = grad_input * gain_row()
        leading = jnp.sum(scaled, axis=1, keepdims=True) * (1.0 / C)
        paired = jnp.sum(scaled * values, axis=1, keepdims=True) * (1.0 / C)
        grad_mixed = cots[...].astype(F32) + inv_std[:, :1] * (scaled - leading - values * paired)
        outputs = sum_out[...]

        def chunk(array, e):
            return jnp.concatenate(
                [array[part * a : part * a + part, BS * e : BS * e + BS] for a in range(6)],
                axis=1,
            )

        for e in range(N_CH):
            chunk_rows[e ^ turn ^ core[1]] = chunk(outputs, e)
            gain_piece = gain_sum[:, BS * e : BS * e + BS]
            gain_high = gain_piece.astype(BF16).astype(F32)
            extra = jnp.concatenate(
                [gain_high, gain_piece - gain_high, jnp.zeros((1, 4 * BS), F32)], axis=1
            )
            extra = jnp.concatenate([extra, jnp.zeros((7, 6 * BS), F32)], axis=0)
            grad_chunks[e ^ turn] = jnp.concatenate(
                [chunk(grad_mixed, e), extra], axis=0
            ).astype(BF16)
        for k in range(N_CH):
            out_chunks[k][...] = chunk_rows[k].astype(BF16)


def lon_back_kernel(chunks, x, stats, t_high, t_low, wire, grad_mixed, gains, scratch):
    average, inv_std = norm_rows(stats)
    pieces = [chunks[e].astype(F32) for e in range(N_CH)]
    gain_first = jnp.zeros((BS, 1), F32)
    for r in range(ROWS):
        values = from_chunks(pieces, r)
        rounded = values.astype(BF16)
        put_row(scratch, r, dot(t_high[...], rounded) + dot(t_low[...], rounded))
        turned = values.T
        grad_mixed[r] = turned.astype(BF16)
        normed = (x[r].astype(F32) - average[r : r + 1]) * inv_std[r : r + 1]
        gain_first = gain_first + jnp.sum(turned * normed, axis=1, keepdims=True)
    flush_rows(scratch, wire)
    gain_second = jnp.zeros((1, BS), F32)
    for piece in pieces:
        row = piece[8 * ROWS : 8 * ROWS + 1]
        gain_second = gain_second + row[:, :BS] + row[:, BS : 2 * BS]
    turned_first = jnp.broadcast_to(gain_first, (BS, 128)).T[0:1, :]
    gains[0:1, :BS] = turned_first
    gains[1:2, :BS] = gain_second


def unmix_kernel(wire, tt_high, tt_low, grad_mixed, x, stats, gain, scaled, sums, scratch):
    average, inv_std = norm_rows(stats)
    load_packed(wire, scratch)
    for r in range(ROWS):
        modes = get_row(scratch, r).astype(BF16)
        back = dot(tt_high[...], modes) + dot(tt_low[...], modes)
        values = (back.T + grad_mixed[r].astype(F32)) * gain[...]
        normed = (x[r].astype(F32) - average[r : r + 1]) * inv_std[r : r + 1]
        scaled[r] = values
        sums[r : r + 1] = jnp.sum(values, axis=0, keepdims=True)
        sums[8 + r : 9 + r] = jnp.sum(values * normed, axis=0, keepdims=True)
    sums[7:8] = jnp.zeros((1, W), F32)
    sums[15:16] = jnp.zeros((1, W), F32)


def final_kernel(scaled, grad_mixed, x, stats, *rest):
    average, inv_std = norm_rows(stats)
    out = rest[-1]
    total = rest[0][...]
    for part in rest[1:-1]:
        total = total + part[...]
    total = total * (1.0 / C)
    for r in range(ROWS):
        inv = inv_std[r : r + 1]
        normed = (x[r].astype(F32) - average[r : r + 1]) * inv
        change = scaled[r] - total[r : r + 1] - normed * total[8 + r : 9 + r]
        out[r] = (grad_mixed[r].astype(F32) + inv * change).astype(BF16)


def pack_kernel(wire, small, *refs):
    out = refs[11]

    def add(parts):
        total = parts[0].astype(F32)
        for part in parts[1:]:
            total = total + part.astype(F32)
        return total

    total_in = add([refs[0][0, 0], refs[1][0, 0], refs[2][0]] + [part[...] for part in refs[3:6]])
    total_out = add([refs[6][0, 0], refs[7][0, 0], refs[8][0], refs[9][...], refs[10][...]])
    total = jnp.concatenate([total_in, total_out], axis=0)
    modes = wire[...].astype(F32).reshape(N_LAT, 8, LANES)
    weights = small[:N_LAT]
    row = lax.broadcasted_iota(jnp.int32, (N_LAT, 8, LANES), 1)
    modes = jnp.where(row == ROWS, weights[:, None, :], modes)
    grads = jnp.concatenate(
        [total[256 * g : 256 * g + 256].reshape(N_LAT, 8, GROUP) for g in range(3)], axis=2
    )
    out[...] = jnp.concatenate([modes, grads], axis=1).astype(BF16)


def spread_kernel(parts, small, out):
    sums = [parts[n].astype(F32) for n in (0, 1)]
    for n in range(2, N_LAT):
        sums[n % 2] = sums[n % 2] + parts[n].astype(F32)
    rows = [
        half[8:16, GROUP * g : GROUP * g + GROUP] for half in sums for g in range(3)
    ]
    weights = sums[0][ROWS : ROWS + 1] + sums[1][ROWS : ROWS + 1]
    last = [weights[:, GROUP * g : GROUP * g + GROUP] for g in range(3)]
    last += [small[N_LAT : N_LAT + 1, :GROUP], jnp.zeros((4, GROUP), F32)]
    total = jnp.concatenate(rows + [jnp.concatenate(last, axis=0)], axis=0).astype(BF16)
    for n in range(N_LAT // 2):
        out[n] = total


def finish_kernel(
    place, mine, theirs, grad_in, grad_out, grad_inner, grad_outer, gain_first, gain_second
):
    first = place[0] == 0
    one, two = mine[...].astype(F32), theirs[...].astype(F32)
    even, odd = jnp.where(first, one, two), jnp.where(first, two, one)

    def rows(start):
        parts = [part[:, start : start + 8][:, None] for part in (even, odd)]
        return jnp.concatenate(parts, axis=1).reshape(256, GROUP)

    for half in range(2):
        total = jnp.concatenate([rows(24 * half + 8 * g) for g in range(3)], axis=0)
        grad_in[384 * half : 384 * half + 384] = total[:384]
        grad_out[:, 384 * half : 384 * half + 384] = total[384:]
    last = rows(48)
    planes = [
        jnp.concatenate([last[8 * n + g : 8 * n + g + 1] for n in range(N_LAT)], axis=0)
        for g in range(4)
    ]
    weights = [
        plane[:, BS * q : BS * q + BS] for plane in planes[:3] for q in range(4)
    ]
    for part in range(2):
        grad_inner[part, 0] = jnp.concatenate(weights[3 * part : 3 * part + 3], axis=0)
        grad_outer[part, 0] = jnp.concatenate(weights[6 + 3 * part : 9 + 3 * part], axis=0)
    gains = jnp.sum(planes[3], axis=0, keepdims=True)
    gain_first[...] = gains[:, :BS] + gains[:, BS : 2 * BS]
    gain_second[...] = gains[:, 2 * BS : 3 * BS] + gains[:, 3 * BS :]


def output_kernel(place, mixed, *refs):
    chunks, out, chunk_rows = refs[:N_CH], refs[N_CH], refs[N_CH + 1]
    for k in range(N_CH):
        chunk_rows[k] = chunks[k][...].astype(F32)
    pieces = [chunk_rows[e ^ place[1]] for e in range(N_CH)]
    for r in range(ROWS):
        out[r] = (from_chunks(pieces, r) + mixed[r]).T.astype(BF16)


def cost(micros):
    return pl.CostEstimate(
        flops=int(micros * 1.0e9), bytes_accessed=int(micros * 2.0e6), transcendentals=0
    )


def call(kernel, out_shape, *args, scratch=(), micros=3, place=None):
    specs = [pl.BlockSpec(memory_space=pltpu.VMEM)] * len(args)
    if place is not None:
        args = (place,) + args
        specs = [pl.BlockSpec(memory_space=pltpu.SMEM)] + specs
    return pl.pallas_call(
        kernel,
        out_shape=out_shape,
        in_specs=specs,
        scratch_shapes=scratch,
        compiler_params=pltpu.CompilerParams(vmem_limit_bytes=VMEM_BYTES),
        cost_estimate=cost(micros),
    )(*args)


def shaped(*shape, dtype=F32):
    return jax.ShapeDtypeStruct(shape, dtype)


def whole(shape):
    return pl.BlockSpec(shape, lambda g: (0,) * len(shape))


def lane_block(rows):
    return pl.BlockSpec((rows, GROUP), lambda g: (0, g))


def block_matrix(weight, swap_columns, swap_rows):
    real, imag = weight[0, 0].T, weight[1, 0].T
    base = [[real, imag], [-imag, real]]
    if swap_columns:
        base = [[imag, -real], [real, imag]]
    if swap_rows:
        base = [[-imag, real], [-real, -imag]]
    one = jnp.concatenate([jnp.concatenate(line, axis=1) for line in base], axis=0)
    zero = jnp.zeros_like(one)
    return jnp.concatenate(
        [jnp.concatenate([one, zero], axis=1), jnp.concatenate([zero, one], axis=1)], axis=0
    )


def to_all(values, axis, count, **kwargs):
    spread = jnp.broadcast_to(values[None], (count,) + values.shape)
    return lax.all_to_all(spread, axis, 0, 0, tiled=True, **kwargs)


def near(values, k):
    return lax.ppermute(values, "ch", [(i, i ^ k) for i in range(N_CH)])


def body(fields, gain_first, w_inner, w_outer, gain_second, fc_in, fc_out, cotangent):
    lat = lax.axis_index("lat")
    core = lat % 2
    me = lax.axis_index("ch")
    place = jnp.stack([core, me]).astype(jnp.int32)
    siblings = [(i, i ^ 1) for i in range(N_LAT)]
    cores = [list(range(0, N_LAT, 2)), list(range(1, N_LAT, 2))]
    t_high, t_low = (jnp.asarray(t) for t in halves(lon_table()))
    tt_high, tt_low = (jnp.asarray(t) for t in halves(lon_table().T))
    forward, inverse = lat_tables()
    lf_high, lf_low = (jnp.asarray(t) for t in halves(forward))
    li_high, li_low = (jnp.asarray(t) for t in halves(inverse))
    swap = jnp.asarray(swap_table())

    x = fields.transpose(1, 0, 2)
    cot = cotangent.transpose(1, 0, 2)
    gain_column = gain_first[:, None]

    with jax.named_scope("stats"):
        x_float = x.astype(F32)
        zero = jnp.zeros((1, W), F32)
        payload = jnp.concatenate(
            [
                jnp.sum(x_float, 1),
                zero,
                jnp.sum(x_float * x_float, 1),
                zero,
                jnp.pad(gain_second, (0, W - BS))[None],
                jnp.zeros((7, W), F32),
            ],
            axis=0,
        )
        gathered = to_all(payload, "ch", N_CH)
        gathered, fc_in, fc_out, cot = lax.optimization_barrier((gathered, fc_in, fc_out, cot))

    with jax.named_scope("weights"):
        half_in = lax.dynamic_slice_in_dim(fc_in, core * 384, 384, 0)
        half_out = lax.dynamic_slice_in_dim(fc_out, core * 384, 384, 1)
        near_in = near(half_in, 1)
        near_out = [near(half_out, k) for k in (2, 4, 6)]

    with jax.named_scope("cot"):
        chunk_shape = shaped(8 * ROWS, 6 * BS, dtype=BF16)
        first, *others = call(
            cot_kernel, [chunk_shape] * N_CH, cot, place=place,
            scratch=[pltpu.VMEM((ROWS, W, BS), F32)],
        )
        cot_chunks = [first] + [near(part, k + 1) for k, part in enumerate(others)]

    with jax.named_scope("stats"):
        stats = gathered[:, :16]
        gains = gathered[:, 16:17, :BS]

    scratch = pltpu.VMEM((LANES // 128, 8 * N_LAT, 128), F32)
    wire_shape = shaped(8 * N_LAT, LANES, dtype=BF16)
    with jax.named_scope("lon"):
        wire = call(
            lon_kernel, wire_shape, x, stats, gain_column, t_high, t_low, scratch=[scratch]
        )
        wire = lax.all_to_all(wire, "lat", 0, 0, tiled=True)

    with jax.named_scope("weights"):
        pair = jnp.stack([half_in, near_in])
        own_in = [pair] + [near(pair, k) for k in (2, 4, 6)]
        quad = jnp.stack([half_out] + near_out)
        own_out = [quad, near(quad, 1)]

    with jax.named_scope("matrices"):
        m1 = split(
            jnp.concatenate(
                [block_matrix(w_inner, False, False), block_matrix(w_inner, False, True)], axis=0
            )
        )
        m2 = split(
            jnp.concatenate(
                [block_matrix(w_outer, False, False), block_matrix(w_outer, True, False)], axis=1
            )
        )
        lane = jnp.arange(LANES, dtype=jnp.int32)[None]
        doubled = jnp.where((lat == 0) & (lane < 2 * BS), 1.0, 2.0).astype(F32)

    table_specs = [whole((H, 512)), whole((H, 512)), whole((GROUP, GROUP))]
    inverse_specs = [lane_block(1), whole((256, 448)), whole((256, 448))]
    params = pltpu.CompilerParams(vmem_limit_bytes=VMEM_BYTES)
    with jax.named_scope("spectral"):
        wire, spectrum, pre_modes = pl.pallas_call(
            spectral_kernel,
            grid=(3,),
            in_specs=[lane_block(256)]
            + table_specs
            + [whole((GROUP, GROUP))] * 2
            + [whole((GROUP, 2 * GROUP))] * 2
            + inverse_specs,
            out_specs=[lane_block(256), lane_block(H), lane_block(H)],
            out_shape=[wire_shape, shaped(H, LANES), shaped(H, LANES)],
            compiler_params=params,
            cost_estimate=cost(11),
        )(
            wire, lf_high, lf_low, swap, m1[0][:GROUP], m1[1][:GROUP], m2[0], m2[1], doubled,
            li_high, li_low,
        )
        own_in[1], own_in[3], wire = lax.optimization_barrier((own_in[1], own_in[3], wire))
        wire = lax.all_to_all(wire, "lat", 0, 0, tiled=True)
        own_in[2], own_out[1], *cot_chunks[:5], wire = lax.optimization_barrier(
            (own_in[2], own_out[1], *cot_chunks[:5], wire)
        )
        weights = own_in + own_out
        weights += [lax.ppermute(part, "lat", siblings) for part in weights]

    with jax.named_scope("mix"):
        mixed, chunks = call(
            mix_kernel,
            [shaped(ROWS, W, BS), shaped(N_CH, 8 * ROWS, 6 * BS)],
            wire, tt_high, tt_low, x, stats, gain_column,
            scratch=[scratch],
        )
        chunks = lax.all_to_all(chunks, "ch", 0, 0, tiled=True)

    cells = 48 * ROWS
    halved = pl.BlockSpec((2, 1, 384, 384), lambda p, place: (0, p, 0, 0))

    def all_of(shape):
        return pl.BlockSpec(shape, lambda e, place: (0,) * len(shape))

    with jax.named_scope("mlp"):
        *out_chunks, grad_chunks, in_own, in_other, out_own, out_other = pl.pallas_call(
            mlp_kernel,
            grid_spec=pltpu.PrefetchScalarGridSpec(
                num_scalar_prefetch=1,
                grid=(4,),
                in_specs=[
                    all_of((N_CH, 8 * ROWS, 6 * BS)),
                    all_of((N_CH, 1, BS)),
                ]
                + [all_of((8 * ROWS, 6 * BS))] * N_CH
                + [pl.BlockSpec(memory_space=pl.ANY)] * 12,
                out_specs=[all_of((8 * ROWS, 6 * BS))] * N_CH
                + [
                    all_of((N_CH, 8 * ROWS + 8, 6 * BS)),
                    halved,
                    halved,
                    halved,
                    halved,
                ],
                scratch_shapes=[
                    pltpu.VMEM((cells, C), F32),
                    pltpu.VMEM((cells, C), BF16),
                    pltpu.VMEM((cells, C), BF16),
                    pltpu.VMEM((cells, 128), F32),
                    pltpu.VMEM((cells, C), F32),
                    pltpu.VMEM((cells, C), F32),
                    pltpu.VMEM((4, C, C), BF16),
                    pltpu.VMEM((4, C, C), BF16),
                    pltpu.VMEM((N_CH, 8 * ROWS, 6 * BS), F32),
                    pltpu.SemaphoreType.DMA((32,)),
                ],
            ),
            out_shape=[chunk_shape] * N_CH
            + [
                shaped(N_CH, 8 * ROWS + 8, 6 * BS, dtype=BF16),
                shaped(2, 4, 384, 384),
                shaped(2, 4, 384, 384, dtype=BF16),
                shaped(2, 4, 384, 384),
                shaped(2, 4, 384, 384, dtype=BF16),
            ],
            compiler_params=params,
            cost_estimate=cost(20),
        )(place, chunks, gains, *cot_chunks, *weights)
        grad_chunks = lax.all_to_all(grad_chunks, "ch", 0, 0, tiled=True)

    with jax.named_scope("grads_ch"):
        theirs_in = lax.ppermute(in_other, "lat", siblings)
        theirs_out = lax.ppermute(out_other, "lat", siblings)

        def merged(part, rows):
            return out_own[part, rows] + theirs_out[part, rows].astype(F32)

        odd = (in_own[1] + theirs_in[1].astype(F32)).astype(BF16)
        one = merged(0, slice(1, 3)).astype(BF16)
        two = merged(1, slice(2, 4)).astype(BF16)
        *_, grad_chunks = lax.optimization_barrier((odd, one, two, grad_chunks))
        odd, one, two = near(odd, 1), near(one, 2), near(two, 6)

    with jax.named_scope("lon_back"):
        wire, grad_mixed, gain_parts = call(
            lon_back_kernel,
            [wire_shape, shaped(ROWS, BS, W, dtype=BF16), shaped(8, 128)],
            grad_chunks, x, stats, t_high, t_low,
            scratch=[scratch],
        )
        wire = lax.all_to_all(wire, "lat", 0, 0, tiled=True)

    with jax.named_scope("grads_ch"):
        one_next = near((merged(0, 3) + one[1].astype(F32)).astype(BF16), 6)
        two_next = near((merged(1, 1) + two[0].astype(F32)).astype(BF16), 2)
        even = in_own[0, 1:] + theirs_in[0, 1:].astype(F32) + odd[1:].astype(F32)
        even = even.astype(BF16)
        far = (merged(1, 0) + two[1].astype(F32) + two_next.astype(F32)).astype(BF16)
        in_parts = [near(even[k // 2 - 1], k) for k in (2, 4, 6)]
        out_part = near(far, 1)
        one_next, even, far, wire = lax.optimization_barrier((one_next, even, far, wire))

    with jax.named_scope("spectral_back"):
        wire, small = pl.pallas_call(
            spectral_back_kernel,
            grid=(3,),
            in_specs=[lane_block(256), lane_block(H), lane_block(H)]
            + table_specs
            + [whole((2 * GROUP, GROUP))] * 2
            + [whole((GROUP, 2 * GROUP))] * 2
            + inverse_specs
            + [whole((1, BS)), whole((8, 128))],
            out_specs=[lane_block(256), whole((N_LAT + 8, LANES))],
            out_shape=[wire_shape, shaped(N_LAT + 8, LANES)],
            scratch_shapes=[
                pltpu.VMEM((GROUP, GROUP), F32),
                pltpu.VMEM((GROUP, GROUP), F32),
                pltpu.VMEM((8, 128), F32),
            ],
            compiler_params=params,
            cost_estimate=cost(14),
        )(
            wire, spectrum, pre_modes, lf_high, lf_low, swap, m1[0], m1[1], m2[0], m2[1], doubled,
            li_high, li_low, gain_first[None], gain_parts,
        )
        *in_parts, out_part, wire = lax.optimization_barrier((*in_parts, out_part, wire))

    with jax.named_scope("pack"):
        corner = pl.BlockSpec((1, 1, 384, 384), lambda g: (0, 0, 0, 0))
        front = pl.BlockSpec((1, 384, 384), lambda g: (0, 0, 0))
        flat = whole((384, 384))
        wire = pl.pallas_call(
            pack_kernel,
            grid=(1,),
            in_specs=[whole((256, LANES)), whole((N_LAT + 8, LANES))]
            + [corner, corner, front, flat, flat, flat]
            + [corner, corner, front, flat, flat],
            out_specs=whole((N_LAT, 16, LANES)),
            out_shape=shaped(N_LAT, 16, LANES, dtype=BF16),
            compiler_params=params,
            cost_estimate=cost(3),
        )(
            wire, small, in_own, theirs_in, odd, *in_parts, out_own, theirs_out, one, one_next,
            out_part,
        )
        *out_chunks, wire = lax.optimization_barrier((*out_chunks, wire))
        wire = lax.all_to_all(wire, "lat", 0, 0, tiled=True)

    with jax.named_scope("output"):
        first, *others = out_chunks
        out_chunks = [first] + [near(part, k + 1) for k, part in enumerate(others)]
        output = call(
            output_kernel, shaped(ROWS, BS, W, dtype=BF16), mixed, *out_chunks, place=place,
            scratch=[pltpu.VMEM((N_CH, 8 * ROWS, 6 * BS), F32)],
        )
        output, wire = lax.optimization_barrier((output, wire))

    with jax.named_scope("unmix"):
        scaled, sums = call(
            unmix_kernel,
            [shaped(ROWS, BS, W), shaped(16, W)],
            wire, tt_high, tt_low, grad_mixed, x, stats, gain_column,
            scratch=[scratch],
        )
    with jax.named_scope("sums"):
        sums = [sums] + [near(sums, k) for k in range(1, N_CH)]

    with jax.named_scope("grads_lat"):
        payload = call(spread_kernel, shaped(N_LAT // 2, 56, GROUP, dtype=BF16), wire, small)
        mine = lax.all_to_all(payload, "lat", 0, 0, tiled=True, axis_index_groups=cores)
        mine, *sums = lax.optimization_barrier((mine, *sums))
        theirs = lax.ppermute(mine, "lat", siblings)
        weight_shape = shaped(2, 1, BS, BS)
        grad_fc_in, grad_fc_out, grad_w_inner, grad_w_outer, grad_first, grad_second = call(
            finish_kernel,
            [
                shaped(C, FF_DEV),
                shaped(FF_DEV, C),
                weight_shape,
                weight_shape,
                shaped(1, BS),
                shaped(1, BS),
            ],
            mine, theirs, place=place,
        )

    with jax.named_scope("final"):
        grad_fields = call(
            final_kernel, shaped(ROWS, BS, W, dtype=BF16), scaled, grad_mixed, x, stats, *sums
        )

    return (
        output.transpose(1, 0, 2),
        grad_fields.transpose(1, 0, 2),
        grad_first[0],
        grad_w_inner,
        grad_w_outer,
        grad_second[0],
        grad_fc_in,
        grad_fc_out,
    )


def solution(mesh):
    placed = (
        P("ch", "lat", None),
        P("ch"),
        P(None, "ch", None, None),
        P(None, "ch", None, None),
        P("ch"),
        P(None, "ch"),
        P("ch", None),
        P("ch", "lat", None),
    )
    return jax.shard_map(
        body,
        mesh=mesh,
        in_specs=placed,
        out_specs=(
            P("ch", "lat", None),
            P("ch", "lat", None),
            P("ch"),
            P(None, "ch", None, None),
            P(None, "ch", None, None),
            P("ch"),
            P(None, "ch"),
            P("ch", None),
        ),
        check_vma=False,
    )
```

```python
import math

import jax
import jax.numpy as jnp
import ml_dtypes
import numpy as np
from jax import lax
from jax.experimental import pallas as pl
from jax.experimental.pallas import tpu as pltpu
from jax.sharding import PartitionSpec as P

C = 768
BS = 96
H = 224
W = 384
KW = 192
N_LAT = 32
N_CH = 8
ROWS = 7
FF_DEV = 384
MODES = KW // N_LAT
PLANES = 2 * MODES
LANES = PLANES * BS
GROUP = 384
EPSILON = 1e-05
BF16 = jnp.bfloat16
F32 = jnp.float32
VMEM_BYTES = 56 * 1024 * 1024


def halves(table):
    high = table.astype(ml_dtypes.bfloat16)
    low = (table - high.astype(np.float64)).astype(ml_dtypes.bfloat16)
    return high, low


def lon_table():
    mode = np.arange(MODES)[:, None] + MODES * np.arange(N_LAT)[None, :]
    angles = 2 * np.pi * ((mode[:, :, None] * np.arange(W)) % W) / W
    table = np.stack([np.cos(angles), -np.sin(angles)], 1) / math.sqrt(W)
    return table.reshape(PLANES * N_LAT, W)


def lat_tables():
    index = np.arange(H)
    angles = 2 * np.pi * ((index[:, None] * index[None, :]) % H) / H
    cosine = np.cos(angles) / math.sqrt(H)
    sine = np.sin(angles) / math.sqrt(H)
    forward = np.zeros((H, 2, N_LAT, 8))
    forward[:, 0, :, :ROWS] = cosine.reshape(H, N_LAT, ROWS)
    forward[:, 1, :, :ROWS] = sine.reshape(H, N_LAT, ROWS)
    inverse = np.zeros((N_LAT, 8, 2, H))
    inverse[:, :ROWS, 0] = cosine.reshape(N_LAT, ROWS, H)
    inverse[:, :ROWS, 1] = -sine.reshape(N_LAT, ROWS, H)
    return forward.reshape(H, 2 * N_LAT * 8), inverse.reshape(N_LAT * 8, 2 * H)


def swap_table():
    table = np.zeros((GROUP, GROUP))
    for mode in range(2):
        for c in range(BS):
            real = mode * 2 * BS + c
            table[real + BS, real] = 1
            table[real, real + BS] = -1
    return table.astype(ml_dtypes.bfloat16)


def dot(left, right):
    return lax.dot_general(left, right, (((1,), (0,)), ((), ())), preferred_element_type=F32)


def dot_nt(left, right):
    return lax.dot_general(left, right, (((1,), (1,)), ((), ())), preferred_element_type=F32)


def dot_tn(left, right):
    return lax.dot_general(left, right, (((0,), (0,)), ((), ())), preferred_element_type=F32)


def split(values):
    high = values.astype(BF16)
    return high, (values - high.astype(F32)).astype(BF16)


def dot3(kind, left, right):
    return kind(left[0], right[0]) + kind(left[1], right[0]) + kind(left[0], right[1])


def gelu_parts(values):
    cdf = 0.5 * (1.0 + lax.erf(values * 0.7071067811865476))
    return values * cdf, cdf + values * 0.3989422804014327 * jnp.exp(-0.5 * values * values)


def gelu_value(values):
    return 0.5 * values * (1.0 + lax.erf(values * 0.7071067811865476))


def norm_rows(stats):
    total = stats[0]
    for e in range(1, N_CH):
        total = total + stats[e]
    average = total[0:8] * (1.0 / C)
    squares = total[8:16] * (1.0 / C)
    return average, lax.rsqrt(squares - average * average + EPSILON)


def put_row(scratch, row, modes):
    wide = jnp.concatenate([modes[32 * k : 32 * k + 32] for k in range(PLANES)], axis=1)
    for t in range(LANES // 128):
        scratch[t, pl.ds(row, N_LAT, stride=8), :] = wide[:, 128 * t : 128 * t + 128]


def flush_rows(scratch, wire):
    for t in range(LANES // 128):
        scratch[t, pl.ds(ROWS, N_LAT, stride=8), :] = jnp.zeros((N_LAT, 128), F32)
        wire[:, 128 * t : 128 * t + 128] = scratch[t].astype(BF16)


def load_rows(wire, scratch):
    for t in range(LANES // 128):
        scratch[t] = wire[:, 128 * t : 128 * t + 128].astype(F32)


def load_packed(wire, scratch):
    for t in range(LANES // 128):
        block = wire[:, :, 128 * t : 128 * t + 128].astype(F32)
        scratch[t] = block[:, :8].reshape(8 * N_LAT, 128)


def get_row(scratch, row):
    wide = jnp.concatenate(
        [scratch[t, pl.ds(row, N_LAT, stride=8), :] for t in range(LANES // 128)], axis=1
    )
    return jnp.concatenate([wide[:, BS * k : BS * k + BS] for k in range(PLANES)], axis=0)


def to_chunk(rows, e):
    return jnp.concatenate(
        [
            jnp.concatenate(
                [values[48 * e + 8 * a : 48 * e + 8 * a + 8] for a in range(6)], axis=1
            )
            for values in rows
        ],
        axis=0,
    )


def from_chunks(chunks, row):
    return jnp.concatenate(
        [
            chunk[8 * row : 8 * row + 8, BS * a : BS * a + BS]
            for chunk in chunks
            for a in range(6)
        ],
        axis=0,
    )


def cot_kernel(place, cot, *refs):
    chunks, scratch = refs[:N_CH], refs[N_CH]
    for r in range(ROWS):
        scratch[r] = cot[r].astype(F32).T
    for k in range(N_CH):
        cells = pl.ds(pl.multiple_of(48 * (place[1] ^ k), 8), 48)
        chunks[k][...] = to_chunk([scratch[r, cells] for r in range(ROWS)], 0).astype(BF16)


def lon_kernel(x, stats, gain, t_high, t_low, wire, scratch):
    average, inv_std = norm_rows(stats)
    table = (t_high[...], t_low[...])
    for r in range(ROWS):
        normed = (x[r].astype(F32) - average[r : r + 1]) * inv_std[r : r + 1]
        lifted = split(normed * gain[...])
        put_row(scratch, r, dot3(dot_nt, table, lifted))
    flush_rows(scratch, wire)


def lat_forward(wire, lf_high, lf_low, swap):
    values = wire[...]
    swapped = dot(values, swap[...]).astype(BF16)
    both = jnp.concatenate([values, swapped], axis=0)
    return dot(lf_high[...], both) + dot(lf_low[...], both)


def lat_inverse(modes, li_high, li_low):
    both = split(jnp.concatenate([modes[:, :GROUP], modes[:, GROUP:]], axis=0))
    return dot3(dot, (li_high[...], li_low[...]), both)


def weight_sum(blocks):
    def block(part, other):
        pieces = [
            blocks[m + BS * part : m + BS * part + BS, m + BS * other : m + BS * other + BS]
            for m in (0, 2 * BS)
        ]
        return pieces[0] + pieces[1]

    return jnp.concatenate(
        [block(0, 0) + block(1, 1), block(1, 0) - block(0, 1)], axis=0
    )


def spectral_kernel(
    wire, lf_high, lf_low, swap, m1_high, m1_low, m2_high, m2_low, doubled, li_high, li_low,
    out, spectrum, pre_modes,
):
    modes = lat_forward(wire, lf_high, lf_low, swap)
    spectrum[...] = modes
    pre = dot3(dot, split(modes), (m1_high[...], m1_low[...]))
    pre_modes[...] = pre
    act = split(gelu_value(pre))
    scale = doubled[...]
    result = dot3(dot, act, (m2_high[...], m2_low[...])) * jnp.concatenate([scale, scale], axis=1)
    out[...] = lat_inverse(result, li_high, li_low).astype(BF16)


def spectral_back_kernel(
    wire, spectrum, pre_modes, lf_high, lf_low, swap, m1_high, m1_low, m2_high, m2_low, doubled,
    li_high, li_low, gain, gain_parts, out, small, grad_outer, grad_inner, gain_sum,
):
    @pl.when(pl.program_id(0) == 0)
    def _():
        grad_outer[...] = jnp.zeros_like(grad_outer)
        grad_inner[...] = jnp.zeros_like(grad_inner)
        gain_sum[...] = jnp.zeros_like(gain_sum)

    grad = split(lat_forward(wire, lf_high, lf_low, swap) * doubled[...])
    act, slope = gelu_parts(pre_modes[...])
    grad_act = dot3(dot_nt, grad, (m2_high[:, :GROUP], m2_low[:, :GROUP]))
    grad_outer[...] += dot3(dot_tn, grad, split(act))
    grad_pre = split(grad_act * slope)
    modes = spectrum[...]
    grad_inner[...] += dot3(dot_tn, grad_pre, split(modes))
    grad_spectrum = dot3(dot_nt, grad_pre, (m1_high[...], m1_low[...]))
    gain_row = jnp.sum(grad_spectrum[:, :GROUP] * modes, axis=0, keepdims=True)
    gain_row = sum(gain_row[:, BS * k : BS * k + BS] for k in range(4))
    gain_sum[0:1, :BS] += gain_row
    out[...] = lat_inverse(grad_spectrum, li_high, li_low).astype(BF16)

    @pl.when(pl.program_id(0) == 2)
    def _():
        first = gain_sum[0:1, :BS] / gain[...] + gain_parts[0:1, :BS]
        weights = [weight_sum(grad_inner[...]), weight_sum(grad_outer[...])]
        small[:N_LAT] = jnp.concatenate(
            [weight[32 * q : 32 * q + 32] for weight in weights for q in range(6)], axis=1
        )
        row = []
        for values in (first, gain_parts[1:2, :BS]):
            high = values.astype(BF16).astype(F32)
            row += [high, values - high]
        row = jnp.concatenate(row + [jnp.zeros((1, 8 * BS), F32)], axis=1)
        small[N_LAT:] = jnp.concatenate([row, jnp.zeros((7, LANES), F32)], axis=0)


def mix_kernel(wire, tt_high, tt_low, x, stats, gain, mixed, chunks, scratch):
    average, inv_std = norm_rows(stats)
    load_rows(wire, scratch)
    rows = []
    for r in range(ROWS):
        x_float = x[r].astype(F32)
        lifted = (x_float - average[r : r + 1]) * inv_std[r : r + 1] * gain[...]
        modes = get_row(scratch, r).astype(BF16)
        filtered = dot(tt_high[...], modes) + dot(tt_low[...], modes)
        values = filtered + (lifted + x_float).T
        mixed[r] = values
        rows.append(values)
    for e in range(N_CH):
        chunks[e] = to_chunk(rows, e)


def mlp_kernel(core, mixed, gain, *refs):
    given_cots, weights, refs = refs[:8], refs[8:20], refs[20:]
    out_chunks, refs = refs[:8], refs[8:]
    grad_chunks, grad_in_own, grad_in_other, grad_out_own, grad_out_other = refs[:5]
    (
        normed, inputs, cots, inv_std, sum_out, sum_grad, weight_in, weight_out, chunk_rows, arrived,
    ) = refs[5:]
    step = pl.program_id(0)
    turn = 4 * core[0]
    cells = 6 * 8 * ROWS
    part = 8 * ROWS

    def gain_row():
        return jnp.concatenate([gain[e ^ turn] for e in range(N_CH)], axis=1)

    def copies(p):
        found = []
        for half in range(2):
            parts = weights[6 * half : 6 * half + 6]
            rows = pl.ds(384 * half, 384)
            for b in range(2):
                units = pl.ds(384 * b, 384)
                found.append((parts[p].at[b], weight_in.at[p, rows, units]))
                found.append((parts[4 + b].at[p], weight_out.at[p, units, rows]))
        return [
            pltpu.make_async_copy(source, target, arrived.at[8 * p + n])
            for n, (source, target) in enumerate(found)
        ]

    @pl.when(step == 0)
    def _():
        for p in range(4):
            for copy in copies(p):
                copy.start()
        pieces = [mixed[e ^ turn] for e in range(N_CH)]
        values = jnp.concatenate(
            [
                jnp.concatenate([piece[:, BS * a : BS * a + BS] for piece in pieces], axis=1)
                for a in range(6)
            ],
            axis=0,
        )
        average = jnp.sum(values, axis=1, keepdims=True) * (1.0 / C)
        squares = jnp.sum(values * values, axis=1, keepdims=True) * (1.0 / C)
        inv = lax.rsqrt(squares - average * average + EPSILON)
        values = (values - average) * inv
        normed[...] = values
        inv_std[...] = jnp.broadcast_to(inv, (cells, 128))
        inputs[...] = (values * gain_row()).astype(BF16)
        for k in range(N_CH):
            chunk_rows[k] = given_cots[k][...].astype(F32)
        pieces = [chunk_rows[e ^ turn ^ core[1]] for e in range(N_CH)]
        cots[...] = jnp.concatenate(
            [
                jnp.concatenate([piece[:, BS * a : BS * a + BS] for piece in pieces], axis=1)
                for a in range(6)
            ],
            axis=0,
        ).astype(BF16)
        sum_out[...] = jnp.zeros_like(sum_out)
        sum_grad[...] = jnp.zeros_like(sum_grad)

    for p in range(4):

        @pl.when(step == p)
        def _():
            for copy in copies(p):
                copy.wait()

    own_in, own_out = weight_in[step], weight_out[step]
    values, given = inputs[...], cots[...]
    hidden, slope = gelu_parts(dot(values, own_in))
    hidden = hidden.astype(BF16)
    grad_pre = (dot_nt(given, own_out) * slope).astype(BF16)
    sum_out[...] += dot(hidden, own_out)
    sum_grad[...] += dot_nt(grad_pre, own_in)
    grad_in = dot_tn(values, grad_pre)
    grad_out = dot_tn(hidden, given)
    for b in range(2):
        units = slice(384 * b, 384 * b + 384)
        grad_in_own[b, 0] = grad_in[:384, units]
        grad_in_other[b, 0] = grad_in[384:, units].astype(BF16)
        grad_out_own[b, 0] = grad_out[units, :384]
        grad_out_other[b, 0] = grad_out[units, 384:].astype(BF16)

    @pl.when(step == 3)
    def _():
        grad_input = sum_grad[...]
        values = normed[...]
        gain_sum = jnp.sum(grad_input * values, axis=0, keepdims=True)
        scaled = grad_input * gain_row()
        leading = jnp.sum(scaled, axis=1, keepdims=True) * (1.0 / C)
        paired = jnp.sum(scaled * values, axis=1, keepdims=True) * (1.0 / C)
        grad_mixed = cots[...].astype(F32) + inv_std[:, :1] * (scaled - leading - values * paired)
        outputs = sum_out[...]

        def chunk(array, e):
            return jnp.concatenate(
                [array[part * a : part * a + part, BS * e : BS * e + BS] for a in range(6)],
                axis=1,
            )

        for e in range(N_CH):
            chunk_rows[e ^ turn ^ core[1]] = chunk(outputs, e)
            gain_piece = gain_sum[:, BS * e : BS * e + BS]
            gain_high = gain_piece.astype(BF16).astype(F32)
            extra = jnp.concatenate(
                [gain_high, gain_piece - gain_high, jnp.zeros((1, 4 * BS), F32)], axis=1
            )
            extra = jnp.concatenate([extra, jnp.zeros((7, 6 * BS), F32)], axis=0)
            grad_chunks[e ^ turn] = jnp.concatenate(
                [chunk(grad_mixed, e), extra], axis=0
            ).astype(BF16)
        for k in range(N_CH):
            out_chunks[k][...] = chunk_rows[k].astype(BF16)


def lon_back_kernel(chunks, x, stats, t_high, t_low, wire, grad_mixed, gains, scratch):
    average, inv_std = norm_rows(stats)
    pieces = [chunks[e].astype(F32) for e in range(N_CH)]
    gain_first = jnp.zeros((BS, 1), F32)
    for r in range(ROWS):
        values = from_chunks(pieces, r)
        rounded = values.astype(BF16)
        put_row(scratch, r, dot(t_high[...], rounded) + dot(t_low[...], rounded))
        turned = values.T
        grad_mixed[r] = turned.astype(BF16)
        normed = (x[r].astype(F32) - average[r : r + 1]) * inv_std[r : r + 1]
        gain_first = gain_first + jnp.sum(turned * normed, axis=1, keepdims=True)
    flush_rows(scratch, wire)
    gain_second = jnp.zeros((1, BS), F32)
    for piece in pieces:
        row = piece[8 * ROWS : 8 * ROWS + 1]
        gain_second = gain_second + row[:, :BS] + row[:, BS : 2 * BS]
    turned_first = jnp.broadcast_to(gain_first, (BS, 128)).T[0:1, :]
    gains[0:1, :BS] = turned_first
    gains[1:2, :BS] = gain_second


def unmix_kernel(wire, tt_high, tt_low, grad_mixed, x, stats, gain, scaled, sums, scratch):
    average, inv_std = norm_rows(stats)
    load_packed(wire, scratch)
    for r in range(ROWS):
        modes = get_row(scratch, r).astype(BF16)
        back = dot(tt_high[...], modes) + dot(tt_low[...], modes)
        values = (back.T + grad_mixed[r].astype(F32)) * gain[...]
        normed = (x[r].astype(F32) - average[r : r + 1]) * inv_std[r : r + 1]
        scaled[r] = values
        sums[r : r + 1] = jnp.sum(values, axis=0, keepdims=True)
        sums[8 + r : 9 + r] = jnp.sum(values * normed, axis=0, keepdims=True)
    sums[7:8] = jnp.zeros((1, W), F32)
    sums[15:16] = jnp.zeros((1, W), F32)


def final_kernel(scaled, grad_mixed, x, stats, *rest):
    average, inv_std = norm_rows(stats)
    out = rest[-1]
    total = rest[0][...]
    for part in rest[1:-1]:
        total = total + part[...]
    total = total * (1.0 / C)
    for r in range(ROWS):
        inv = inv_std[r : r + 1]
        normed = (x[r].astype(F32) - average[r : r + 1]) * inv
        change = scaled[r] - total[r : r + 1] - normed * total[8 + r : 9 + r]
        out[r] = (grad_mixed[r].astype(F32) + inv * change).astype(BF16)


def pack_kernel(wire, small, *refs):
    out = refs[11]

    def add(parts):
        total = parts[0].astype(F32)
        for part in parts[1:]:
            total = total + part.astype(F32)
        return total

    total_in = add([refs[0][0, 0], refs[1][0, 0], refs[2][0]] + [part[...] for part in refs[3:6]])
    total_out = add([refs[6][0, 0], refs[7][0, 0], refs[8][0], refs[9][...], refs[10][...]])
    total = jnp.concatenate([total_in, total_out], axis=0)
    modes = wire[...].astype(F32).reshape(N_LAT, 8, LANES)
    weights = small[:N_LAT]
    row = lax.broadcasted_iota(jnp.int32, (N_LAT, 8, LANES), 1)
    modes = jnp.where(row == ROWS, weights[:, None, :], modes)
    grads = jnp.concatenate(
        [total[256 * g : 256 * g + 256].reshape(N_LAT, 8, GROUP) for g in range(3)], axis=2
    )
    out[...] = jnp.concatenate([modes, grads], axis=1).astype(BF16)


def spread_kernel(parts, small, out):
    sums = [parts[n].astype(F32) for n in (0, 1)]
    for n in range(2, N_LAT):
        sums[n % 2] = sums[n % 2] + parts[n].astype(F32)
    rows = [
        half[8:16, GROUP * g : GROUP * g + GROUP] for half in sums for g in range(3)
    ]
    weights = sums[0][ROWS : ROWS + 1] + sums[1][ROWS : ROWS + 1]
    last = [weights[:, GROUP * g : GROUP * g + GROUP] for g in range(3)]
    last += [small[N_LAT : N_LAT + 1, :GROUP], jnp.zeros((4, GROUP), F32)]
    total = jnp.concatenate(rows + [jnp.concatenate(last, axis=0)], axis=0).astype(BF16)
    for n in range(N_LAT // 2):
        out[n] = total


def finish_kernel(
    place, mine, theirs, grad_in, grad_out, grad_inner, grad_outer, gain_first, gain_second
):
    first = place[0] == 0
    one, two = mine[...].astype(F32), theirs[...].astype(F32)
    even, odd = jnp.where(first, one, two), jnp.where(first, two, one)

    def rows(start):
        parts = [part[:, start : start + 8][:, None] for part in (even, odd)]
        return jnp.concatenate(parts, axis=1).reshape(256, GROUP)

    for half in range(2):
        total = jnp.concatenate([rows(24 * half + 8 * g) for g in range(3)], axis=0)
        grad_in[384 * half : 384 * half + 384] = total[:384]
        grad_out[:, 384 * half : 384 * half + 384] = total[384:]
    last = rows(48)
    planes = [
        jnp.concatenate([last[8 * n + g : 8 * n + g + 1] for n in range(N_LAT)], axis=0)
        for g in range(4)
    ]
    weights = [
        plane[:, BS * q : BS * q + BS] for plane in planes[:3] for q in range(4)
    ]
    for part in range(2):
        grad_inner[part, 0] = jnp.concatenate(weights[3 * part : 3 * part + 3], axis=0)
        grad_outer[part, 0] = jnp.concatenate(weights[6 + 3 * part : 9 + 3 * part], axis=0)
    gains = jnp.sum(planes[3], axis=0, keepdims=True)
    gain_first[...] = gains[:, :BS] + gains[:, BS : 2 * BS]
    gain_second[...] = gains[:, 2 * BS : 3 * BS] + gains[:, 3 * BS :]


def output_kernel(place, mixed, *refs):
    chunks, out, chunk_rows = refs[:N_CH], refs[N_CH], refs[N_CH + 1]
    for k in range(N_CH):
        chunk_rows[k] = chunks[k][...].astype(F32)
    pieces = [chunk_rows[e ^ place[1]] for e in range(N_CH)]
    for r in range(ROWS):
        out[r] = (from_chunks(pieces, r) + mixed[r]).T.astype(BF16)


def cost(micros):
    return pl.CostEstimate(
        flops=int(micros * 1.0e9), bytes_accessed=int(micros * 2.0e6), transcendentals=0
    )


def call(kernel, out_shape, *args, scratch=(), micros=3, place=None):
    specs = [pl.BlockSpec(memory_space=pltpu.VMEM)] * len(args)
    if place is not None:
        args = (place,) + args
        specs = [pl.BlockSpec(memory_space=pltpu.SMEM)] + specs
    return pl.pallas_call(
        kernel,
        out_shape=out_shape,
        in_specs=specs,
        scratch_shapes=scratch,
        compiler_params=pltpu.CompilerParams(vmem_limit_bytes=VMEM_BYTES),
        cost_estimate=cost(micros),
    )(*args)


def shaped(*shape, dtype=F32):
    return jax.ShapeDtypeStruct(shape, dtype)


def whole(shape):
    return pl.BlockSpec(shape, lambda g: (0,) * len(shape))


def lane_block(rows):
    return pl.BlockSpec((rows, GROUP), lambda g: (0, g))


def block_matrix(weight, swap_columns, swap_rows):
    real, imag = weight[0, 0].T, weight[1, 0].T
    base = [[real, imag], [-imag, real]]
    if swap_columns:
        base = [[imag, -real], [real, imag]]
    if swap_rows:
        base = [[-imag, real], [-real, -imag]]
    one = jnp.concatenate([jnp.concatenate(line, axis=1) for line in base], axis=0)
    zero = jnp.zeros_like(one)
    return jnp.concatenate(
        [jnp.concatenate([one, zero], axis=1), jnp.concatenate([zero, one], axis=1)], axis=0
    )


def to_all(values, axis, count, **kwargs):
    spread = jnp.broadcast_to(values[None], (count,) + values.shape)
    return lax.all_to_all(spread, axis, 0, 0, tiled=True, **kwargs)


def near(values, k):
    return lax.ppermute(values, "ch", [(i, i ^ k) for i in range(N_CH)])


def body(fields, gain_first, w_inner, w_outer, gain_second, fc_in, fc_out, cotangent):
    lat = lax.axis_index("lat")
    core = lat % 2
    me = lax.axis_index("ch")
    place = jnp.stack([core, me]).astype(jnp.int32)
    siblings = [(i, i ^ 1) for i in range(N_LAT)]
    cores = [list(range(0, N_LAT, 2)), list(range(1, N_LAT, 2))]
    t_high, t_low = (jnp.asarray(t) for t in halves(lon_table()))
    tt_high, tt_low = (jnp.asarray(t) for t in halves(lon_table().T))
    forward, inverse = lat_tables()
    lf_high, lf_low = (jnp.asarray(t) for t in halves(forward))
    li_high, li_low = (jnp.asarray(t) for t in halves(inverse))
    swap = jnp.asarray(swap_table())

    x = fields.transpose(1, 0, 2)
    cot = cotangent.transpose(1, 0, 2)
    gain_column = gain_first[:, None]

    with jax.named_scope("stats"):
        x_float = x.astype(F32)
        zero = jnp.zeros((1, W), F32)
        payload = jnp.concatenate(
            [
                jnp.sum(x_float, 1),
                zero,
                jnp.sum(x_float * x_float, 1),
                zero,
                jnp.pad(gain_second, (0, W - BS))[None],
                jnp.zeros((7, W), F32),
            ],
            axis=0,
        )
        gathered = to_all(payload, "ch", N_CH)
        gathered, fc_in, fc_out, cot = lax.optimization_barrier((gathered, fc_in, fc_out, cot))

    with jax.named_scope("weights"):
        half_in = lax.dynamic_slice_in_dim(fc_in, core * 384, 384, 0)
        half_out = lax.dynamic_slice_in_dim(fc_out, core * 384, 384, 1)
        near_in = near(half_in, 1)
        near_out = [near(half_out, k) for k in (2, 4, 6)]

    with jax.named_scope("cot"):
        chunk_shape = shaped(8 * ROWS, 6 * BS, dtype=BF16)
        first, *others = call(
            cot_kernel, [chunk_shape] * N_CH, cot, place=place,
            scratch=[pltpu.VMEM((ROWS, W, BS), F32)],
        )
        cot_chunks = [first] + [near(part, k + 1) for k, part in enumerate(others)]

    with jax.named_scope("stats"):
        stats = gathered[:, :16]
        gains = gathered[:, 16:17, :BS]

    scratch = pltpu.VMEM((LANES // 128, 8 * N_LAT, 128), F32)
    wire_shape = shaped(8 * N_LAT, LANES, dtype=BF16)
    with jax.named_scope("lon"):
        wire = call(
            lon_kernel, wire_shape, x, stats, gain_column, t_high, t_low, scratch=[scratch]
        )
        wire = lax.all_to_all(wire, "lat", 0, 0, tiled=True)

    with jax.named_scope("weights"):
        pair = jnp.stack([half_in, near_in])
        own_in = [pair] + [near(pair, k) for k in (2, 4, 6)]
        quad = jnp.stack([half_out] + near_out)
        own_out = [quad, near(quad, 1)]

    with jax.named_scope("matrices"):
        m1 = split(
            jnp.concatenate(
                [block_matrix(w_inner, False, False), block_matrix(w_inner, False, True)], axis=0
            )
        )
        m2 = split(
            jnp.concatenate(
                [block_matrix(w_outer, False, False), block_matrix(w_outer, True, False)], axis=1
            )
        )
        lane = jnp.arange(LANES, dtype=jnp.int32)[None]
        doubled = jnp.where((lat == 0) & (lane < 2 * BS), 1.0, 2.0).astype(F32)

    table_specs = [whole((H, 512)), whole((H, 512)), whole((GROUP, GROUP))]
    inverse_specs = [lane_block(1), whole((256, 448)), whole((256, 448))]
    params = pltpu.CompilerParams(vmem_limit_bytes=VMEM_BYTES)
    with jax.named_scope("spectral"):
        wire, spectrum, pre_modes = pl.pallas_call(
            spectral_kernel,
            grid=(3,),
            in_specs=[lane_block(256)]
            + table_specs
            + [whole((GROUP, GROUP))] * 2
            + [whole((GROUP, 2 * GROUP))] * 2
            + inverse_specs,
            out_specs=[lane_block(256), lane_block(H), lane_block(H)],
            out_shape=[wire_shape, shaped(H, LANES), shaped(H, LANES)],
            compiler_params=params,
            cost_estimate=cost(11),
        )(
            wire, lf_high, lf_low, swap, m1[0][:GROUP], m1[1][:GROUP], m2[0], m2[1], doubled,
            li_high, li_low,
        )
        own_in[1], own_in[3], wire = lax.optimization_barrier((own_in[1], own_in[3], wire))
        wire = lax.all_to_all(wire, "lat", 0, 0, tiled=True)
        own_in[2], own_out[1], *cot_chunks[:7], wire = lax.optimization_barrier(
            (own_in[2], own_out[1], *cot_chunks[:7], wire)
        )
        weights = own_in + own_out
        weights += [lax.ppermute(part, "lat", siblings) for part in weights]

    with jax.named_scope("mix"):
        mixed, chunks = call(
            mix_kernel,
            [shaped(ROWS, W, BS), shaped(N_CH, 8 * ROWS, 6 * BS)],
            wire, tt_high, tt_low, x, stats, gain_column,
            scratch=[scratch],
        )
        chunks = lax.all_to_all(chunks, "ch", 0, 0, tiled=True)

    cells = 48 * ROWS
    halved = pl.BlockSpec((2, 1, 384, 384), lambda p, place: (0, p, 0, 0))

    def all_of(shape):
        return pl.BlockSpec(shape, lambda e, place: (0,) * len(shape))

    with jax.named_scope("mlp"):
        *out_chunks, grad_chunks, in_own, in_other, out_own, out_other = pl.pallas_call(
            mlp_kernel,
            grid_spec=pltpu.PrefetchScalarGridSpec(
                num_scalar_prefetch=1,
                grid=(4,),
                in_specs=[
                    all_of((N_CH, 8 * ROWS, 6 * BS)),
                    all_of((N_CH, 1, BS)),
                ]
                + [all_of((8 * ROWS, 6 * BS))] * N_CH
                + [pl.BlockSpec(memory_space=pl.ANY)] * 12,
                out_specs=[all_of((8 * ROWS, 6 * BS))] * N_CH
                + [
                    all_of((N_CH, 8 * ROWS + 8, 6 * BS)),
                    halved,
                    halved,
                    halved,
                    halved,
                ],
                scratch_shapes=[
                    pltpu.VMEM((cells, C), F32),
                    pltpu.VMEM((cells, C), BF16),
                    pltpu.VMEM((cells, C), BF16),
                    pltpu.VMEM((cells, 128), F32),
                    pltpu.VMEM((cells, C), F32),
                    pltpu.VMEM((cells, C), F32),
                    pltpu.VMEM((4, C, C), BF16),
                    pltpu.VMEM((4, C, C), BF16),
                    pltpu.VMEM((N_CH, 8 * ROWS, 6 * BS), F32),
                    pltpu.SemaphoreType.DMA((32,)),
                ],
            ),
            out_shape=[chunk_shape] * N_CH
            + [
                shaped(N_CH, 8 * ROWS + 8, 6 * BS, dtype=BF16),
                shaped(2, 4, 384, 384),
                shaped(2, 4, 384, 384, dtype=BF16),
                shaped(2, 4, 384, 384),
                shaped(2, 4, 384, 384, dtype=BF16),
            ],
            compiler_params=params,
            cost_estimate=cost(20),
        )(place, chunks, gains, *cot_chunks, *weights)
        grad_chunks = lax.all_to_all(grad_chunks, "ch", 0, 0, tiled=True)

    with jax.named_scope("grads_ch"):
        theirs_in = lax.ppermute(in_other, "lat", siblings)
        theirs_out = lax.ppermute(out_other, "lat", siblings)

        def merged(part, rows):
            return out_own[part, rows] + theirs_out[part, rows].astype(F32)

        odd = (in_own[1] + theirs_in[1].astype(F32)).astype(BF16)
        one = merged(0, slice(1, 3)).astype(BF16)
        two = merged(1, slice(2, 4)).astype(BF16)
        *_, grad_chunks = lax.optimization_barrier((odd, one, two, grad_chunks))
        odd, one, two = near(odd, 1), near(one, 2), near(two, 6)

    with jax.named_scope("lon_back"):
        wire, grad_mixed, gain_parts = call(
            lon_back_kernel,
            [wire_shape, shaped(ROWS, BS, W, dtype=BF16), shaped(8, 128)],
            grad_chunks, x, stats, t_high, t_low,
            scratch=[scratch],
        )
        wire = lax.all_to_all(wire, "lat", 0, 0, tiled=True)

    with jax.named_scope("grads_ch"):
        one_next = near((merged(0, 3) + one[1].astype(F32)).astype(BF16), 6)
        two_next = near((merged(1, 1) + two[0].astype(F32)).astype(BF16), 2)
        even = in_own[0, 1:] + theirs_in[0, 1:].astype(F32) + odd[1:].astype(F32)
        even = even.astype(BF16)
        far = (merged(1, 0) + two[1].astype(F32) + two_next.astype(F32)).astype(BF16)
        odd, one, one_next, even, far, wire = lax.optimization_barrier(
            (odd, one, one_next, even, far, wire)
        )
        in_parts = [near(even[k // 2 - 1], k) for k in (2, 4, 6)]
        out_part = near(far, 1)

    with jax.named_scope("spectral_back"):
        wire, small = pl.pallas_call(
            spectral_back_kernel,
            grid=(3,),
            in_specs=[lane_block(256), lane_block(H), lane_block(H)]
            + table_specs
            + [whole((2 * GROUP, GROUP))] * 2
            + [whole((GROUP, 2 * GROUP))] * 2
            + inverse_specs
            + [whole((1, BS)), whole((8, 128))],
            out_specs=[lane_block(256), whole((N_LAT + 8, LANES))],
            out_shape=[wire_shape, shaped(N_LAT + 8, LANES)],
            scratch_shapes=[
                pltpu.VMEM((GROUP, GROUP), F32),
                pltpu.VMEM((GROUP, GROUP), F32),
                pltpu.VMEM((8, 128), F32),
            ],
            compiler_params=params,
            cost_estimate=cost(14),
        )(
            wire, spectrum, pre_modes, lf_high, lf_low, swap, m1[0], m1[1], m2[0], m2[1], doubled,
            li_high, li_low, gain_first[None], gain_parts,
        )
        *in_parts, out_part, wire = lax.optimization_barrier((*in_parts, out_part, wire))

    with jax.named_scope("pack"):
        corner = pl.BlockSpec((1, 1, 384, 384), lambda g: (0, 0, 0, 0))
        front = pl.BlockSpec((1, 384, 384), lambda g: (0, 0, 0))
        flat = whole((384, 384))
        wire = pl.pallas_call(
            pack_kernel,
            grid=(1,),
            in_specs=[whole((256, LANES)), whole((N_LAT + 8, LANES))]
            + [corner, corner, front, flat, flat, flat]
            + [corner, corner, front, flat, flat],
            out_specs=whole((N_LAT, 16, LANES)),
            out_shape=shaped(N_LAT, 16, LANES, dtype=BF16),
            compiler_params=params,
            cost_estimate=cost(3),
        )(
            wire, small, in_own, theirs_in, odd, *in_parts, out_own, theirs_out, one, one_next,
            out_part,
        )
        *out_chunks, wire = lax.optimization_barrier((*out_chunks, wire))
        wire = lax.all_to_all(wire, "lat", 0, 0, tiled=True)

    with jax.named_scope("output"):
        first, *others = out_chunks
        out_chunks = [first] + [near(part, k + 1) for k, part in enumerate(others)]
        output = call(
            output_kernel, shaped(ROWS, BS, W, dtype=BF16), mixed, *out_chunks, place=place,
            scratch=[pltpu.VMEM((N_CH, 8 * ROWS, 6 * BS), F32)],
        )
        output, wire = lax.optimization_barrier((output, wire))

    with jax.named_scope("unmix"):
        scaled, sums = call(
            unmix_kernel,
            [shaped(ROWS, BS, W), shaped(16, W)],
            wire, tt_high, tt_low, grad_mixed, x, stats, gain_column,
            scratch=[scratch],
        )
    with jax.named_scope("sums"):
        sums = [sums] + [near(sums, k) for k in range(1, N_CH)]

    with jax.named_scope("grads_lat"):
        payload = call(spread_kernel, shaped(N_LAT // 2, 56, GROUP, dtype=BF16), wire, small)
        mine = lax.all_to_all(payload, "lat", 0, 0, tiled=True, axis_index_groups=cores)
        mine, *sums = lax.optimization_barrier((mine, *sums))
        theirs = lax.ppermute(mine, "lat", siblings)
        weight_shape = shaped(2, 1, BS, BS)
        grad_fc_in, grad_fc_out, grad_w_inner, grad_w_outer, grad_first, grad_second = call(
            finish_kernel,
            [
                shaped(C, FF_DEV),
                shaped(FF_DEV, C),
                weight_shape,
                weight_shape,
                shaped(1, BS),
                shaped(1, BS),
            ],
            mine, theirs, place=place,
        )

    with jax.named_scope("final"):
        grad_fields = call(
            final_kernel, shaped(ROWS, BS, W, dtype=BF16), scaled, grad_mixed, x, stats, *sums
        )

    return (
        output.transpose(1, 0, 2),
        grad_fields.transpose(1, 0, 2),
        grad_first[0],
        grad_w_inner,
        grad_w_outer,
        grad_second[0],
        grad_fc_in,
        grad_fc_out,
    )


def solution(mesh):
    placed = (
        P("ch", "lat", None),
        P("ch"),
        P(None, "ch", None, None),
        P(None, "ch", None, None),
        P("ch"),
        P(None, "ch"),
        P("ch", None),
        P("ch", "lat", None),
    )
    return jax.shard_map(
        body,
        mesh=mesh,
        in_specs=placed,
        out_specs=(
            P("ch", "lat", None),
            P("ch", "lat", None),
            P("ch"),
            P(None, "ch", None, None),
            P(None, "ch", None, None),
            P("ch"),
            P(None, "ch"),
            P("ch", None),
        ),
        check_vma=False,
    )
```
